256 devices in a mesh: gx: 32 (over y, z), gy: 8 (over x, core).
Axes of the slice: x: 4, y: 4, z: 8, core: 2. Of those that a mesh axis runs over, the one named last changes fastest.
Arguments:
- source: float32 [16, 512, 2048], P(None, 'gx', 'gy'), may hold values from -540 to 540
Outputs:
- pressure: float32 [16, 512, 2048], P(None, 'gx', 'gy')
The draws below stay inside these ranges and needn't reach their ends.
All inputs are finite; a program needn't handle non-finite values.
Results may differ from the reference program's by a relative error of at most 0.00085.
Values sent between devices are 32-bit elements; how exact they have to be, the bound alone decides.
No kernel may reach another device: no remote copies, remote signals or barrier semaphores. Data moves between devices by JAX's collectives and lax.ppermute only.
A program may use at most 128 MiB of HBM per device.

```python
import math
import jax
import jax.numpy as jnp
import numpy as np
from jax import lax

NODES_FINE = 8
NODES_MID = 4
NODES_COARSE = 2
LAYERS = 2
CHEB_DEGREE = 3
CG_ITERS = 8
EXG = 64
EYG = 256
ZF = 16
XF = 512
YF = 2048


def draw_source(key, part):
    key = jax.random.fold_in(key, 7)
    noise_key, factor_key = jax.random.split(key, 2)
    rows_pos = jnp.arange(XF, dtype=jnp.float32) / XF
    cols_pos = jnp.arange(YF, dtype=jnp.float32) / YF
    slope_factor = jnp.exp(jnp.log(3.0) * (rows_pos[:, None] + cols_pos[None, :]))
    factors = jax.random.uniform(factor_key, (LAYERS, EXG, EYG), jnp.float32, 0.6, 1.5)
    factors = jnp.repeat(jnp.repeat(jnp.repeat(factors, NODES_FINE, axis=0), NODES_FINE, axis=1), NODES_FINE, axis=2)
    noise_field = jnp.clip(jax.random.normal(noise_key, (ZF, XF, YF), jnp.float32), -4.0, 4.0)
    return 10.0 * noise_field * factors * slope_factor[None]


def setup_inputs(seed: int = 0) -> dict:
    arg_keys = jax.random.split(jax.random.key(seed), 2)
    source = draw_source(jax.random.fold_in(arg_keys[1], 71), 0)
    return dict(source=source)


mass_coef = 0.000125
cheb_ratio = 0.1
highest = lax.Precision.HIGHEST


def legendre_pair(points, order):
    previous = 0.0 * points + 1.0
    current = points * 1.0
    for degree in range(2, order + 1):
        previous, current = current, ((2.0 * degree - 1.0) * points * current - (degree - 1.0) * previous) / degree
    return previous, current


def gll_tables(order):
    count_nodes = order + 1
    points = -np.cos(math.pi * np.arange(count_nodes) / order)
    for sweep in range(60):
        previous, values_at = legendre_pair(points, order)
        points = points - (points * values_at - previous) / (count_nodes * values_at)
    previous, values_at = legendre_pair(points, order)
    weights = 2.0 / (order * (order + 1) * values_at * values_at)
    spacing = points[:, None] - points[None, :]
    safe_spacing = np.where(spacing == 0.0, 1.0, spacing)
    derivative = values_at[:, None] / (values_at[None, :] * safe_spacing)
    derivative = derivative * (1.0 - np.eye(count_nodes))
    corner_value = order * (order + 1) / 4.0
    end_values = np.concatenate([np.array([-corner_value]), np.zeros(count_nodes - 2), np.array([corner_value])])
    return points, weights, derivative + np.eye(count_nodes) * end_values[None, :]


def interp_table(fine_order, coarse_order):
    fine_points = gll_tables(fine_order)[0]
    coarse_points = gll_tables(coarse_order)[0]
    numer = fine_points[:, None, None] - coarse_points[None, None, :]
    denom = coarse_points[None, :, None] - coarse_points[None, None, :]
    same_node = np.eye(len(coarse_points))[None, :, :] > 0.5
    ratio = np.where(same_node, 1.0, numer / np.where(same_node, 1.0, denom))
    return ratio.prod(axis=2)


def element_bound(order):
    points, weights, derivative = gll_tables(order)
    mass = np.eye(order + 1) * weights[None, :]
    stiff = np.dot(derivative.T, np.dot(mass, derivative))
    full = 0.5 * (np.kron(np.kron(mass, mass), stiff) + np.kron(np.kron(mass, stiff), mass) + np.kron(np.kron(stiff, mass), mass)) + mass_coef * np.kron(np.kron(mass, mass), mass)
    diagonal_entries = np.sum(full * np.eye(full.shape[0]), axis=1)
    ratio = np.abs(full).sum(axis=1) / diagonal_entries
    return float(ratio.max())


def tiled(table, length):
    return jnp.tile(jnp.asarray(table, dtype=jnp.float32), length // table.shape[0])


def layer_share(length, count_nodes):
    position = jnp.arange(length)
    node_index = position % count_nodes
    layer_index = position // count_nodes
    shared = ((node_index == 0) & (layer_index > 0)) | ((node_index == count_nodes - 1) & (layer_index < length // count_nodes - 1))
    return jnp.where(shared, 0.5, 1.0).astype(jnp.float32)


def plane_share(length, count_nodes):
    node_index = jnp.arange(length) % count_nodes
    return jnp.where((node_index == 0) | (node_index == count_nodes - 1), 0.5, 1.0).astype(jnp.float32)


def node_masks(length, count_nodes):
    node_index = jnp.arange(length) % count_nodes
    return node_index == 0, node_index == count_nodes - 1


def fold_pair(center, before, after, lead_mask, tail_mask):
    return center + jnp.where(lead_mask, before, 0.0) + jnp.where(tail_mask, after, 0.0)


def fold_depth(field_in, count_nodes):
    zero_plane = jnp.zeros_like(field_in[:1])
    before = jnp.concatenate([zero_plane, field_in[:-1]], axis=0)
    after = jnp.concatenate([field_in[1:], zero_plane], axis=0)
    lead_mask, tail_mask = node_masks(field_in.shape[0], count_nodes)
    return fold_pair(field_in, before, after, lead_mask[:, None, None], tail_mask[:, None, None])


def assemble_pattern(field_in, count_nodes):
    rows_lead, rows_tail = node_masks(field_in.shape[1], count_nodes)
    cols_lead, cols_tail = node_masks(field_in.shape[2], count_nodes)
    across = fold_pair(field_in, jnp.roll(field_in, 1, axis=1), jnp.roll(field_in, -1, axis=1), rows_lead[:, None], rows_tail[:, None])
    summed = fold_pair(across, jnp.roll(across, 1, axis=2), jnp.roll(across, -1, axis=2), cols_lead, cols_tail)
    return fold_depth(summed, count_nodes)


def along_depth(field_in, matrix):
    count_in = matrix.shape[1]
    blocks = field_in.reshape(field_in.shape[0] // count_in, count_in, field_in.shape[1], field_in.shape[2])
    result = jnp.einsum('oi,eixy->eoxy', matrix, blocks, precision=highest)
    return result.reshape(-1, field_in.shape[1], field_in.shape[2])


def along_rows(field_in, matrix):
    count_in = matrix.shape[1]
    blocks = field_in.reshape(field_in.shape[0], field_in.shape[1] // count_in, count_in, field_in.shape[2])
    result = jnp.einsum('oi,zeiy->zeoy', matrix, blocks, precision=highest)
    return result.reshape(field_in.shape[0], -1, field_in.shape[2])


def along_columns(field_in, matrix):
    count_in = matrix.shape[1]
    blocks = field_in.reshape(field_in.shape[0], field_in.shape[1], field_in.shape[2] // count_in, count_in)
    result = jnp.einsum('oi,zxei->zxeo', matrix, blocks, precision=highest)
    return result.reshape(field_in.shape[0], field_in.shape[1], -1)


def build_level(order, shape):
    points, weights, derivative = gll_tables(order)
    count_nodes = order + 1
    stiff_diag = np.sum(weights[:, None] * derivative * derivative, axis=0)
    depth_w = tiled(weights, shape[0])
    rows_w = tiled(weights, shape[1])
    cols_w = tiled(weights, shape[2])
    depth_k = tiled(stiff_diag, shape[0])
    rows_k = tiled(stiff_diag, shape[1])
    cols_k = tiled(stiff_diag, shape[2])
    weight_cube = (depth_w[:, None, None] * rows_w[None, :, None]) * cols_w[None, None, :]
    local_diag = 0.5 * ((depth_w[:, None, None] * rows_k[None, :, None]) * cols_w[None, None, :] + (depth_w[:, None, None] * rows_w[None, :, None]) * cols_k[None, None, :] + (depth_k[:, None, None] * rows_w[None, :, None]) * cols_w[None, None, :]) + mass_coef * weight_cube
    inverse_diag = 1.0 / assemble_pattern(local_diag, count_nodes)
    shares = (layer_share(shape[0], count_nodes), plane_share(shape[1], count_nodes), plane_share(shape[2], count_nodes))
    return (count_nodes, jnp.asarray(derivative, dtype=jnp.float32), weight_cube, inverse_diag, shares, element_bound(order))


def apply_share(field_in, level):
    shares = level[4]
    return field_in * shares[0][:, None, None] * shares[1][None, :, None] * shares[2][None, None, :]


def local_op(field_in, level):
    derivative = level[1]
    weight_cube = level[2]
    gradient = along_rows(field_in, derivative)
    total = along_rows(weight_cube * gradient, derivative.T)
    gradient = along_columns(field_in, derivative)
    total = total + along_columns(weight_cube * gradient, derivative.T)
    gradient = along_depth(field_in, derivative)
    total = total + along_depth(weight_cube * gradient, derivative.T)
    return 0.5 * total + mass_coef * (weight_cube * field_in)


def apply_op(field_in, level):
    return assemble_pattern(local_op(field_in, level), level[0])


def restrict(field_in, table):
    matrix = table.T
    return along_columns(along_rows(along_depth(field_in, matrix), matrix), matrix)


def prolong(field_in, table):
    return along_columns(along_rows(along_depth(field_in, table), table), table)


def smooth_level(level, solution, rhs, start_zero):
    upper = level[5]
    lower = cheb_ratio * upper
    center = 0.5 * (upper + lower)
    half_width = 0.5 * (upper - lower)
    inverse_diag = level[3]
    if start_zero:
        residual = rhs
    else:
        residual = rhs - apply_op(solution, level)
    sigma_one = center / half_width
    rho_now = 1.0 / sigma_one
    direction = inverse_diag * residual / center
    for index in range(CHEB_DEGREE):
        solution = solution + direction
        if index + 1 < CHEB_DEGREE:
            residual = residual - apply_op(direction, level)
            rho_next = 1.0 / (2.0 * sigma_one - rho_now)
            direction = rho_next * rho_now * direction + (2.0 * rho_next / half_width) * (inverse_diag * residual)
            rho_now = rho_next
    return solution


def coarse_solve(rhs, level):
    solution = jnp.zeros_like(rhs)
    residual = rhs
    direction = rhs
    norm_now = jnp.sum(apply_share(residual * residual, level))
    for index in range(CG_ITERS):
        image = apply_op(direction, level)
        alpha = norm_now / jnp.sum(apply_share(direction * image, level))
        solution = solution + alpha * direction
        residual = residual - alpha * image
        if index + 1 < CG_ITERS:
            norm_next = jnp.sum(apply_share(residual * residual, level))
            direction = residual + (norm_next / norm_now) * direction
            norm_now = norm_next
    return solution


def reference(source):
    fine = build_level(NODES_FINE - 1, source.shape)
    middle = build_level(NODES_MID - 1, (LAYERS * NODES_MID, EXG * NODES_MID, EYG * NODES_MID))
    coarse = build_level(NODES_COARSE - 1, (LAYERS * NODES_COARSE, EXG * NODES_COARSE, EYG * NODES_COARSE))
    fine_table = jnp.asarray(interp_table(NODES_FINE - 1, NODES_MID - 1), dtype=jnp.float32)
    coarse_table = jnp.asarray(interp_table(NODES_MID - 1, NODES_COARSE - 1), dtype=jnp.float32)
    rhs_fine = assemble_pattern((0.125 * fine[2]) * source, fine[0])
    fine_x = smooth_level(fine, jnp.zeros_like(rhs_fine), rhs_fine, True)
    fine_r = rhs_fine - apply_op(fine_x, fine)
    rhs_mid = assemble_pattern(restrict(apply_share(fine_r, fine), fine_table), middle[0])
    mid_x = smooth_level(middle, jnp.zeros_like(rhs_mid), rhs_mid, True)
    mid_r = rhs_mid - apply_op(mid_x, middle)
    rhs_coarse = assemble_pattern(restrict(apply_share(mid_r, middle), coarse_table), coarse[0])
    coarse_x = coarse_solve(rhs_coarse, coarse)
    mid_x = smooth_level(middle, mid_x + prolong(coarse_x, coarse_table), rhs_mid, False)
    return smooth_level(fine, fine_x + prolong(mid_x, fine_table), rhs_fine, False)
```

```python
import math

import jax
import jax.numpy as jnp
import ml_dtypes
import numpy as np
from jax import lax
from jax.experimental import pallas as pl
from jax.experimental.pallas import tpu as pltpu
from jax.sharding import PartitionSpec as P

CG_ITERS = 8
mass_coef = 0.000125
cheb_ratio = 0.1
f32 = jnp.float32
bf16 = jnp.bfloat16
MB = 1024 * 1024


def legendre_pair(points, order):
    previous = 0.0 * points + 1.0
    current = points * 1.0
    for degree in range(2, order + 1):
        previous, current = (
            current,
            ((2.0 * degree - 1.0) * points * current - (degree - 1.0) * previous) / degree,
        )
    return (previous, current)


def gll_tables(order):
    count_nodes = order + 1
    points = -np.cos(math.pi * np.arange(count_nodes) / order)
    for sweep in range(60):
        previous, values_at = legendre_pair(points, order)
        points = points - (points * values_at - previous) / (count_nodes * values_at)
    previous, values_at = legendre_pair(points, order)
    weights = 2.0 / (order * (order + 1) * values_at * values_at)
    spacing = points[:, None] - points[None, :]
    safe_spacing = np.where(spacing == 0.0, 1.0, spacing)
    derivative = values_at[:, None] / (values_at[None, :] * safe_spacing)
    derivative = derivative * (1.0 - np.eye(count_nodes))
    corner_value = order * (order + 1) / 4.0
    end_values = np.concatenate(
        [np.array([-corner_value]), np.zeros(count_nodes - 2), np.array([corner_value])]
    )
    return (points, weights, derivative + np.eye(count_nodes) * end_values[None, :])


def interp_table(fine_order, coarse_order):
    fine_points = gll_tables(fine_order)[0]
    coarse_points = gll_tables(coarse_order)[0]
    numer = fine_points[:, None, None] - coarse_points[None, None, :]
    denom = coarse_points[None, :, None] - coarse_points[None, None, :]
    same_node = np.eye(len(coarse_points))[None, :, :] > 0.5
    ratio = np.where(same_node, 1.0, numer / np.where(same_node, 1.0, denom))
    return ratio.prod(axis=2)


def element_bound(order):
    points, weights, derivative = gll_tables(order)
    mass = np.eye(order + 1) * weights[None, :]
    stiff = np.dot(derivative.T, np.dot(mass, derivative))
    full = 0.5 * (
        np.kron(np.kron(mass, mass), stiff)
        + np.kron(np.kron(mass, stiff), mass)
        + np.kron(np.kron(stiff, mass), mass)
    ) + mass_coef * np.kron(np.kron(mass, mass), mass)
    diagonal_entries = np.sum(full * np.eye(full.shape[0]), axis=1)
    ratio = np.abs(full).sum(axis=1) / diagonal_entries
    return float(ratio.max())


def sum_matrix(elements, n, cyclic):
    out = np.eye(elements * n)
    for e in range(elements):
        if cyclic or e + 1 < elements:
            a, b = e * n + n - 1, ((e + 1) % elements) * n
            out[a, b] += 1.0
            out[b, a] += 1.0
    return out


def blocks(matrix, count):
    return np.kron(np.eye(count), matrix)


class Level:
    def __init__(self, order):
        n = self.n = order + 1
        _, w, dm = gll_tables(order)
        self.w = w
        self.k = dm.T @ np.diag(w) @ dm
        self.sum_z = sum_matrix(2, n, False)
        self.k_z = self.sum_z @ blocks(self.k, 2)
        self.w_z = self.sum_z @ np.tile(w, 2)
        self.w_p = w.copy()
        self.w_p[0] += w[-1]
        self.w_p[-1] += w[0]
        kd = np.diag(self.k).copy()
        kd_p = kd.copy()
        kd_p[0] += kd[-1]
        kd_p[-1] += kd[0]
        kd_z = self.sum_z @ np.tile(kd, 2)
        wz, wp = self.w_z, self.w_p
        diag = 0.5 * (
            np.einsum("z,r,c->zrc", wz, kd_p, wp)
            + np.einsum("z,r,c->zrc", wz, wp, kd_p)
            + np.einsum("z,r,c->zrc", kd_z, wp, wp)
        ) + mass_coef * np.einsum("z,r,c->zrc", wz, wp, wp)
        self.dinv = 1.0 / diag
        upper = element_bound(order)
        lower = cheb_ratio * upper
        center, half = 0.5 * (upper + lower), 0.5 * (upper - lower)
        sigma = center / half
        rho = 1.0 / sigma
        self.first = 1.0 / center
        self.steps = []
        for _ in range(2):
            rho2 = 1.0 / (2.0 * sigma - rho)
            self.steps.append((float(rho2 * rho), 2.0 * rho2 / half))
            rho = rho2
        self.m_p = np.ones(n)
        self.m_p[0] = self.m_p[-1] = 0.5
        self.m_z = np.ones(2 * n)
        self.m_z[n - 1] = self.m_z[n] = 0.5


def hi_lo(matrix):
    matrix = np.asarray(matrix, np.float64)
    hi = matrix.astype(ml_dtypes.bfloat16)
    lo = (matrix - hi.astype(np.float64)).astype(ml_dtypes.bfloat16)
    return hi, lo


def packed_left(matrix):
    hi, lo = hi_lo(matrix)
    return np.block([[hi, hi], [lo, np.zeros_like(lo)]])


def packed_right(matrix):
    hi, lo = hi_lo(matrix)
    return np.block([[hi, lo], [hi, np.zeros_like(lo)]])


FINE, MID, COARSE = Level(7), Level(3), Level(1)
J_FINE, J_MID = interp_table(7, 3), interp_table(3, 1)


def pattern(level, lanes):
    d = level.dinv.reshape(2 * level.n * level.n, level.n)
    return np.tile(d, (1, lanes // level.n))


def fine_constants():
    n = 8
    m1 = (
        0.5 * (np.kron(FINE.k_z, np.diag(FINE.w)) + np.kron(np.diag(FINE.w_z), FINE.k))
        + mass_coef * np.kron(np.diag(FINE.w_z), np.diag(FINE.w))
    )
    dinv = pattern(FINE, 128)
    return dict(
        m1=packed_left(m1),
        kc=packed_right(blocks(FINE.k, 16).T),
        wc=np.tile(FINE.w_p, 16)[None, :].astype(np.float32),
        cf=np.repeat(0.5 * np.kron(FINE.w_z, FINE.w_p)[:, None], 128, axis=1).astype(np.float32),
        d1=(FINE.first * dinv).astype(np.float32),
        d2=(FINE.steps[0][1] * dinv).astype(np.float32),
        d3=(FINE.steps[1][1] * dinv).astype(np.float32),
    )


def mid_operator(rows):
    n = 4
    s = sum_matrix(rows, n, False)
    k_r = s @ blocks(MID.k, rows)
    w_r = np.tile(MID.w_p, rows)
    k_r, w_r = k_r.reshape(rows, n, rows, n), np.diag(w_r).reshape(rows, n, rows, n)
    kz, wz = MID.k_z, np.diag(MID.w_z)
    t = (
        0.5 * np.einsum("zy,eafb->ezafyb", kz, w_r)
        + 0.5 * np.einsum("zy,eafb->ezafyb", wz, k_r)
        + mass_coef * np.einsum("zy,eafb->ezafyb", wz, w_r)
    )
    return t.reshape(rows * 32, rows * 32)


def mid_sum(rows):
    s = sum_matrix(rows, 4, False).reshape(rows, 4, rows, 4)
    return np.einsum("zy,eafb->ezafyb", MID.sum_z, s).reshape(rows * 32, rows * 32)


def mid_constants(rows):
    dinv = np.tile(pattern(MID, 256), (rows, 1))
    kc = sum_matrix(64, 4, True) @ blocks(MID.k, 64)
    kh, kl = hi_lo(kc.T)
    return dict(
        kh=kh,
        kl=kl,
        wc=np.tile(MID.w_p, 64)[None, :].astype(np.float32),
        cf=np.tile(
            np.repeat(0.5 * np.kron(MID.w_z, MID.w_p)[:, None], 256, axis=1), (rows, 1)
        ).astype(np.float32),
        d1=(MID.first * dinv).astype(np.float32),
        d2=(MID.steps[0][1] * dinv).astype(np.float32),
        d3=(MID.steps[1][1] * dinv).astype(np.float32),
    )


def dot(a, b):
    return jnp.dot(a, b, preferred_element_type=f32)


def split(u):
    h = u.astype(bf16)
    return h, (u - h.astype(f32)).astype(bf16)


def dot_left(ch, cl, u):
    h, l = split(u)
    return dot(ch, h) + dot(ch, l) + dot(cl, h)


def dot_right(u, ch, cl):
    h, l = split(u)
    return dot(h, ch) + dot(l, ch) + dot(h, cl)


def wide(tile):
    return jnp.concatenate([tile, tile, tile], axis=-1)


def row_sum(before, here, after):
    lanes = here.shape[-1]
    cube = (16, 8, lanes)
    node = lax.broadcasted_iota(jnp.int32, cube, 1)
    b = pltpu.roll(before.reshape(cube), 1, 1)
    a = pltpu.roll(after.reshape(cube), 7, 1)
    out = here.reshape(cube) + jnp.where(node == 0, b, 0.0) + jnp.where(node == 7, a, 0.0)
    return out.reshape(128, lanes)


def col_sum(y):
    lanes = y.shape[-1]
    node = lax.broadcasted_iota(jnp.int32, y.shape, 1) % 8
    b = pltpu.roll(y, 1, 1)
    a = pltpu.roll(y, lanes - 1, 1)
    return y + jnp.where(node == 0, b, 0.0) + jnp.where(node == 7, a, 0.0)


def fine_apply(us, c):
    parts = [split(u) for u in us]
    m1 = c["m1"][...]
    t = []
    for h, l in parts:
        y = dot(m1, jnp.concatenate([h, l], axis=0))
        t.append(y[:128] + y[128:])
    kc = c["kc"][...]
    wc, cf = wide(c["wc"][...]), wide(c["cf"][...])
    out = []
    for e in range(1, len(us) - 1):
        h, l = parts[e]
        y = []
        for k in range(3):
            s = slice(128 * k, 128 * k + 128)
            z = dot(jnp.concatenate([h[:, s], l[:, s]], axis=1), kc)
            y.append(z[:, :128] + z[:, 128:])
        y = col_sum(jnp.concatenate(y, axis=1))
        out.append(wc * row_sum(t[e - 1], t[e], t[e + 1]) + cf * y)
    return out


def mid_apply(m_h, m_l, u, lo, hi, c):
    h, l = split(u)
    t = dot(m_h, h) + dot(m_h, l) + dot(m_l, h)
    kh, kl = c["kh"][...], c["kl"][...]
    y = dot(h[lo:hi], kh) + dot(l[lo:hi], kh) + dot(h[lo:hi], kl)
    return c["wc"][...] * t + c["cf"][: hi - lo] * y


def call(body, outs, consts, args, vmem=40 * MB):
    names = sorted(consts)

    def kernel(*refs):
        c = dict(zip(names, refs[: len(names)]))
        ins = refs[len(names) : len(names) + len(args)]
        body(c, ins, refs[len(names) + len(args) :])

    spec = pl.BlockSpec(memory_space=pltpu.VMEM)
    return pl.pallas_call(
        kernel,
        out_shape=[jax.ShapeDtypeStruct(s, f32) for s in outs],
        in_specs=[spec] * (len(names) + len(args)),
        out_specs=[spec] * len(outs),
        compiler_params=pltpu.CompilerParams(vmem_limit_bytes=vmem),
    )(*[jnp.asarray(consts[k]) for k in names], *args)


def restrict_rows(level, table, rows):
    z = blocks(table.T, 2) @ np.diag(level.m_z)
    r = table.T @ np.diag(level.m_p)
    return blocks(np.kron(z, r), rows)


def pre_fine(blk, p1, m1, p2, m2):
    consts = fine_constants()
    consts["w"] = np.repeat(0.125 * np.kron(np.tile(FINE.w, 2), FINE.w)[:, None], 128, axis=1).astype(
        np.float32
    ) * np.tile(FINE.w, 16)[None, :].astype(np.float32)
    consts["rh"], consts["rl"] = hi_lo(restrict_rows(FINE, J_FINE, 2))
    consts["ch"], consts["cl"] = hi_lo(blocks(J_FINE.T @ np.diag(FINE.m_p), 32).T)

    def body(c, ins, outs):
        blk, p1, m1, p2, m2 = ins
        w = wide(c["w"][...])
        src = [m2[:128], m1[0], m1[1], blk[0], blk[1], p1[0], p1[1], p2[:128]]
        src = [w * s for s in src]
        lanes = 384
        node = lax.broadcasted_iota(jnp.int32, (16, 8, lanes), 1)
        w_end = w.reshape(16, 8, lanes)[:, 0:1, :]
        low = jnp.broadcast_to(m2[128:].reshape(16, 1, lanes) * w_end, (16, 8, lanes))
        top = jnp.broadcast_to(p2[128:].reshape(16, 1, lanes) * w_end, (16, 8, lanes))
        src = [low.reshape(128, lanes)] + src + [top.reshape(128, lanes)]
        b = []
        for e in range(1, 9):
            y = col_sum(row_sum(src[e - 1], src[e], src[e + 1]))
            mid = y[56:64] + y[64:72]
            b.append(jnp.concatenate([y[:56], mid, mid, y[72:]], axis=0))
        d1, d2, d3 = wide(c["d1"][...]), wide(c["d2"][...]), wide(c["d3"][...])
        d = [d1 * v for v in b]
        x = [d[3], d[4]]
        g = fine_apply(d, c)
        r = [v - a for v, a in zip(b[1:-1], g)]
        d = [FINE.steps[0][0] * v + d2 * a for v, a in zip(d[1:-1], r)]
        x = [x[0] + d[2], x[1] + d[3]]
        g = fine_apply(d, c)
        r = [v - a for v, a in zip(r[1:-1], g)]
        d = [FINE.steps[1][0] * v + d3 * a for v, a in zip(d[1:-1], r)]
        x = [x[0] + d[1], x[1] + d[2]]
        g = fine_apply(d, c)
        r = [v - a for v, a in zip(r[1:-1], g)]
        x0, r0, rhs = outs
        for e in range(2):
            x0[e] = x[e][:, :256]
            r0[e] = r[e]
        own = jnp.concatenate([r[0][:, :256], r[1][:, :256]], axis=0)
        rows = dot_left(c["rh"][...], c["rl"][...], own)
        rhs[...] = dot_right(rows, c["ch"][...], c["cl"][...])

    return call(
        body,
        [(2, 128, 256), (2, 128, 384), (64, 128)],
        consts,
        (blk, p1, m1, p2, m2),
    )


def pre_mid(blk, p1, m1, p2, m2):
    consts = mid_constants(8)
    consts["mh"], consts["ml"] = hi_lo(mid_operator(8))
    consts["sh"] = mid_sum(10)[32:-32].astype(ml_dtypes.bfloat16)
    consts["sc"] = sum_matrix(64, 4, True).T.astype(ml_dtypes.bfloat16)
    z = np.zeros((3, 8))
    zz = blocks(J_MID.T, 2) @ np.diag(MID.m_z)
    z[0], z[1], z[2] = zz[0], zz[1] + zz[2], zz[3]
    r1 = J_MID.T @ np.diag(MID.m_p)
    rr = np.zeros((2, 8, 4, 2, 8, 4))[:, 0, 0]
    rdr = np.zeros((4, 4, 2, 8, 4))
    for e in range(2):
        for k in range(2):
            rdr[e + k, :3, e] += np.einsum("zy,b->zyb", z, r1[k])
    consts["rh"], consts["rl"] = hi_lo(rdr.reshape(16, 64))
    rc = np.zeros((256, 32))
    for v in range(32):
        rc[4 * v : 4 * v + 4, v] += r1[0]
        left = (4 * v - 4) % 256
        rc[left : left + 4, v] += r1[1]
    consts["ch"], consts["cl"] = hi_lo(np.tile(rc, (1, 12)))

    def body(c, ins, outs):
        blk, p1, m1, p2, m2 = ins
        u = jnp.concatenate([m2[...], m1[...], blk[...], p1[...], p2[...]], axis=0)
        h, l = split(u)
        sh, sc = c["sh"][...], c["sc"][...]
        u = dot(sh, h) + dot(sh, l)
        h, l = split(u)
        b = dot(h, sc) + dot(l, sc)
        mh, ml = c["mh"][...], c["ml"][...]
        d = c["d1"][...] * b
        x = d
        r = b - mid_apply(mh, ml, d, 0, 256, c)
        d = MID.steps[0][0] * d + c["d2"][...] * r
        x = x + d
        r = r - mid_apply(mh, ml, d, 0, 256, c)
        d = MID.steps[1][0] * d + c["d3"][...] * r
        x = x + d
        r = r - mid_apply(mh, ml, d, 0, 256, c)
        x1, r1, chunk = outs
        x1[...] = x[64:192]
        own = r[96:160]
        r1[...] = own
        rows = dot_left(c["rh"][...], c["rl"][...], own)
        t = dot_right(rows, c["ch"][...], c["cl"][...])
        q = lax.broadcasted_iota(jnp.int32, t.shape, 0)
        lane = lax.broadcasted_iota(jnp.int32, t.shape, 1) // 32
        t = jnp.sum(jnp.where(q == lane, t, 0.0), axis=0, keepdims=True)
        chunk[...] = jnp.broadcast_to(t, chunk.shape)

    return call(
        body,
        [(128, 256), (64, 256), (256, 384)],
        consts,
        (blk, p1, m1, p2, m2),
    )


def coarse_solve(gathered):
    kz = np.zeros((4, 4))
    kz[:3, :3] = [[0.5, -0.5, 0.0], [-0.5, 1.0, -0.5], [0.0, -0.5, 0.5]]
    wz = np.array([1.0, 2.0, 1.0, 0.0])
    near = np.eye(32, k=1) + np.eye(32, k=-1)
    inner = 2.0 * np.kron(kz, np.eye(32)) + np.kron(np.diag(wz), 2.0 * np.eye(32) - 0.5 * near)
    up, down = np.zeros((32, 32)), np.zeros((32, 32))
    up[0, 31] = -0.5
    down[31, 0] = -0.5
    matrix = np.concatenate([inner, np.kron(np.diag(wz), up), np.kron(np.diag(wz), down)], axis=0)
    consts = dict(
        m=matrix.astype(ml_dtypes.bfloat16),
        wz=np.repeat(wz, 32)[None, :].astype(np.float32),
    )

    def body(c, ins, outs):
        (g,) = ins
        (x_out,) = outs
        m, wz = c["m"][...], c["wz"][...]

        def after(u):
            return jnp.concatenate([u[8:], u[:8]], axis=0)

        def before(u):
            return jnp.concatenate([u[-8:], u[:-8]], axis=0)

        def shifted(u, by):
            return pltpu.roll(u.reshape(32, 8, 128), by, 1).reshape(256, 128)

        def columns(u):
            a = u.astype(bf16)
            rest = u - a.astype(f32)
            b = rest.astype(bf16)
            e = (rest - b.astype(f32)).astype(bf16)
            t = None
            for part in (a, b, e):
                wide_part = part.astype(f32)
                v = dot(
                    jnp.concatenate(
                        [
                            part,
                            shifted(wide_part, 7).astype(bf16),
                            shifted(wide_part, 1).astype(bf16),
                        ],
                        axis=1,
                    ),
                    m,
                )
                t = v if t is None else t + v
            return t

        half = -0.5 * wz
        mass = 4.0 * mass_coef * wz

        def apply(p):
            p0, p1 = p
            return (
                columns(p0) + half * (p1 + before(p1)) + mass * p0,
                columns(p1) + half * (p0 + after(p0)) + mass * p1,
            )

        def inner_product(a, b):
            s = jnp.sum(a[0] * b[0] + a[1] * b[1], axis=0, keepdims=True)
            return jnp.sum(s, axis=1, keepdims=True)

        r = (g[:, 0:128] + before(g[:, 256:384]), g[:, 128:256])
        p = r
        x = (jnp.zeros_like(r[0]), jnp.zeros_like(r[1]))
        norm = inner_product(r, r)
        for it in range(CG_ITERS):
            q = apply(p)
            alpha = norm / inner_product(p, q)
            x = tuple(a + alpha * b for a, b in zip(x, p))
            if it + 1 < CG_ITERS:
                r = tuple(a - alpha * b for a, b in zip(r, q))
                new = inner_product(r, r)
                beta = new / norm
                p = tuple(a + beta * b for a, b in zip(r, p))
                norm = new
        x_out[:, 0:128] = x[0]
        x_out[:, 128:256] = x[1]

    return call(body, [(256, 256)], consts, (gathered,))[0]


def post(x2, mid_x, mid_r, fine_x, fine_r):
    consts = {"f_" + k: v for k, v in fine_constants().items()}
    consts.update({"m_" + k: v for k, v in mid_constants(12).items()})
    mh, ml = hi_lo(mid_operator(14)[32:-32])
    consts["m_mh"], consts["m_ml"] = mh, ml
    jc = np.zeros((3, 3, 4, 32, 256))
    for e in range(64):
        element = e if e < 48 else e - 64
        for k in range(2):
            v = element + k
            dev, col = v // 32 + 1, v % 32
            for z in range(3):
                jc[z, dev, z, col, 4 * e : 4 * e + 4] = J_MID[:, k]
    jc = jc.reshape(3, 384, 256)
    jc = np.concatenate([jc[0], jc[1], jc[2]], axis=1)
    consts["vch"], consts["vcl"] = hi_lo(jc)
    jz = np.zeros((8, 3))
    jz[:4, :2] += J_MID
    jz[4:, 1:] += J_MID
    jdr = np.zeros((14, 8, 4, 3, 16))
    for e in range(14):
        for k in range(2):
            jdr[e, :, :, :, e + k] += np.einsum("zp,a->zap", jz, J_MID[:, k])
    consts["vdh"], consts["vdl"] = hi_lo(jdr.reshape(448, 48))
    fc = np.zeros((256, 384))
    for e in range(48):
        src = e if e < 40 else e + 16
        fc[4 * src : 4 * src + 4, 8 * e : 8 * e + 8] = J_FINE.T
    consts["fch"], consts["fcl"] = hi_lo(fc)
    consts["fdh"], consts["fdl"] = hi_lo(np.kron(blocks(J_FINE, 2), J_FINE))

    def body(c, ins, outs):
        x2, mid_x, mid_r, fine_x, fine_r = ins[:5]
        out, twice, rows = outs[0], outs[1], outs[2]
        i, j = lax.axis_index("gx"), lax.axis_index("gy")
        f = {k[2:]: v for k, v in c.items() if k.startswith("f_")}
        m = {k[2:]: v for k, v in c.items() if k.startswith("m_")}
        twice[0:256] = x2[...]
        twice[256:512] = x2[...]
        first = lax.rem(i + 29, 32)
        picked = twice[pl.ds(pl.multiple_of(first * 8, 8), 64), :].reshape(8, 8, 256)
        sub = lax.broadcasted_iota(jnp.int32, (8, 8, 256), 1)
        for d in range(3):
            own = lax.rem(j + 7 + d, 8)
            v = jnp.sum(jnp.where(sub == own, picked, 0.0), axis=1)
            for k in range(2):
                rows[8 * k : 8 * k + 8, 128 * d : 128 * d + 128] = v[:, 128 * k : 128 * k + 128]
        y = dot_right(rows[...], c["vch"][...], c["vcl"][...])
        y = jnp.concatenate([y[:, :256], y[:, 256:512], y[:, 512:]], axis=0)
        e2 = dot_left(c["vdh"][...], c["vdl"][...], y)
        mh, ml = c["m_mh"], c["m_ml"]
        r = mid_r[...] - mid_apply(mh[...], ml[...], e2, 32, 416, m)
        d = m["d1"][...] * r
        x = mid_x[...] + e2[96:352] + d[64:320]
        r = r[32:352] - mid_apply(mh[:320, :384], ml[:320, :384], d, 32, 352, m)
        d = MID.steps[0][0] * d[32:352] + m["d2"][:320] * r
        x = x + d[32:288]
        r = r[32:288] - mid_apply(mh[:256, :320], ml[:256, :320], d, 32, 288, m)
        d = MID.steps[1][0] * d[32:288] + m["d3"][:256] * r
        x = x + d
        x = dot_right(x, c["fch"][...], c["fcl"][...])
        fdh, fdl = c["fdh"][...], c["fdl"][...]
        e1 = [dot_left(fdh, fdl, x[32 * e : 32 * e + 32]) for e in range(8)]
        g = fine_apply(e1, f)
        r = [fine_r[e] - g[e] for e in range(6)]
        d1, d2, d3 = wide(f["d1"][...]), wide(f["d2"][...]), wide(f["d3"][...])
        d = [d1 * v for v in r]
        x = [fine_x[e] + (e1[3 + e] + d[2 + e])[:, :256] for e in range(2)]
        g = fine_apply(d, f)
        r = [v - a for v, a in zip(r[1:-1], g)]
        d = [FINE.steps[0][0] * v + d2 * a for v, a in zip(d[1:-1], r)]
        x = [x[e] + d[1 + e][:, :256] for e in range(2)]
        g = fine_apply(d, f)
        r = [v - a for v, a in zip(r[1:-1], g)]
        d = [FINE.steps[1][0] * v + d3 * a for v, a in zip(d[1:-1], r)]
        for e in range(2):
            v = (x[e] + d[e][:, :256]).reshape(16, 8, 256)
            out[:, 8 * e : 8 * e + 8, :] = v

    order = [2 * (q % 8) + q // 8 for q in range(16)]
    for name in ("vdh", "vdl"):
        t = consts[name].reshape(448, 3, 16)
        consts[name] = np.ascontiguousarray(t[:, :, order]).reshape(448, 48)

    names = sorted(consts)
    args = (x2, mid_x, mid_r, fine_x, fine_r)

    def kernel(*refs):
        body(
            dict(zip(names, refs[: len(names)])),
            refs[len(names) : len(names) + len(args)],
            refs[len(names) + len(args) :],
        )

    spec = pl.BlockSpec(memory_space=pltpu.VMEM)
    return pl.pallas_call(
        kernel,
        out_shape=jax.ShapeDtypeStruct((16, 16, 256), f32),
        in_specs=[spec] * (len(names) + len(args)),
        out_specs=spec,
        scratch_shapes=[pltpu.VMEM((512, 256), f32), pltpu.VMEM((16, 384), f32)],
        compiler_params=pltpu.CompilerParams(vmem_limit_bytes=48 * MB),
    )(*[jnp.asarray(consts[k]) for k in names], *args)


def fetch(value, axis, offset):
    count = lax.axis_size(axis)
    return lax.ppermute(value, axis, [((i + offset) % count, i) for i in range(count)])


def with_columns(low, high):
    right = fetch(low, "gy", 1)
    left = fetch(high, "gy", -1)
    lane = lax.broadcasted_iota(jnp.int32, right.shape, right.ndim - 1)
    return jnp.where(lane < 64, right, left)


def local(source):
    s = source.reshape(16, 2, 8, 256).transpose(1, 0, 2, 3).reshape(2, 128, 256)
    blk = jnp.concatenate([s, with_columns(s[:, :, :128], s[:, :, 128:])], axis=2)
    faces = blk.reshape(2, 16, 8, 384)
    up = jnp.concatenate([blk[0], faces[1, :, 0]], axis=0)
    down = jnp.concatenate([blk[1], faces[0, :, 7]], axis=0)
    p1, m1 = fetch(blk, "gx", 1), fetch(blk, "gx", -1)
    p2, m2 = fetch(up, "gx", 2), fetch(down, "gx", -2)
    x0, r0, rhs = pre_fine(blk, p1, m1, p2, m2)

    blk = jnp.concatenate([rhs, with_columns(rhs, rhs)], axis=1)
    p1, m1 = fetch(blk, "gx", 1), fetch(blk, "gx", -1)
    p2, m2 = fetch(blk, "gx", 2), fetch(blk, "gx", -2)
    x1, r1, chunk = pre_mid(blk, p1, m1, p2, m2)

    gathered = lax.all_to_all(chunk, ("gx", "gy"), 0, 0, tiled=True)
    r0p, r0m = fetch(r0, "gx", 1), fetch(r0, "gx", -1)
    fine_r = jnp.concatenate([r0m, r0, r0p], axis=0)
    both = jnp.concatenate([r1, x1[32:]], axis=0)
    bothm = jnp.concatenate([r1, x1[:96]], axis=0)
    fp, fm = fetch(both, "gx", 1), fetch(bothm, "gx", -1)
    r2p, r2m = fetch(r1, "gx", 2), fetch(r1, "gx", -2)
    r3p, r3m = fetch(r1[:32], "gx", 3), fetch(r1[32:], "gx", -3)
    mid_r = jnp.concatenate([r3m, r2m, fm[:64], r1, fp[:64], r2p, r3p], axis=0)
    mid_x = jnp.concatenate([fm[64 : 64 + 96], x1[32:96], fp[64 : 64 + 96]], axis=0)
    x2 = coarse_solve(gathered)
    return post(x2, mid_x, mid_r, x0, fine_r)


def solution(mesh):
    return jax.shard_map(
        local,
        mesh=mesh,
        in_specs=(P(None, "gx", "gy"),),
        out_specs=P(None, "gx", "gy"),
        check_vma=False,
    )
```

```python
import math

import jax
import jax.numpy as jnp
import ml_dtypes
import numpy as np
from jax import lax
from jax.experimental import pallas as pl
from jax.experimental.pallas import tpu as pltpu
from jax.sharding import PartitionSpec as P

CG_ITERS = 8
mass_coef = 0.000125
cheb_ratio = 0.1
f32 = jnp.float32
bf16 = jnp.bfloat16
MB = 1024 * 1024


def legendre_pair(points, order):
    previous = 0.0 * points + 1.0
    current = points * 1.0
    for degree in range(2, order + 1):
        previous, current = (
            current,
            ((2.0 * degree - 1.0) * points * current - (degree - 1.0) * previous) / degree,
        )
    return (previous, current)


def gll_tables(order):
    count_nodes = order + 1
    points = -np.cos(math.pi * np.arange(count_nodes) / order)
    for sweep in range(60):
        previous, values_at = legendre_pair(points, order)
        points = points - (points * values_at - previous) / (count_nodes * values_at)
    previous, values_at = legendre_pair(points, order)
    weights = 2.0 / (order * (order + 1) * values_at * values_at)
    spacing = points[:, None] - points[None, :]
    safe_spacing = np.where(spacing == 0.0, 1.0, spacing)
    derivative = values_at[:, None] / (values_at[None, :] * safe_spacing)
    derivative = derivative * (1.0 - np.eye(count_nodes))
    corner_value = order * (order + 1) / 4.0
    end_values = np.concatenate(
        [np.array([-corner_value]), np.zeros(count_nodes - 2), np.array([corner_value])]
    )
    return (points, weights, derivative + np.eye(count_nodes) * end_values[None, :])


def interp_table(fine_order, coarse_order):
    fine_points = gll_tables(fine_order)[0]
    coarse_points = gll_tables(coarse_order)[0]
    numer = fine_points[:, None, None] - coarse_points[None, None, :]
    denom = coarse_points[None, :, None] - coarse_points[None, None, :]
    same_node = np.eye(len(coarse_points))[None, :, :] > 0.5
    ratio = np.where(same_node, 1.0, numer / np.where(same_node, 1.0, denom))
    return ratio.prod(axis=2)


def element_bound(order):
    points, weights, derivative = gll_tables(order)
    mass = np.eye(order + 1) * weights[None, :]
    stiff = np.dot(derivative.T, np.dot(mass, derivative))
    full = 0.5 * (
        np.kron(np.kron(mass, mass), stiff)
        + np.kron(np.kron(mass, stiff), mass)
        + np.kron(np.kron(stiff, mass), mass)
    ) + mass_coef * np.kron(np.kron(mass, mass), mass)
    diagonal_entries = np.sum(full * np.eye(full.shape[0]), axis=1)
    ratio = np.abs(full).sum(axis=1) / diagonal_entries
    return float(ratio.max())


def sum_matrix(elements, n, cyclic):
    out = np.eye(elements * n)
    for e in range(elements):
        if cyclic or e + 1 < elements:
            a, b = e * n + n - 1, ((e + 1) % elements) * n
            out[a, b] += 1.0
            out[b, a] += 1.0
    return out


def blocks(matrix, count):
    return np.kron(np.eye(count), matrix)


class Level:
    def __init__(self, order):
        n = self.n = order + 1
        _, w, dm = gll_tables(order)
        self.w = w
        self.k = dm.T @ np.diag(w) @ dm
        self.sum_z = sum_matrix(2, n, False)
        self.k_z = self.sum_z @ blocks(self.k, 2)
        self.w_z = self.sum_z @ np.tile(w, 2)
        self.w_p = w.copy()
        self.w_p[0] += w[-1]
        self.w_p[-1] += w[0]
        kd = np.diag(self.k).copy()
        kd_p = kd.copy()
        kd_p[0] += kd[-1]
        kd_p[-1] += kd[0]
        kd_z = self.sum_z @ np.tile(kd, 2)
        wz, wp = self.w_z, self.w_p
        diag = 0.5 * (
            np.einsum("z,r,c->zrc", wz, kd_p, wp)
            + np.einsum("z,r,c->zrc", wz, wp, kd_p)
            + np.einsum("z,r,c->zrc", kd_z, wp, wp)
        ) + mass_coef * np.einsum("z,r,c->zrc", wz, wp, wp)
        self.dinv = 1.0 / diag
        upper = element_bound(order)
        lower = cheb_ratio * upper
        center, half = 0.5 * (upper + lower), 0.5 * (upper - lower)
        sigma = center / half
        rho = 1.0 / sigma
        self.first = 1.0 / center
        self.steps = []
        for _ in range(2):
            rho2 = 1.0 / (2.0 * sigma - rho)
            self.steps.append((float(rho2 * rho), 2.0 * rho2 / half))
            rho = rho2
        self.m_p = np.ones(n)
        self.m_p[0] = self.m_p[-1] = 0.5
        self.m_z = np.ones(2 * n)
        self.m_z[n - 1] = self.m_z[n] = 0.5


def hi_lo(matrix):
    matrix = np.asarray(matrix, np.float64)
    hi = matrix.astype(ml_dtypes.bfloat16)
    lo = (matrix - hi.astype(np.float64)).astype(ml_dtypes.bfloat16)
    return hi, lo


def packed_left(matrix):
    hi, lo = hi_lo(matrix)
    return np.block([[hi, hi], [lo, np.zeros_like(lo)]])


def packed_right(matrix):
    hi, lo = hi_lo(matrix)
    return np.block([[hi, lo], [hi, np.zeros_like(lo)]])


FINE, MID, COARSE = Level(7), Level(3), Level(1)
J_FINE, J_MID = interp_table(7, 3), interp_table(3, 1)


def pattern(level, lanes):
    d = level.dinv.reshape(2 * level.n * level.n, level.n)
    return np.tile(d, (1, lanes // level.n))


def closed_operator(level, rows):
    n = level.n
    k_r = sum_matrix(rows, n, False) @ blocks(level.k, rows)
    k_r[0, 0] += level.k[-1, -1]
    k_r[-1, -1] += level.k[0, 0]
    return tensor_rows(level, k_r.reshape(rows, n, rows, n), rows)


def tensor_rows(level, k_r, rows):
    n = level.n
    w_r = np.diag(np.tile(level.w_p, rows)).reshape(rows, n, rows, n)
    kz, wz = level.k_z, np.diag(level.w_z)
    t = (
        0.5 * np.einsum("zy,eafb->ezafyb", kz, w_r)
        + 0.5 * np.einsum("zy,eafb->ezafyb", wz, k_r)
        + mass_coef * np.einsum("zy,eafb->ezafyb", wz, w_r)
    )
    return t.reshape(rows * 2 * n * n, rows * 2 * n * n)


def window_operator(level, rows):
    n = level.n
    k_r = sum_matrix(rows, n, False) @ blocks(level.k, rows)
    size = 2 * n * n
    return tensor_rows(level, k_r.reshape(rows, n, rows, n), rows)[size:-size]


def plane_matrix(n, low, high, count=2):
    t = np.zeros((2, 2 * n, count, 2 * n, n))
    for z in range(2 * n):
        t[0, z, 0, z] = low
        t[1, z, count - 1, z] = high
    return t.reshape(4 * n, count * 2 * n * n)


def inner_lines(level):
    low, high = level.k[0].copy(), level.k[-1].copy()
    low[0] = 0.0
    high[-1] = 0.0
    return low, high


def face_matrix(level, count=2):
    n = level.n
    first, last = np.eye(n)[0], np.eye(n)[-1]
    t = plane_matrix(n, first, last, count).T
    return t * np.tile(0.5 * level.w_z, 2)[None, :]


def pair(consts, name, matrix):
    consts[name + "h"], consts[name + "l"] = hi_lo(matrix)


def fine_constants():
    dinv = pattern(FINE, 128)
    return dict(
        kc=packed_right(blocks(FINE.k, 16).T),
        wc=np.tile(FINE.w_p, 16)[None, :].astype(np.float32),
        cf=np.repeat(0.5 * np.kron(FINE.w_z, FINE.w_p)[:, None], 128, axis=1).astype(np.float32),
        d1=(FINE.first * dinv).astype(np.float32),
        d2=(FINE.steps[0][1] * dinv).astype(np.float32),
        d3=(FINE.steps[1][1] * dinv).astype(np.float32),
    )


def own_constants():
    c = fine_constants()
    pair(c, "m", closed_operator(FINE, 2))
    pair(c, "pl", plane_matrix(8, *inner_lines(FINE)))
    pair(c, "pf", face_matrix(FINE))
    return c


def mid_constants():
    dinv = pattern(MID, 256)
    c = dict(
        wc=np.tile(MID.w_p, 64)[None, :].astype(np.float32),
        cf=np.repeat(0.5 * np.kron(MID.w_z, MID.w_p)[:, None], 256, axis=1).astype(np.float32),
        d1=(MID.first * dinv).astype(np.float32),
        d2=(MID.steps[0][1] * dinv).astype(np.float32),
        d3=(MID.steps[1][1] * dinv).astype(np.float32),
    )
    pair(c, "k", (sum_matrix(64, 4, True) @ blocks(MID.k, 64)).T)
    return c


def mid_own_constants():
    c = mid_constants()
    pair(c, "m", closed_operator(MID, 2))
    pair(c, "pl", plane_matrix(4, *inner_lines(MID)))
    pair(c, "pf", face_matrix(MID))
    return c


def dot(a, b):
    return jnp.dot(a, b, preferred_element_type=f32)


def split(u):
    h = u.astype(bf16)
    return h, (u - h.astype(f32)).astype(bf16)


def left(c, name, parts):
    h, l = parts
    th, tl = c[name + "h"][...], c[name + "l"][...]
    return dot(th, h) + dot(th, l) + dot(tl, h)


def right(c, name, parts):
    h, l = parts
    th, tl = c[name + "h"][...], c[name + "l"][...]
    return dot(h, th) + dot(l, th) + dot(h, tl)


def tiles(ref, rows, lanes):
    t = ref[...]
    if lanes > 1:
        t = jnp.concatenate([t] * lanes, axis=1)
    if rows > 1:
        t = jnp.concatenate([t] * rows, axis=0)
    return t


def row_sum(before, here, after):
    lanes = here.shape[-1]
    cube = (16, 8, lanes)
    node = lax.broadcasted_iota(jnp.int32, cube, 1)
    out = here.reshape(cube)
    if before is not None:
        out = out + jnp.where(node == 0, pltpu.roll(before.reshape(cube), 1, 1), 0.0)
    if after is not None:
        out = out + jnp.where(node == 7, pltpu.roll(after.reshape(cube), 7, 1), 0.0)
    return out.reshape(128, lanes)


def col_sum(y):
    lanes = y.shape[-1]
    node = lax.broadcasted_iota(jnp.int32, y.shape, 1) % 8
    b = pltpu.roll(y, 1, 1)
    a = pltpu.roll(y, lanes - 1, 1)
    return y + jnp.where(node == 0, b, 0.0) + jnp.where(node == 7, a, 0.0)


def col_stiff(parts, kc):
    h, l = parts
    y = []
    for k in range(h.shape[1] // 128):
        s = slice(128 * k, 128 * k + 128)
        z = dot(jnp.concatenate([h[:, s], l[:, s]], axis=1), kc)
        y.append(z[:, :128] + z[:, 128:])
    return col_sum(jnp.concatenate(y, axis=1))


def fine_own(parts, c, planes=None):
    lanes = parts[0].shape[1] // 128
    t = left(c, "m", parts)
    if planes is not None:
        t = t + left(c, "pf", split(planes))
    return tiles(c["wc"], 1, lanes) * t + tiles(c["cf"], 2, lanes) * col_stiff(parts, c["kc"][...])


def mid_apply(t, parts, c):
    y = right(c, "k", parts)
    return c["wc"][...] * t + tiles(c["cf"], t.shape[0] // 32, 1) * y


def mid_own(u, c, planes=None):
    parts = split(u)
    t = left(c, "m", parts)
    if planes is not None:
        t = t + left(c, "pf", split(planes))
    return mid_apply(t, parts, c)


class Table:
    def __init__(self, ref, at, shape, count):
        self.ref, self.at, self.shape, self.count = ref, at, shape, count

    def __getitem__(self, index):
        rows, lanes = self.shape
        step = rows + -rows % 16
        parts = [self.ref[self.at + step * k : self.at + step * k + rows] for k in range(self.count)]
        value = parts[0] if self.count == 1 else jnp.concatenate(parts, axis=1)
        value = value[:, :lanes]
        return value if index is Ellipsis else value[index]


def packed(consts):
    arrays, places = [], {}
    for kind in (np.float32, ml_dtypes.bfloat16):
        pieces, at = [], 0
        for name in sorted(consts):
            t = consts[name]
            if t.dtype != kind:
                continue
            rows, lanes = t.shape
            count = -(-lanes // 128)
            t = np.pad(t, ((0, -rows % 16), (0, count * 128 - lanes)))
            places[name] = (len(arrays), at, (rows, lanes), count)
            pieces += [t[:, 128 * k : 128 * k + 128] for k in range(count)]
            at += count * t.shape[0]
        if pieces:
            arrays.append(np.concatenate(pieces, axis=0))
    return arrays, places


def call(body, outs, consts, args, scratch=(), vmem=24):
    arrays, places = packed(consts)
    n, k = len(arrays), len(args)

    def kernel(*refs):
        c = {name: Table(refs[p[0]], *p[1:]) for name, p in places.items()}
        body(c, refs[n : n + k], refs[n + k :])

    spec = pl.BlockSpec(memory_space=pltpu.VMEM)
    return pl.pallas_call(
        kernel,
        out_shape=[jax.ShapeDtypeStruct(s, f32) for s in outs],
        in_specs=[spec] * (n + k),
        out_specs=[spec] * len(outs),
        scratch_shapes=list(scratch),
        compiler_params=pltpu.CompilerParams(vmem_limit_bytes=vmem * MB),
    )(*[jnp.asarray(a) for a in arrays], *args)


def fine_rhs(source, from_right, from_left):
    c = fine_constants()
    w = np.kron(np.tile(FINE.w, 2), FINE.w)[:, None] * np.tile(FINE.w, 16)[None, :]
    consts = dict(w=(0.125 * w).astype(np.float32), d1=c["d1"])
    pair(consts, "pl", plane_matrix(8, *inner_lines(FINE)))

    def body(c, ins, outs):
        source, from_right, from_left = ins
        b_out, low, high = outs
        w = tiles(c["w"], 1, 4)
        src = []
        for e in range(2):
            s = slice(8 * e, 8 * e + 8)
            src.append(
                jnp.concatenate(
                    [
                        source[:, s, :].reshape(128, 256),
                        from_right[:, s, :].reshape(128, 128),
                        from_left[:, s, :].reshape(128, 128),
                    ],
                    axis=1,
                )
                * w
            )
        b = []
        for y in (row_sum(None, src[0], src[1]), row_sum(src[0], src[1], None)):
            y = col_sum(y)
            inner = y[56:64] + y[64:72]
            b.append(jnp.concatenate([y[:56], inner, inner, y[72:]], axis=0))
        face0 = b[0].reshape(16, 8, 512)[:, 0, :]
        face1 = b[1].reshape(16, 8, 512)[:, 7, :]
        b = jnp.concatenate(b, axis=0)
        b_out[...] = b
        planes = left(c, "pl", split(tiles(c["d1"], 2, 4) * b))
        low[0:16] = face0
        low[16:32] = planes[:16]
        high[0:16] = face1
        high[16:32] = planes[16:]

    return call(
        body, [(256, 512), (32, 512), (32, 512)], consts, (source, from_right, from_left)
    )


def faced(low, high, at, rows):
    return jnp.concatenate([low[at : at + rows], high[at : at + rows]], axis=0)


def fine_middle(b, below, above):
    consts = own_constants()
    consts["f"] = plane_matrix(8, np.eye(8)[0], np.eye(8)[7]).T.astype(ml_dtypes.bfloat16)
    inside = np.ones(8)
    inside[0] = inside[7] = 0.0
    pair(consts, "q", plane_matrix(8, J_FINE[:, 0] * inside, J_FINE[:, 3] * inside))

    def body(c, ins, outs):
        b, below, above = ins
        x_out, r_out, d_out, low, high = outs
        h, l = split(faced(below, above, 0, 16))
        f = c["f"][...]
        b = b[...] + dot(f, h) + dot(f, l)
        d1, d2, d3 = (tiles(c[k], 2, 4) for k in ("d1", "d2", "d3"))
        d = d1 * b
        x = d
        r = b - fine_own(split(d), c, faced(below, above, 16, 16))
        d = FINE.steps[0][0] * d + d2 * r
        x_out[...] = (x + d)[:, :256]
        parts = split(d)
        plane1 = left(c, "pl", parts)
        r = r - fine_own(parts, c)
        d = FINE.steps[1][0] * d + d3 * r
        r_out[...] = r
        d_out[...] = d
        parts = split(d)
        plane2 = left(c, "pl", parts)
        row = lax.broadcasted_iota(jnp.int32, d.shape, 0)
        node = row % 8
        outer = ((row < 128) & (node == 0)) | ((row >= 128) & (node == 7))
        r = r - fine_own(split(jnp.where(outer, 0.0, d)), c)
        plane3 = left(c, "q", split(r))
        for k, plane in enumerate((plane1, plane2, plane3)):
            low[16 * k : 16 * k + 16] = plane[:16]
            high[16 * k : 16 * k + 16] = plane[16:]

    return call(
        body,
        [(256, 256), (256, 512), (256, 512), (48, 512), (48, 512)],
        consts,
        (b, below, above),
    )


def fine_last(x, r, d, below, above):
    consts = {"f_" + k: v for k, v in own_constants().items()}
    consts.update({"m_" + k: v for k, v in mid_own_constants().items()})
    kappa = float(np.sum(J_FINE[1:7, 0] * FINE.k[1:7, 0]))
    t = kappa * plane_matrix(8, np.eye(8)[0], np.eye(8)[7])
    pair(consts, "e", t * np.tile(0.5 * FINE.w_z, 2)[:, None])
    z = MID.sum_z @ blocks(J_FINE.T, 2) @ np.diag(FINE.m_z)
    rows = sum_matrix(2, 4, False) @ blocks(J_FINE.T @ np.diag(FINE.m_p), 2)
    rows[0, 0] += 0.5
    rows[-1, -1] += 0.5
    t = np.einsum("zy,eafb->ezafyb", z, rows.reshape(2, 4, 2, 8)).reshape(64, 256)
    pair(consts, "ra", t)
    t = np.zeros((2, 8, 4, 2, 16))
    t[0, :, 0, 0] = z
    t[1, :, 3, 1] = z
    pair(consts, "rp", t.reshape(64, 32))
    t = sum_matrix(64, 4, True) @ blocks(J_FINE.T @ np.diag(FINE.m_p), 64)
    pair(consts, "rc", t.T)

    def body(c, ins, outs):
        x, r, d, below, above = ins
        x0, r0, b_out, r1_out, low, high = outs
        f = {k[2:]: v for k, v in c.items() if k.startswith("f_")}
        m = {k[2:]: v for k, v in c.items() if k.startswith("m_")}
        wc = tiles(f["wc"], 1, 4)
        change = wc * left(f, "pf", split(faced(below, above, 0, 16)))
        r = r[...] - change
        d = d[...] - tiles(f["d3"], 2, 4) * change
        x0[...] = x[...] + d[:, :256]
        parts = split(d)
        r = r - fine_own(parts, f, faced(below, above, 16, 16))
        lane = lax.broadcasted_iota(jnp.int32, (256, 128), 1)
        r0[:, :256] = r[:, :256]
        r0[:, 256:] = jnp.where(lane < 64, r[:, 256:384], r[:, 384:])
        beyond = faced(below, above, 32, 16) - wc * left(c, "e", parts)
        b = left(c, "ra", split(r)) + left(c, "rp", split(beyond))
        b = right(c, "rc", split(b))
        b_out[...] = b
        d = tiles(m["d1"], 2, 1) * b
        plane1 = left(m, "pl", split(d))
        r = b - mid_own(d, m)
        r1_out[...] = r
        d = MID.steps[0][0] * d + tiles(m["d2"], 2, 1) * r
        plane2 = left(m, "pl", split(d))
        for k, plane in enumerate((plane1, plane2)):
            low[8 * k : 8 * k + 8] = plane[:8]
            high[8 * k : 8 * k + 8] = plane[8:]

    return call(
        body,
        [(256, 256), (256, 384), (64, 256), (64, 256), (16, 256), (16, 256)],
        consts,
        (x, r, d, below, above),
    )


def mid_last(b, r1, below, above):
    consts = mid_own_constants()
    top = np.zeros((3, 4))
    top[0, 0] = top[1, 1] = top[1, 2] = top[2, 3] = 1.0
    jz = top @ blocks(J_MID.T, 2)

    def down(z_part, r_part):
        t = np.zeros((4, 4, 2, 8, 4))
        for e in range(2):
            for k in range(2):
                t[e + k, :3, e] += np.einsum("zy,b->zyb", jz @ z_part, (J_MID.T @ r_part)[k])
        return t.reshape(16, 64)

    def across(part):
        t = np.zeros((256, 32))
        for v in range(32):
            t[4 * v : 4 * v + 4, v] += (J_MID.T @ part)[0]
            at = (4 * v - 4) % 256
            t[at : at + 4, v] += (J_MID.T @ part)[1]
        return np.tile(t, (1, 12))

    wz, wr = blocks(np.diag(MID.w), 2), np.diag(MID.w)
    kz = blocks(MID.k, 2)
    pair(consts, "sm", down(np.diag(MID.m_z), np.diag(MID.m_p)))
    pair(
        consts,
        "s1",
        0.5 * down(kz, wr) + 0.5 * down(wz, MID.k) + mass_coef * down(wz, wr),
    )
    pair(consts, "s2", 0.5 * down(wz, wr))
    pair(
        consts,
        "sc",
        np.concatenate([across(np.diag(MID.m_p)), -across(wr), -across(MID.k)], axis=0),
    )

    def body(c, ins, outs):
        b, r1, below, above = ins
        chunk, lo, hi, lo2, hi2 = outs
        d1, d2, d3 = (tiles(c[k], 2, 1) for k in ("d1", "d2", "d3"))
        d = d1 * b[...]
        x = d
        r = r1[...] - c["wc"][...] * left(c, "pf", split(faced(below, above, 0, 8)))
        d = MID.steps[0][0] * d + d2 * r
        x = x + d
        r = r - mid_own(d, c, faced(below, above, 8, 8))
        d = MID.steps[1][0] * d + d3 * r
        x = x + d
        parts = split(d)
        t = jnp.concatenate(
            [left(c, "sm", split(r)), left(c, "s1", parts), left(c, "s2", parts)], axis=1
        )
        t = right(c, "sc", split(t))
        q = lax.broadcasted_iota(jnp.int32, t.shape, 0)
        lane = lax.broadcasted_iota(jnp.int32, t.shape, 1) // 32
        t = jnp.sum(jnp.where(q == lane, t, 0.0), axis=0, keepdims=True)
        chunk[...] = jnp.broadcast_to(t, chunk.shape)
        plane1 = left(c, "pl", parts)
        r = r - mid_own(d, c)
        plane2 = left(c, "pl", split(d1 * r))
        for near, far, at in ((lo, lo2, 0), (hi, hi2, 1)):
            near[0:64] = r
            near[64:72] = plane1[8 * at : 8 * at + 8]
            near[72:104] = x[32 * at : 32 * at + 32]
            far[0:8] = plane1[8 * at : 8 * at + 8]
            far[8:16] = plane2[8 * at : 8 * at + 8]

    return call(
        body,
        [(256, 384), (104, 256), (104, 256), (16, 256), (16, 256)],
        consts,
        (b, r1, below, above),
    )


def coarse_constants():
    kz = np.zeros((4, 4))
    kz[:3, :3] = [[0.5, -0.5, 0.0], [-0.5, 1.0, -0.5], [0.0, -0.5, 0.5]]
    wz = np.array([1.0, 2.0, 1.0, 0.0])
    near = np.eye(32, k=1) + np.eye(32, k=-1)
    inner = 2.0 * np.kron(kz, np.eye(32)) + np.kron(np.diag(wz), 2.0 * np.eye(32) - 0.5 * near)
    up, down = np.zeros((32, 32)), np.zeros((32, 32))
    up[0, 31] = -0.5
    down[31, 0] = -0.5
    matrix = np.concatenate([inner, np.kron(np.diag(wz), up), np.kron(np.diag(wz), down)], axis=0)
    return dict(
        g_m=matrix.astype(ml_dtypes.bfloat16),
        g_wz=np.repeat(wz, 32)[None, :].astype(np.float32),
    )


def coarse_solve(g, c):
    m, wz = c["g_m"][...], c["g_wz"][...]

    def after(u):
        return jnp.concatenate([u[8:], u[:8]], axis=0)

    def before(u):
        return jnp.concatenate([u[-8:], u[:-8]], axis=0)

    def shifted(u, by):
        return pltpu.roll(u.reshape(32, 8, 128), by, 1).reshape(256, 128)

    def columns(u):
        a = u.astype(bf16)
        rest = u - a.astype(f32)
        b = rest.astype(bf16)
        e = (rest - b.astype(f32)).astype(bf16)
        t = None
        for part in (a, b, e):
            wide_part = part.astype(f32)
            v = dot(
                jnp.concatenate(
                    [
                        part,
                        shifted(wide_part, 7).astype(bf16),
                        shifted(wide_part, 1).astype(bf16),
                    ],
                    axis=1,
                ),
                m,
            )
            t = v if t is None else t + v
        return t

    half = -0.5 * wz
    mass = 4.0 * mass_coef * wz

    def apply(p):
        p0, p1 = p
        return (
            columns(p0) + half * (p1 + before(p1)) + mass * p0,
            columns(p1) + half * (p0 + after(p0)) + mass * p1,
        )

    def inner_product(a, b):
        s = jnp.sum(a[0] * b[0] + a[1] * b[1], axis=0, keepdims=True)
        return jnp.sum(s, axis=1, keepdims=True)

    r = (g[:, 0:128] + before(g[:, 256:384]), g[:, 128:256])
    p = r
    x = (jnp.zeros_like(r[0]), jnp.zeros_like(r[1]))
    norm = inner_product(r, r)
    for it in range(CG_ITERS):
        q = apply(p)
        alpha = norm / inner_product(p, q)
        x = tuple(a + alpha * b for a, b in zip(x, p))
        if it + 1 < CG_ITERS:
            r = tuple(a - alpha * b for a, b in zip(r, q))
            new = inner_product(r, r)
            beta = new / norm
            p = tuple(a + beta * b for a, b in zip(r, p))
            norm = new
    return jnp.concatenate(x, axis=1)


def second_smoothing(gathered, x0, r0, own_lo, own_hi, below, above, below2, above2):
    consts = coarse_constants()
    consts.update({"f_" + k: v for k, v in own_constants().items()})
    consts.update({"m_" + k: v for k, v in mid_constants().items()})
    pair(consts, "a", window_operator(MID, 10))
    pair(consts, "c", closed_operator(MID, 6))
    pair(consts, "p6", face_matrix(MID, 6))
    pair(consts, "p3", blocks(face_matrix(MID), 3))
    low, high = inner_lines(MID)
    pair(consts, "pl", plane_matrix(4, high, low))
    jc = np.zeros((3, 3, 4, 32, 256))
    for e in range(64):
        element = e if e < 48 else e - 64
        for k in range(2):
            v = element + k
            dev, col = v // 32 + 1, v % 32
            for z in range(3):
                jc[z, dev, z, col, 4 * e : 4 * e + 4] = J_MID[:, k]
    jc = jc.reshape(3, 384, 256)
    pair(consts, "vc", np.concatenate([jc[0], jc[1], jc[2]], axis=1))
    jz = np.zeros((8, 3))
    jz[:4, :2] += J_MID
    jz[4:, 1:] += J_MID
    jdr = np.zeros((10, 8, 4, 3, 16))
    for e in range(10):
        for k in range(2):
            jdr[e, :, :, :, e + k] += np.einsum("zp,a->zap", jz, J_MID[:, k])
    order = [2 * (q % 8) + q // 8 for q in range(16)]
    pair(consts, "vd", jdr[..., order].reshape(320, 48))
    fc = np.zeros((256, 384))
    for e in range(48):
        src = e if e < 40 else e + 16
        fc[4 * src : 4 * src + 4, 8 * e : 8 * e + 8] = J_FINE.T
    pair(consts, "fc", fc)
    fd = np.kron(blocks(J_FINE, 2), J_FINE)
    pair(consts, "fd", blocks(fd, 2))
    low, high = inner_lines(FINE)
    pair(consts, "fp", plane_matrix(8, high, low) @ blocks(fd, 2))

    def body(c, ins, outs):
        gathered, x0, r0, own_lo, own_hi, below, above, below2, above2 = ins
        s_out, r_out, d_out, low, high, twice, rows = outs
        i, j = lax.axis_index("gx"), lax.axis_index("gy")
        f = {k[2:]: v for k, v in c.items() if k.startswith("f_")}
        m = {k[2:]: v for k, v in c.items() if k.startswith("m_")}
        x2 = coarse_solve(gathered, c)
        twice[0:256] = x2
        twice[256:512] = x2
        first = lax.rem(i + 30, 32)
        picked = twice[pl.ds(pl.multiple_of(first * 8, 8), 64), :].reshape(8, 8, 256)
        sub = lax.broadcasted_iota(jnp.int32, (8, 8, 256), 1)
        for g in range(3):
            v = jnp.sum(jnp.where(sub == lax.rem(j + 7 + g, 8), picked, 0.0), axis=1)
            for k in range(2):
                rows[8 * k : 8 * k + 8, 128 * g : 128 * g + 128] = v[:, 128 * k : 128 * k + 128]
        y = right(c, "vc", split(rows[...]))
        y = jnp.concatenate([y[:, :256], y[:, 256:512], y[:, 512:]], axis=0)
        e2 = left(c, "vd", split(y))

        def window(u, size):
            h, l = split(u)
            th, tl = c["ah"][:size, : size + 64], c["al"][:size, : size + 64]
            t = dot(th, h) + dot(th, l) + dot(tl, h)
            return mid_apply(t, (h[32:-32], l[32:-32]), m)

        def table(name, count):
            return tiles(m[name], count, 1)

        planes = jnp.concatenate(
            [
                below2[:8],
                own_lo[64:72],
                below[64:72],
                above[64:72],
                own_hi[64:72],
                above2[:8],
            ],
            axis=0,
        )
        g = window(e2, 256)
        r = jnp.concatenate([below[:64], own_lo[:64], above[:64]], axis=0)
        r = r - m["wc"][...] * left(c, "p3", split(planes)) - g[32:224]
        d = table("d1", 6) * r
        x = jnp.concatenate([below[72:104], own_lo[72:104], own_hi[72:104], above[72:104]], axis=0)
        x = x + e2[96:224] + d[32:160]
        outer = jnp.concatenate([g[:32], g[224:]], axis=0) * table("d1", 2)
        planes = faced(below2, above2, 8, 8) - left(c, "pl", split(outer))
        parts = split(d)
        r = r - mid_apply(left(c, "c", parts) + left(c, "p6", split(planes)), parts, m)
        d = MID.steps[0][0] * d + table("d2", 6) * r
        x = x + d[32:160]
        r = r[32:160] - window(d, 128)
        d = MID.steps[1][0] * d[32:160] + table("d3", 4) * r
        x = x + d
        x = right(c, "fc", split(x))
        e1 = left(c, "fd", split(x[32:96]))
        planes = left(c, "fp", split(jnp.concatenate([x[:32], x[96:]], axis=0)))
        r = r0[...] - fine_own(split(e1), f, planes)
        d = tiles(f["d1"], 2, 3) * r
        s_out[...] = x0[...] + (e1 + d)[:, :256]
        parts = split(d)
        plane1 = left(f, "pl", parts)
        r = r - fine_own(parts, f)
        d = FINE.steps[0][0] * d + tiles(f["d2"], 2, 3) * r
        plane2 = left(f, "pl", split(d))
        r_out[...] = r
        d_out[...] = d
        for k, plane in enumerate((plane1, plane2)):
            low[16 * k : 16 * k + 16] = plane[:16]
            high[16 * k : 16 * k + 16] = plane[16:]

    return call(
        body,
        [(256, 256), (256, 384), (256, 384), (32, 384), (32, 384)],
        consts,
        (gathered, x0, r0, own_lo, own_hi, below, above, below2, above2),
        scratch=[pltpu.VMEM((512, 256), f32), pltpu.VMEM((16, 384), f32)],
    )


def last_step(s, r, d, below, above):
    consts = own_constants()

    def body(c, ins, outs):
        s, r, d, below, above = ins
        (out,) = outs
        change = tiles(c["wc"], 1, 3) * left(c, "pf", split(faced(below, above, 0, 16)))
        r = r[...] - change
        d = d[...] - tiles(c["d2"], 2, 3) * change
        r = r - fine_own(split(d), c, faced(below, above, 16, 16))
        v = s[...] + d[:, :256]
        d = FINE.steps[1][0] * d + tiles(c["d3"], 2, 3) * r
        v = v + d[:, :256]
        for e in range(2):
            out[:, 8 * e : 8 * e + 8, :] = v[128 * e : 128 * e + 128].reshape(16, 8, 256)

    return call(body, [(16, 16, 256)], consts, (s, r, d, below, above))[0]


def fetch(value, axis, offset):
    count = lax.axis_size(axis)
    return lax.ppermute(value, axis, [((i + offset) % count, i) for i in range(count)])


def both(low, high, offset=1):
    return fetch(high, "gx", -offset), fetch(low, "gx", offset)


def local(source):
    from_right = fetch(source[:, :, :128], "gy", 1)
    from_left = fetch(source[:, :, 128:], "gy", -1)
    b, low, high = fine_rhs(source, from_right, from_left)
    x, r, d, low, high = fine_middle(b, *both(low, high))
    x0, r0, b, r1, low, high = fine_last(x, r, d, *both(low, high))
    chunk, lo, hi, lo2, hi2 = mid_last(b, r1, *both(low, high))
    gathered = lax.all_to_all(chunk, ("gx", "gy"), 0, 0, tiled=True)
    s, r, d, low, high = second_smoothing(
        gathered, x0, r0, lo, hi, *both(lo, hi), *both(lo2, hi2, 2)
    )
    return last_step(s, r, d, *both(low, high))


def solution(mesh):
    return jax.shard_map(
        local,
        mesh=mesh,
        in_specs=(P(None, "gx", "gy"),),
        out_specs=P(None, "gx", "gy"),
        check_vma=False,
    )
```

```python
import math

import jax
import jax.numpy as jnp
import ml_dtypes
import numpy as np
from jax import lax
from jax.experimental import pallas as pl
from jax.experimental.pallas import tpu as pltpu
from jax.sharding import PartitionSpec as P

CG_ITERS = 8
mass_coef = 0.000125
cheb_ratio = 0.1
f32 = jnp.float32
bf16 = jnp.bfloat16
MB = 1024 * 1024


def legendre_pair(points, order):
    previous = 0.0 * points + 1.0
    current = points * 1.0
    for degree in range(2, order + 1):
        previous, current = (
            current,
            ((2.0 * degree - 1.0) * points * current - (degree - 1.0) * previous) / degree,
        )
    return (previous, current)


def gll_tables(order):
    count_nodes = order + 1
    points = -np.cos(math.pi * np.arange(count_nodes) / order)
    for sweep in range(60):
        previous, values_at = legendre_pair(points, order)
        points = points - (points * values_at - previous) / (count_nodes * values_at)
    previous, values_at = legendre_pair(points, order)
    weights = 2.0 / (order * (order + 1) * values_at * values_at)
    spacing = points[:, None] - points[None, :]
    safe_spacing = np.where(spacing == 0.0, 1.0, spacing)
    derivative = values_at[:, None] / (values_at[None, :] * safe_spacing)
    derivative = derivative * (1.0 - np.eye(count_nodes))
    corner_value = order * (order + 1) / 4.0
    end_values = np.concatenate(
        [np.array([-corner_value]), np.zeros(count_nodes - 2), np.array([corner_value])]
    )
    return (points, weights, derivative + np.eye(count_nodes) * end_values[None, :])


def interp_table(fine_order, coarse_order):
    fine_points = gll_tables(fine_order)[0]
    coarse_points = gll_tables(coarse_order)[0]
    numer = fine_points[:, None, None] - coarse_points[None, None, :]
    denom = coarse_points[None, :, None] - coarse_points[None, None, :]
    same_node = np.eye(len(coarse_points))[None, :, :] > 0.5
    ratio = np.where(same_node, 1.0, numer / np.where(same_node, 1.0, denom))
    return ratio.prod(axis=2)


def element_bound(order):
    points, weights, derivative = gll_tables(order)
    mass = np.eye(order + 1) * weights[None, :]
    stiff = np.dot(derivative.T, np.dot(mass, derivative))
    full = 0.5 * (
        np.kron(np.kron(mass, mass), stiff)
        + np.kron(np.kron(mass, stiff), mass)
        + np.kron(np.kron(stiff, mass), mass)
    ) + mass_coef * np.kron(np.kron(mass, mass), mass)
    diagonal_entries = np.sum(full * np.eye(full.shape[0]), axis=1)
    ratio = np.abs(full).sum(axis=1) / diagonal_entries
    return float(ratio.max())


def sum_matrix(elements, n, cyclic):
    out = np.eye(elements * n)
    for e in range(elements):
        if cyclic or e + 1 < elements:
            a, b = e * n + n - 1, ((e + 1) % elements) * n
            out[a, b] += 1.0
            out[b, a] += 1.0
    return out


def blocks(matrix, count):
    return np.kron(np.eye(count), matrix)


class Level:
    def __init__(self, order):
        n = self.n = order + 1
        _, w, dm = gll_tables(order)
        self.w = w
        self.k = dm.T @ np.diag(w) @ dm
        self.sum_z = sum_matrix(2, n, False)
        self.k_z = self.sum_z @ blocks(self.k, 2)
        self.w_z = self.sum_z @ np.tile(w, 2)
        self.w_p = w.copy()
        self.w_p[0] += w[-1]
        self.w_p[-1] += w[0]
        kd = np.diag(self.k).copy()
        kd_p = kd.copy()
        kd_p[0] += kd[-1]
        kd_p[-1] += kd[0]
        kd_z = self.sum_z @ np.tile(kd, 2)
        wz, wp = self.w_z, self.w_p
        diag = 0.5 * (
            np.einsum("z,r,c->zrc", wz, kd_p, wp)
            + np.einsum("z,r,c->zrc", wz, wp, kd_p)
            + np.einsum("z,r,c->zrc", kd_z, wp, wp)
        ) + mass_coef * np.einsum("z,r,c->zrc", wz, wp, wp)
        self.dinv = 1.0 / diag
        upper = element_bound(order)
        lower = cheb_ratio * upper
        center, half = 0.5 * (upper + lower), 0.5 * (upper - lower)
        sigma = center / half
        rho = 1.0 / sigma
        self.first = 1.0 / center
        self.steps = []
        for _ in range(2):
            rho2 = 1.0 / (2.0 * sigma - rho)
            self.steps.append((float(rho2 * rho), 2.0 * rho2 / half))
            rho = rho2
        self.m_p = np.ones(n)
        self.m_p[0] = self.m_p[-1] = 0.5
        self.m_z = np.ones(2 * n)
        self.m_z[n - 1] = self.m_z[n] = 0.5


def hi_lo(matrix):
    matrix = np.asarray(matrix, np.float64)
    hi = matrix.astype(ml_dtypes.bfloat16)
    lo = (matrix - hi.astype(np.float64)).astype(ml_dtypes.bfloat16)
    return hi, lo


def packed_left(matrix):
    hi, lo = hi_lo(matrix)
    return np.block([[hi, hi], [lo, np.zeros_like(lo)]])


def packed_right(matrix):
    hi, lo = hi_lo(matrix)
    return np.block([[hi, lo], [hi, np.zeros_like(lo)]])


FINE, MID, COARSE = Level(7), Level(3), Level(1)
J_FINE, J_MID = interp_table(7, 3), interp_table(3, 1)


def pattern(level, lanes):
    d = level.dinv.reshape(2 * level.n * level.n, level.n)
    return np.tile(d, (1, lanes // level.n))


def closed_operator(level, rows):
    n = level.n
    k_r = sum_matrix(rows, n, False) @ blocks(level.k, rows)
    k_r[0, 0] += level.k[-1, -1]
    k_r[-1, -1] += level.k[0, 0]
    return tensor_rows(level, k_r.reshape(rows, n, rows, n), rows)


def tensor_rows(level, k_r, rows):
    n = level.n
    w_r = np.diag(np.tile(level.w_p, rows)).reshape(rows, n, rows, n)
    kz, wz = level.k_z, np.diag(level.w_z)
    t = (
        0.5 * np.einsum("zy,eafb->ezafyb", kz, w_r)
        + 0.5 * np.einsum("zy,eafb->ezafyb", wz, k_r)
        + mass_coef * np.einsum("zy,eafb->ezafyb", wz, w_r)
    )
    return t.reshape(rows * 2 * n * n, rows * 2 * n * n)


def window_operator(level, rows):
    n = level.n
    k_r = sum_matrix(rows, n, False) @ blocks(level.k, rows)
    size = 2 * n * n
    return tensor_rows(level, k_r.reshape(rows, n, rows, n), rows)[size:-size]


def plane_matrix(n, low, high, count=2):
    t = np.zeros((2, 2 * n, count, 2 * n, n))
    for z in range(2 * n):
        t[0, z, 0, z] = low
        t[1, z, count - 1, z] = high
    return t.reshape(4 * n, count * 2 * n * n)


def inner_lines(level):
    low, high = level.k[0].copy(), level.k[-1].copy()
    low[0] = 0.0
    high[-1] = 0.0
    return low, high


def face_matrix(level, count=2):
    n = level.n
    first, last = np.eye(n)[0], np.eye(n)[-1]
    t = plane_matrix(n, first, last, count).T
    return t * np.tile(0.5 * level.w_z, 2)[None, :]


def pair(consts, name, matrix):
    consts[name + "h"], consts[name + "l"] = hi_lo(matrix)


def fine_constants():
    dinv = pattern(FINE, 128)
    return dict(
        kc=packed_right(blocks(FINE.k, 16).T),
        wc=np.tile(FINE.w_p, 16)[None, :].astype(np.float32),
        cf=np.repeat(0.5 * np.kron(FINE.w_z, FINE.w_p)[:, None], 128, axis=1).astype(np.float32),
        d1=(FINE.first * dinv).astype(np.float32),
        d2=(FINE.steps[0][1] * dinv).astype(np.float32),
        d3=(FINE.steps[1][1] * dinv).astype(np.float32),
    )


def own_constants():
    c = fine_constants()
    pair(c, "m", closed_operator(FINE, 2))
    pair(c, "pl", plane_matrix(8, *inner_lines(FINE)))
    pair(c, "pf", face_matrix(FINE))
    return c


def mid_constants():
    dinv = pattern(MID, 256)
    c = dict(
        wc=np.tile(MID.w_p, 64)[None, :].astype(np.float32),
        cf=np.repeat(0.5 * np.kron(MID.w_z, MID.w_p)[:, None], 256, axis=1).astype(np.float32),
        d1=(MID.first * dinv).astype(np.float32),
        d2=(MID.steps[0][1] * dinv).astype(np.float32),
        d3=(MID.steps[1][1] * dinv).astype(np.float32),
    )
    pair(c, "k", (sum_matrix(64, 4, True) @ blocks(MID.k, 64)).T)
    return c


def mid_own_constants():
    c = mid_constants()
    pair(c, "m", closed_operator(MID, 2))
    pair(c, "pl", plane_matrix(4, *inner_lines(MID)))
    pair(c, "pf", face_matrix(MID))
    return c


def dot(a, b):
    return jnp.dot(a, b, preferred_element_type=f32)


def split(u):
    h = u.astype(bf16)
    return h, (u - h.astype(f32)).astype(bf16)


def left(c, name, parts):
    h, l = parts
    th, tl = c[name + "h"][...], c[name + "l"][...]
    return dot(th, h) + dot(th, l) + dot(tl, h)


def right(c, name, parts):
    h, l = parts
    th, tl = c[name + "h"][...], c[name + "l"][...]
    return dot(h, th) + dot(l, th) + dot(h, tl)


def tiles(ref, rows, lanes):
    t = ref[...]
    if lanes > 1:
        t = jnp.concatenate([t] * lanes, axis=1)
    if rows > 1:
        t = jnp.concatenate([t] * rows, axis=0)
    return t


def row_sum(before, here, after):
    lanes = here.shape[-1]
    cube = (16, 8, lanes)
    node = lax.broadcasted_iota(jnp.int32, cube, 1)
    out = here.reshape(cube)
    if before is not None:
        out = out + jnp.where(node == 0, pltpu.roll(before.reshape(cube), 1, 1), 0.0)
    if after is not None:
        out = out + jnp.where(node == 7, pltpu.roll(after.reshape(cube), 7, 1), 0.0)
    return out.reshape(128, lanes)


def col_sum(y):
    lanes = y.shape[-1]
    node = lax.broadcasted_iota(jnp.int32, y.shape, 1) % 8
    b = pltpu.roll(y, 1, 1)
    a = pltpu.roll(y, lanes - 1, 1)
    return y + jnp.where(node == 0, b, 0.0) + jnp.where(node == 7, a, 0.0)


def col_stiff(parts, kc):
    h, l = parts
    y = []
    for k in range(h.shape[1] // 128):
        s = slice(128 * k, 128 * k + 128)
        z = dot(jnp.concatenate([h[:, s], l[:, s]], axis=1), kc)
        y.append(z[:, :128] + z[:, 128:])
    return col_sum(jnp.concatenate(y, axis=1))


def fine_own(parts, c, planes=None):
    lanes = parts[0].shape[1] // 128
    t = left(c, "m", parts)
    if planes is not None:
        t = t + left(c, "pf", split(planes))
    return tiles(c["wc"], 1, lanes) * t + tiles(c["cf"], 2, lanes) * col_stiff(parts, c["kc"][...])


def mid_apply(t, parts, c):
    y = right(c, "k", parts)
    return c["wc"][...] * t + tiles(c["cf"], t.shape[0] // 32, 1) * y


def mid_own(u, c, planes=None):
    parts = split(u)
    t = left(c, "m", parts)
    if planes is not None:
        t = t + left(c, "pf", split(planes))
    return mid_apply(t, parts, c)


class Table:
    def __init__(self, ref, at, shape, count):
        self.ref, self.at, self.shape, self.count = ref, at, shape, count

    def __getitem__(self, index):
        rows, lanes = self.shape
        step = rows + -rows % 16
        parts = [self.ref[self.at + step * k : self.at + step * k + rows] for k in range(self.count)]
        value = parts[0] if self.count == 1 else jnp.concatenate(parts, axis=1)
        value = value[:, :lanes]
        return value if index is Ellipsis else value[index]


def packed(consts):
    arrays, places = [], {}
    for kind in (np.float32, ml_dtypes.bfloat16):
        pieces, at = [], 0
        for name in sorted(consts):
            t = consts[name]
            if t.dtype != kind:
                continue
            rows, lanes = t.shape
            count = -(-lanes // 128)
            t = np.pad(t, ((0, -rows % 16), (0, count * 128 - lanes)))
            places[name] = (len(arrays), at, (rows, lanes), count)
            pieces += [t[:, 128 * k : 128 * k + 128] for k in range(count)]
            at += count * t.shape[0]
        if pieces:
            arrays.append(np.concatenate(pieces, axis=0))
    return arrays, places


def ready(held):
    def body(c, ins, outs):
        outs[0][...] = jnp.zeros((8, 128), f32)

    return call(body, [(8, 128)], held, ())[0]


def call(body, outs, held, args, scratch=(), vmem=24):
    arrays, places = held
    n, k = len(arrays), len(args)

    def kernel(*refs):
        c = {name: Table(refs[p[0]], *p[1:]) for name, p in places.items()}
        body(c, refs[n : n + k], refs[n + k :])

    spec = pl.BlockSpec(memory_space=pltpu.VMEM)
    return pl.pallas_call(
        kernel,
        out_shape=[jax.ShapeDtypeStruct(s, f32) for s in outs],
        in_specs=[spec] * (n + k),
        out_specs=[spec] * len(outs),
        scratch_shapes=list(scratch),
        compiler_params=pltpu.CompilerParams(vmem_limit_bytes=vmem * MB),
    )(*arrays, *args)


def under(c, prefix):
    return {k[2:]: v for k, v in c.items() if k.startswith(prefix)}


def rhs_tables(consts):
    w = np.kron(np.tile(FINE.w, 2), FINE.w)[:, None] * np.tile(FINE.w, 16)[None, :]
    consts["w"] = (0.125 * w).astype(np.float32)


def fine_rhs(held, first, second, from_right, from_left, at_hand):
    def body(c, ins, outs):
        parts = ins[:4]
        b_out, low, high = outs
        w = tiles(c["w"], 1, 4)
        src = []
        for e in range(2):
            s = slice(8 * e, 8 * e + 8)
            src.append(jnp.concatenate([v[:, s, :].reshape(128, 128) for v in parts], axis=1) * w)
        b = []
        for y in (row_sum(None, src[0], src[1]), row_sum(src[0], src[1], None)):
            y = col_sum(y)
            inner = y[56:64] + y[64:72]
            b.append(jnp.concatenate([y[:56], inner, inner, y[72:]], axis=0))
        face0 = b[0].reshape(16, 8, 512)[:, 0, :]
        face1 = b[1].reshape(16, 8, 512)[:, 7, :]
        b = jnp.concatenate(b, axis=0)
        b_out[...] = b
        planes = left(c, "f_pl", split(tiles(c["f_d1"], 2, 4) * b))
        low[0:16] = face0
        low[16:32] = planes[:16]
        high[0:16] = face1
        high[16:32] = planes[16:]

    return call(
        body,
        [(256, 512), (32, 512), (32, 512)],
        held,
        (first, second, from_right, from_left, at_hand),
    )


def faced(low, high, at, rows):
    return jnp.concatenate([low[at : at + rows], high[at : at + rows]], axis=0)


def middle_tables(consts):
    consts["f"] = plane_matrix(8, np.eye(8)[0], np.eye(8)[7]).T.astype(ml_dtypes.bfloat16)
    inside = np.ones(8)
    inside[0] = inside[7] = 0.0
    pair(consts, "q", plane_matrix(8, J_FINE[:, 0] * inside, J_FINE[:, 3] * inside))


def fine_middle(held, b, below, above):
    def body(c, ins, outs):
        b, below, above = ins
        x_out, r_out, d_out, low, high = outs
        h, l = split(faced(below, above, 0, 16))
        f = c["f"][...]
        b = b[...] + dot(f, h) + dot(f, l)
        q = {"h": c["qh"], "l": c["ql"]}
        c = under(c, "f_")
        d1, d2, d3 = (tiles(c[k], 2, 4) for k in ("d1", "d2", "d3"))
        d = d1 * b
        x = d
        r = b - fine_own(split(d), c, faced(below, above, 16, 16))
        d = FINE.steps[0][0] * d + d2 * r
        x_out[...] = (x + d)[:, :256]
        parts = split(d)
        plane1 = left(c, "pl", parts)
        r = r - fine_own(parts, c)
        d = FINE.steps[1][0] * d + d3 * r
        r_out[...] = r
        d_out[...] = d
        parts = split(d)
        plane2 = left(c, "pl", parts)
        row = lax.broadcasted_iota(jnp.int32, d.shape, 0)
        node = row % 8
        outer = ((row < 128) & (node == 0)) | ((row >= 128) & (node == 7))
        r = r - fine_own(split(jnp.where(outer, 0.0, d)), c)
        plane3 = left(q, "", split(r))
        for k, plane in enumerate((plane1, plane2, plane3)):
            low[16 * k : 16 * k + 16] = plane[:16]
            high[16 * k : 16 * k + 16] = plane[16:]

    return call(
        body,
        [(256, 256), (256, 512), (256, 512), (48, 512), (48, 512)],
        held,
        (b, below, above),
    )


def last_tables(consts):
    kappa = float(np.sum(J_FINE[1:7, 0] * FINE.k[1:7, 0]))
    t = kappa * plane_matrix(8, np.eye(8)[0], np.eye(8)[7])
    pair(consts, "e", t * np.tile(0.5 * FINE.w_z, 2)[:, None])
    z = MID.sum_z @ blocks(J_FINE.T, 2) @ np.diag(FINE.m_z)
    rows = sum_matrix(2, 4, False) @ blocks(J_FINE.T @ np.diag(FINE.m_p), 2)
    rows[0, 0] += 0.5
    rows[-1, -1] += 0.5
    t = np.einsum("zy,eafb->ezafyb", z, rows.reshape(2, 4, 2, 8)).reshape(64, 256)
    pair(consts, "ra", t)
    t = np.zeros((2, 8, 4, 2, 16))
    t[0, :, 0, 0] = z
    t[1, :, 3, 1] = z
    pair(consts, "rp", t.reshape(64, 32))
    t = sum_matrix(64, 4, True) @ blocks(J_FINE.T @ np.diag(FINE.m_p), 64)
    pair(consts, "rc", t.T)


def fine_last(held, x, r, d, below, above):
    def body(c, ins, outs):
        x, r, d, below, above = ins
        x0, r0, b_out, r1_out, low, high = outs
        f, m = under(c, "f_"), under(c, "m_")
        wc = tiles(f["wc"], 1, 4)
        change = wc * left(f, "pf", split(faced(below, above, 0, 16)))
        r = r[...] - change
        d = d[...] - tiles(f["d3"], 2, 4) * change
        x0[...] = x[...] + d[:, :256]
        parts = split(d)
        r = r - fine_own(parts, f, faced(below, above, 16, 16))
        lane = lax.broadcasted_iota(jnp.int32, (256, 128), 1)
        r0[:, :256] = r[:, :256]
        r0[:, 256:] = jnp.where(lane < 64, r[:, 256:384], r[:, 384:])
        beyond = faced(below, above, 32, 16) - wc * left(c, "e", parts)
        b = left(c, "ra", split(r)) + left(c, "rp", split(beyond))
        b = right(c, "rc", split(b))
        b_out[...] = b
        d = tiles(m["d1"], 2, 1) * b
        plane1 = left(m, "pl", split(d))
        r = b - mid_own(d, m)
        r1_out[...] = r
        d = MID.steps[0][0] * d + tiles(m["d2"], 2, 1) * r
        plane2 = left(m, "pl", split(d))
        for k, plane in enumerate((plane1, plane2)):
            low[8 * k : 8 * k + 8] = plane[:8]
            high[8 * k : 8 * k + 8] = plane[8:]

    return call(
        body,
        [(256, 256), (256, 384), (64, 256), (64, 256), (16, 256), (16, 256)],
        held,
        (x, r, d, below, above),
    )


def share_tables(consts):
    top = np.zeros((3, 4))
    top[0, 0] = top[1, 1] = top[1, 2] = top[2, 3] = 1.0
    jz = top @ blocks(J_MID.T, 2)

    def down(z_part, r_part):
        t = np.zeros((4, 4, 2, 8, 4))
        for e in range(2):
            for k in range(2):
                t[e + k, :3, e] += np.einsum("zy,b->zyb", jz @ z_part, (J_MID.T @ r_part)[k])
        return t.reshape(16, 64)

    def across(part):
        t = np.zeros((256, 32))
        for v in range(32):
            t[4 * v : 4 * v + 4, v] += (J_MID.T @ part)[0]
            at = (4 * v - 4) % 256
            t[at : at + 4, v] += (J_MID.T @ part)[1]
        return np.tile(t, (1, 4))

    wz, wr = blocks(np.diag(MID.w), 2), np.diag(MID.w)
    kz = blocks(MID.k, 2)
    pair(consts, "sm", down(np.diag(MID.m_z), np.diag(MID.m_p)))
    pair(
        consts,
        "s1",
        0.5 * down(kz, wr) + 0.5 * down(wz, MID.k) + mass_coef * down(wz, wr),
    )
    pair(consts, "s2", 0.5 * down(wz, wr))
    pair(
        consts,
        "sc",
        np.concatenate([across(np.diag(MID.m_p)), -across(wr), -across(MID.k)], axis=0),
    )


def mid_last(held, b, r1, below, above):
    def body(c, ins, outs):
        b, r1, below, above = ins
        down, c = c, under(c, "m_")
        chunk, lo, hi, lo2, hi2 = outs
        d1, d2, d3 = (tiles(c[k], 2, 1) for k in ("d1", "d2", "d3"))
        d = d1 * b[...]
        x = d
        r = r1[...] - c["wc"][...] * left(c, "pf", split(faced(below, above, 0, 8)))
        d = MID.steps[0][0] * d + d2 * r
        x = x + d
        r = r - mid_own(d, c, faced(below, above, 8, 8))
        d = MID.steps[1][0] * d + d3 * r
        x = x + d
        parts = split(d)
        t = jnp.concatenate(
            [left(down, "sm", split(r)), left(down, "s1", parts), left(down, "s2", parts)], axis=1
        )
        t = right(down, "sc", split(t))
        t = jnp.concatenate([t, t, t], axis=1)
        q = lax.broadcasted_iota(jnp.int32, t.shape, 0)
        lane = lax.broadcasted_iota(jnp.int32, t.shape, 1) // 32
        chunk[...] = jnp.sum(jnp.where(q == lane, t, 0.0), axis=0, keepdims=True)
        plane1 = left(c, "pl", parts)
        r = r - mid_own(d, c)
        plane2 = left(c, "pl", split(d1 * r))
        for near, far, at in ((lo, lo2, 0), (hi, hi2, 1)):
            near[0:64] = r
            near[64:72] = plane1[8 * at : 8 * at + 8]
            near[72:104] = x[32 * at : 32 * at + 32]
            far[0:8] = plane1[8 * at : 8 * at + 8]
            far[8:16] = plane2[8 * at : 8 * at + 8]

    return call(
        body,
        [(1, 384), (104, 256), (104, 256), (16, 256), (16, 256)],
        held,
        (b, r1, below, above),
    )


def coarse_operator():
    row = lax.broadcasted_iota(jnp.int32, (128, 128), 0)
    lane = lax.broadcasted_iota(jnp.int32, (128, 128), 1)
    z, z2 = row >> 5, lane >> 5
    apart = jnp.abs((row & 31) - (lane & 31))
    w = jnp.where(z == 1, 2.0, jnp.where(z == 3, 0.0, 1.0))
    w = jnp.where(z == z2, w, 0.0)
    next_plane = (jnp.abs(z - z2) == 1) & (z + z2 < 5)
    inner = jnp.where(apart == 0, 3.0 * w - next_plane.astype(f32), 0.0)
    inner = inner - jnp.where(apart == 1, 0.5 * w, 0.0)
    ends = jnp.where(apart == 31, -0.5 * w, 0.0)
    m = jnp.concatenate([inner, ends], axis=1).astype(bf16)
    return jnp.concatenate([m, m], axis=0)


def coarse_solve(g):
    m = coarse_operator()
    plane = lax.broadcasted_iota(jnp.int32, (1, 128), 1) // 32
    wz = jnp.where(plane == 1, 2.0, jnp.where(plane == 3, 0.0, 1.0))

    def after(u):
        return jnp.concatenate([u[8:], u[:8]], axis=0)

    def before(u):
        return jnp.concatenate([u[-8:], u[:-8]], axis=0)

    column = lax.broadcasted_iota(jnp.int32, (32, 8, 128), 2) % 32

    def columns(u):
        t = dot(jnp.concatenate(split(u), axis=1), m)
        ends = t[:, 128:].reshape(32, 8, 128)
        ends = jnp.where(
            column == 31,
            pltpu.roll(ends, 7, 1),
            jnp.where(column == 0, pltpu.roll(ends, 1, 1), 0.0),
        )
        return t[:, :128] + ends.reshape(256, 128)

    half = -0.5 * wz
    mass = 4.0 * mass_coef * wz

    def apply(p):
        p0, p1 = p
        return (
            columns(p0) + half * (p1 + before(p1)) + mass * p0,
            columns(p1) + half * (p0 + after(p0)) + mass * p1,
        )

    def inner_product(a, b):
        s = jnp.sum(a[0] * b[0] + a[1] * b[1], axis=0, keepdims=True)
        return jnp.sum(s, axis=1, keepdims=True)

    r = (g[:, 0:128] + before(g[:, 256:384]), g[:, 128:256])
    p = r
    x = (jnp.zeros_like(r[0]), jnp.zeros_like(r[1]))
    norm = inner_product(r, r)
    for it in range(CG_ITERS):
        q = apply(p)
        alpha = norm / inner_product(p, q)
        x = tuple(a + alpha * b for a, b in zip(x, p))
        if it + 1 < CG_ITERS:
            r = tuple(a - alpha * b for a, b in zip(r, q))
            new = inner_product(r, r)
            beta = new / norm
            p = tuple(a + beta * b for a, b in zip(r, p))
            norm = new
    return jnp.concatenate(x, axis=1)


def second_tables(consts):
    pair(consts, "a", window_operator(MID, 6))
    pair(consts, "c", closed_operator(MID, 6))
    pair(consts, "p", np.concatenate([blocks(face_matrix(MID), 3), face_matrix(MID, 6)], axis=1))
    low, high = inner_lines(MID)
    pair(consts, "po", plane_matrix(4, high, low))
    jc = np.zeros((4, 32, 256))
    for e in range(64):
        element = e if e < 48 else e - 64
        for k in range(2):
            v = element + k
            dev, col = v // 32 + 1, v % 32
            jc[dev, col, 4 * e : 4 * e + 4] = J_MID[:, k]
    pair(consts, "vc", jc.reshape(128, 256))
    jz = np.zeros((8, 3))
    jz[:4, :2] += J_MID
    jz[4:, 1:] += J_MID
    jdr = np.zeros((10, 8, 4, 3, 16))
    for e in range(10):
        for k in range(2):
            jdr[e, :, :, :, e + k] += np.einsum("zp,a->zap", jz, J_MID[:, k])
    order = [2 * (q % 8) + q // 8 for q in range(16)]
    pair(consts, "vd", jdr[..., order].reshape(320, 48))
    pair(consts, "fo", blocks(J_FINE.T, 32))
    fc = np.zeros((128, 128))
    for e in range(16):
        src = e if e < 8 else e + 16
        fc[4 * src : 4 * src + 4, 8 * e : 8 * e + 8] = J_FINE.T
    pair(consts, "fh", fc)
    fd = np.kron(blocks(J_FINE, 2), J_FINE)
    pair(consts, "fd", blocks(fd, 2))
    low, high = inner_lines(FINE)
    pair(consts, "fp", plane_matrix(8, high, low) @ blocks(fd, 2))


def second_smoothing(held, gathered, x0, r0, own_lo, own_hi, below, above, below2, above2):
    def body(c, ins, outs):
        gathered, x0, r0, own_lo, own_hi, below, above, below2, above2 = ins
        s_out, r_out, d_out, low, high, twice = outs
        i, j = lax.axis_index("gx"), lax.axis_index("gy")
        f, m = under(c, "f_"), under(c, "m_")
        x2 = coarse_solve(gathered)
        twice[0:256] = x2
        twice[256:512] = x2
        first = lax.rem(i + 30, 32)
        picked = twice[pl.ds(pl.multiple_of(first * 8, 8), 64), :].reshape(8, 8, 256)
        sub = lax.broadcasted_iota(jnp.int32, (8, 8, 256), 1)
        near = []
        for g in range(3):
            v = jnp.sum(jnp.where(sub == lax.rem(j + 7 + g, 8), picked, 0.0), axis=1)
            near.append(jnp.concatenate([v[:, :128], v[:, 128:]], axis=0))
        block = lax.broadcasted_iota(jnp.int32, (16, 128), 1) // 32
        y = []
        for z in range(3):
            v = [pltpu.roll(near[g], (32 * (g - z)) % 128, 1) if g != z else near[g] for g in range(3)]
            y.append(
                jnp.where(block == 0, v[0], jnp.where(block == 1, v[1], jnp.where(block == 2, v[2], 0.0)))
            )
        y = right(c, "vc", split(jnp.concatenate(y, axis=0)))
        e2 = left(c, "vd", split(y))

        def window(u):
            h, l = split(u)
            t = [left(c, "a", (h[k : k + 192], l[k : k + 192])) for k in range(0, len(u) - 64, 128)]
            return mid_apply(jnp.concatenate(t, axis=0), (h[32:-32], l[32:-32]), m)

        def table(name, count):
            return tiles(m[name], count, 1)

        p3 = {"h": c["ph"][:, :48], "l": c["pl"][:, :48]}
        p6 = {"h": c["ph"][:, 48:], "l": c["pl"][:, 48:]}
        planes = jnp.concatenate(
            [
                below2[:8],
                own_lo[64:72],
                below[64:72],
                above[64:72],
                own_hi[64:72],
                above2[:8],
            ],
            axis=0,
        )
        g = window(e2)
        r = jnp.concatenate([below[:64], own_lo[:64], above[:64]], axis=0)
        r = r - m["wc"][...] * left(p3, "", split(planes)) - g[32:224]
        d = table("d1", 6) * r
        x = jnp.concatenate([below[72:104], own_lo[72:104], own_hi[72:104], above[72:104]], axis=0)
        x = x + e2[96:224] + d[32:160]
        outer = jnp.concatenate([g[:32], g[224:]], axis=0) * table("d1", 2)
        planes = faced(below2, above2, 8, 8) - left(c, "po", split(outer))
        parts = split(d)
        r = r - mid_apply(left(c, "c", parts) + left(p6, "", split(planes)), parts, m)
        d = MID.steps[0][0] * d + table("d2", 6) * r
        x = x + d[32:160]
        r = r[32:160] - window(d)
        d = MID.steps[1][0] * d[32:160] + table("d3", 4) * r
        x = x + d
        h, l = split(x)
        x = jnp.concatenate(
            [
                right(c, "fo", (h[:, :128], l[:, :128])),
                right(c, "fh", (h[:, 128:], l[:, 128:])),
            ],
            axis=1,
        )
        e1 = left(c, "fd", split(x[32:96]))
        planes = left(c, "fp", split(jnp.concatenate([x[:32], x[96:]], axis=0)))
        r = r0[...] - fine_own(split(e1), f, planes)
        d = tiles(f["d1"], 2, 3) * r
        s_out[...] = x0[...] + (e1 + d)[:, :256]
        parts = split(d)
        plane1 = left(f, "pl", parts)
        r = r - fine_own(parts, f)
        d = FINE.steps[0][0] * d + tiles(f["d2"], 2, 3) * r
        plane2 = left(f, "pl", split(d))
        r_out[...] = r
        d_out[...] = d
        for k, plane in enumerate((plane1, plane2)):
            low[16 * k : 16 * k + 16] = plane[:16]
            high[16 * k : 16 * k + 16] = plane[16:]

    return call(
        body,
        [(256, 256), (256, 384), (256, 384), (32, 384), (32, 384)],
        held,
        (gathered, x0, r0, own_lo, own_hi, below, above, below2, above2),
        scratch=[pltpu.VMEM((512, 256), f32)],
    )


def last_step(held, s, r, d, below, above):
    def body(c, ins, outs):
        c = under(c, "f_")
        s, r, d, below, above = ins
        (out,) = outs
        change = tiles(c["wc"], 1, 3) * left(c, "pf", split(faced(below, above, 0, 16)))
        r = r[...] - change
        d = d[...] - tiles(c["d2"], 2, 3) * change
        r = r - fine_own(split(d), c, faced(below, above, 16, 16))
        v = s[...] + d[:, :256]
        d = FINE.steps[1][0] * d + tiles(c["d3"], 2, 3) * r
        v = v + d[:, :256]
        for e in range(2):
            out[:, 8 * e : 8 * e + 8, :] = v[128 * e : 128 * e + 128].reshape(16, 8, 256)

    return call(body, [(16, 16, 256)], held, (s, r, d, below, above))[0]


def fetch(value, axis, offset):
    count = lax.axis_size(axis)
    return lax.ppermute(value, axis, [((i + offset) % count, i) for i in range(count)])


def both(low, high, offset=1):
    return fetch(high, "gx", -offset), fetch(low, "gx", offset)


def tables(*adds, mid=mid_own_constants):
    consts = {"f_" + k: v for k, v in own_constants().items()}
    consts.update({"m_" + k: v for k, v in mid().items()})
    for add in adds:
        add(consts)
    arrays, places = packed(consts)
    return [jnp.asarray(a) for a in arrays], places


def local(source):
    first, second = source[:, :, :128], source[:, :, 128:]
    from_right, from_left = fetch(first, "gy", 1), fetch(second, "gy", -1)
    held = tables(rhs_tables, middle_tables, last_tables, share_tables)
    b, low, high = fine_rhs(held, first, second, from_right, from_left, ready(held))
    x, r, d, low, high = fine_middle(held, b, *both(low, high))
    x0, r0, b, r1, low, high = fine_last(held, x, r, d, *both(low, high))
    chunk, lo, hi, lo2, hi2 = mid_last(held, b, r1, *both(low, high))
    chunk = jnp.broadcast_to(chunk, (lax.axis_size("gx") * lax.axis_size("gy"), 384))
    gathered = lax.all_to_all(chunk, ("gx", "gy"), 0, 0, tiled=True)
    s, r, d, low, high = second_smoothing(
        tables(second_tables, mid=mid_constants), gathered, x0, r0, lo, hi, *both(lo, hi), *both(lo2, hi2, 2)
    )
    return last_step(tables(mid=dict), s, r, d, *both(low, high))


def solution(mesh):
    return jax.shard_map(
        local,
        mesh=mesh,
        in_specs=(P(None, "gx", "gy"),),
        out_specs=P(None, "gx", "gy"),
        check_vma=False,
    )
```

```python
import math

import jax
import jax.numpy as jnp
import ml_dtypes
import numpy as np
from jax import lax
from jax.experimental import pallas as pl
from jax.experimental.pallas import tpu as pltpu
from jax.sharding import PartitionSpec as P

CG_ITERS = 8
mass_coef = 0.000125
cheb_ratio = 0.1
f32 = jnp.float32
bf16 = jnp.bfloat16
MB = 1024 * 1024


def legendre_pair(points, order):
    previous = 0.0 * points + 1.0
    current = points * 1.0
    for degree in range(2, order + 1):
        previous, current = (
            current,
            ((2.0 * degree - 1.0) * points * current - (degree - 1.0) * previous) / degree,
        )
    return (previous, current)


def gll_tables(order):
    count_nodes = order + 1
    points = -np.cos(math.pi * np.arange(count_nodes) / order)
    for sweep in range(60):
        previous, values_at = legendre_pair(points, order)
        points = points - (points * values_at - previous) / (count_nodes * values_at)
    previous, values_at = legendre_pair(points, order)
    weights = 2.0 / (order * (order + 1) * values_at * values_at)
    spacing = points[:, None] - points[None, :]
    safe_spacing = np.where(spacing == 0.0, 1.0, spacing)
    derivative = values_at[:, None] / (values_at[None, :] * safe_spacing)
    derivative = derivative * (1.0 - np.eye(count_nodes))
    corner_value = order * (order + 1) / 4.0
    end_values = np.concatenate(
        [np.array([-corner_value]), np.zeros(count_nodes - 2), np.array([corner_value])]
    )
    return (points, weights, derivative + np.eye(count_nodes) * end_values[None, :])


def interp_table(fine_order, coarse_order):
    fine_points = gll_tables(fine_order)[0]
    coarse_points = gll_tables(coarse_order)[0]
    numer = fine_points[:, None, None] - coarse_points[None, None, :]
    denom = coarse_points[None, :, None] - coarse_points[None, None, :]
    same_node = np.eye(len(coarse_points))[None, :, :] > 0.5
    ratio = np.where(same_node, 1.0, numer / np.where(same_node, 1.0, denom))
    return ratio.prod(axis=2)


def element_bound(order):
    points, weights, derivative = gll_tables(order)
    mass = np.eye(order + 1) * weights[None, :]
    stiff = np.dot(derivative.T, np.dot(mass, derivative))
    full = 0.5 * (
        np.kron(np.kron(mass, mass), stiff)
        + np.kron(np.kron(mass, stiff), mass)
        + np.kron(np.kron(stiff, mass), mass)
    ) + mass_coef * np.kron(np.kron(mass, mass), mass)
    diagonal_entries = np.sum(full * np.eye(full.shape[0]), axis=1)
    ratio = np.abs(full).sum(axis=1) / diagonal_entries
    return float(ratio.max())


def sum_matrix(elements, n, cyclic):
    out = np.eye(elements * n)
    for e in range(elements):
        if cyclic or e + 1 < elements:
            a, b = e * n + n - 1, ((e + 1) % elements) * n
            out[a, b] += 1.0
            out[b, a] += 1.0
    return out


def blocks(matrix, count):
    return np.kron(np.eye(count), matrix)


class Level:
    def __init__(self, order):
        n = self.n = order + 1
        _, w, dm = gll_tables(order)
        self.w = w
        self.k = dm.T @ np.diag(w) @ dm
        self.sum_z = sum_matrix(2, n, False)
        self.k_z = self.sum_z @ blocks(self.k, 2)
        self.w_z = self.sum_z @ np.tile(w, 2)
        self.w_p = w.copy()
        self.w_p[0] += w[-1]
        self.w_p[-1] += w[0]
        kd = np.diag(self.k).copy()
        kd_p = kd.copy()
        kd_p[0] += kd[-1]
        kd_p[-1] += kd[0]
        kd_z = self.sum_z @ np.tile(kd, 2)
        wz, wp = self.w_z, self.w_p
        diag = 0.5 * (
            np.einsum("z,r,c->zrc", wz, kd_p, wp)
            + np.einsum("z,r,c->zrc", wz, wp, kd_p)
            + np.einsum("z,r,c->zrc", kd_z, wp, wp)
        ) + mass_coef * np.einsum("z,r,c->zrc", wz, wp, wp)
        self.dinv = 1.0 / diag
        upper = element_bound(order)
        lower = cheb_ratio * upper
        center, half = 0.5 * (upper + lower), 0.5 * (upper - lower)
        sigma = center / half
        rho = 1.0 / sigma
        self.first = 1.0 / center
        self.steps = []
        for _ in range(2):
            rho2 = 1.0 / (2.0 * sigma - rho)
            self.steps.append((float(rho2 * rho), 2.0 * rho2 / half))
            rho = rho2
        self.m_p = np.ones(n)
        self.m_p[0] = self.m_p[-1] = 0.5
        self.m_z = np.ones(2 * n)
        self.m_z[n - 1] = self.m_z[n] = 0.5


def hi_lo(matrix):
    matrix = np.asarray(matrix, np.float64)
    hi = matrix.astype(ml_dtypes.bfloat16)
    lo = (matrix - hi.astype(np.float64)).astype(ml_dtypes.bfloat16)
    return hi, lo


def packed_left(matrix):
    hi, lo = hi_lo(matrix)
    return np.block([[hi, hi], [lo, np.zeros_like(lo)]])


def packed_right(matrix):
    hi, lo = hi_lo(matrix)
    return np.block([[hi, lo], [hi, np.zeros_like(lo)]])


FINE, MID, COARSE = Level(7), Level(3), Level(1)
J_FINE, J_MID = interp_table(7, 3), interp_table(3, 1)


def pattern(level, lanes):
    d = level.dinv.reshape(2 * level.n * level.n, level.n)
    return np.tile(d, (1, lanes // level.n))


def closed_operator(level, rows):
    n = level.n
    k_r = sum_matrix(rows, n, False) @ blocks(level.k, rows)
    k_r[0, 0] += level.k[-1, -1]
    k_r[-1, -1] += level.k[0, 0]
    return tensor_rows(level, k_r.reshape(rows, n, rows, n), rows)


def tensor_rows(level, k_r, rows):
    n = level.n
    w_r = np.diag(np.tile(level.w_p, rows)).reshape(rows, n, rows, n)
    kz, wz = level.k_z, np.diag(level.w_z)
    t = (
        0.5 * np.einsum("zy,eafb->ezafyb", kz, w_r)
        + 0.5 * np.einsum("zy,eafb->ezafyb", wz, k_r)
        + mass_coef * np.einsum("zy,eafb->ezafyb", wz, w_r)
    )
    return t.reshape(rows * 2 * n * n, rows * 2 * n * n)


def window_operator(level, rows):
    n = level.n
    k_r = sum_matrix(rows, n, False) @ blocks(level.k, rows)
    size = 2 * n * n
    return tensor_rows(level, k_r.reshape(rows, n, rows, n), rows)[size:-size]


def plane_matrix(n, low, high, count=2, weight=None):
    t = np.zeros((2, 2 * n, count, 2 * n, n))
    for z in range(2 * n):
        t[0, z, 0, z] = low * (1.0 if weight is None else weight[z])
        t[1, z, count - 1, z] = high * (1.0 if weight is None else weight[z])
    return t.reshape(4 * n, count * 2 * n * n)


def row_planes(level):
    return plane_matrix(level.n, *inner_lines(level), weight=0.5 * level.w_z)


def beside_planes(level):
    low, high = inner_lines(level)
    return plane_matrix(level.n, high, low, weight=0.5 * level.w_z)


def inner_lines(level):
    low, high = level.k[0].copy(), level.k[-1].copy()
    low[0] = 0.0
    high[-1] = 0.0
    return low, high


def face_matrix(level, count=2):
    n = level.n
    return plane_matrix(n, np.eye(n)[0], np.eye(n)[-1], count).T


def pair(consts, name, matrix):
    consts[name + "h"], consts[name + "l"] = hi_lo(matrix)


def fine_constants():
    dinv = pattern(FINE, 128)
    return dict(
        kc=packed_right(blocks(FINE.k, 16).T),
        wc=np.tile(FINE.w_p, 16)[None, :].astype(np.float32),
        cf=np.repeat(0.5 * np.kron(FINE.w_z, FINE.w_p)[:, None], 128, axis=1).astype(np.float32),
        d1=(FINE.first * dinv).astype(np.float32),
        d2=(FINE.steps[0][1] * dinv).astype(np.float32),
        d3=(FINE.steps[1][1] * dinv).astype(np.float32),
    )


def own_constants():
    c = fine_constants()
    pair(c, "m", closed_operator(FINE, 2))
    pair(c, "pl", row_planes(FINE))
    return c


def mid_constants():
    dinv = pattern(MID, 256)
    c = dict(
        wc=np.tile(MID.w_p, 64)[None, :].astype(np.float32),
        cf=np.repeat(0.5 * np.kron(MID.w_z, MID.w_p)[:, None], 256, axis=1).astype(np.float32),
        d1=(MID.first * dinv).astype(np.float32),
        d2=(MID.steps[0][1] * dinv).astype(np.float32),
        d3=(MID.steps[1][1] * dinv).astype(np.float32),
    )
    pair(c, "k", (sum_matrix(64, 4, True) @ blocks(MID.k, 64)).T)
    return c


def mid_own_constants():
    c = mid_constants()
    pair(c, "m", closed_operator(MID, 2))
    pair(c, "pl", row_planes(MID))
    c["pf"] = face_matrix(MID).astype(ml_dtypes.bfloat16)
    return c


def dot(a, b):
    return jnp.dot(a, b, preferred_element_type=f32)


def split(u):
    h = u.astype(bf16)
    return h, (u - h.astype(f32)).astype(bf16)


def left(c, name, parts):
    h, l = parts
    th, tl = c[name + "h"][...], c[name + "l"][...]
    return dot(th, h) + dot(th, l) + dot(tl, h)


def lefts(tables, parts):
    h, l = parts
    th = jnp.concatenate([c[name + "h"][...] for c, name in tables], axis=0)
    tl = jnp.concatenate([c[name + "l"][...] for c, name in tables], axis=0)
    t = dot(th, h) + dot(th, l) + dot(tl, h)
    out, at = [], 0
    for c, name in tables:
        rows = c[name + "h"].shape[0]
        out.append(t[at : at + rows])
        at += rows
    return out


def on_faces(planes):
    cube = (32, 8, planes.shape[1])
    which = lax.broadcasted_iota(jnp.int32, cube, 0)
    node = lax.broadcasted_iota(jnp.int32, cube, 1)
    outer = ((which < 16) & (node == 0)) | ((which >= 16) & (node == 7))
    return jnp.where(outer, planes.reshape(32, 1, -1), 0.0).reshape(256, -1)


def mid_faces(table, planes):
    h, l = split(planes)
    return dot(table, h) + dot(table, l)


def right(c, name, parts):
    h, l = parts
    th, tl = c[name + "h"][...], c[name + "l"][...]
    return dot(h, th) + dot(l, th) + dot(h, tl)


def tiles(ref, rows, lanes):
    t = ref[...]
    if lanes > 1:
        t = jnp.concatenate([t] * lanes, axis=1)
    if rows > 1:
        t = jnp.concatenate([t] * rows, axis=0)
    return t


def row_sum(before, here, after):
    lanes = here.shape[-1]
    cube = (16, 8, lanes)
    node = lax.broadcasted_iota(jnp.int32, cube, 1)
    out = here.reshape(cube)
    if before is not None:
        out = out + jnp.where(node == 0, pltpu.roll(before.reshape(cube), 1, 1), 0.0)
    if after is not None:
        out = out + jnp.where(node == 7, pltpu.roll(after.reshape(cube), 7, 1), 0.0)
    return out.reshape(128, lanes)


def col_sum(y):
    lanes = y.shape[-1]
    node = lax.broadcasted_iota(jnp.int32, y.shape, 1) % 8
    b = pltpu.roll(y, 1, 1)
    a = pltpu.roll(y, lanes - 1, 1)
    return y + jnp.where(node == 0, b, 0.0) + jnp.where(node == 7, a, 0.0)


def col_stiff(parts, kc):
    h, l = parts
    y = []
    for k in range(h.shape[1] // 128):
        s = slice(128 * k, 128 * k + 128)
        z = dot(jnp.concatenate([h[:, s], l[:, s]], axis=1), kc)
        y.append(z[:, :128] + z[:, 128:])
    return col_sum(jnp.concatenate(y, axis=1))


def fine_own(parts, c, planes=None, more=()):
    lanes = parts[0].shape[1] // 128
    t, *rest = lefts([(c, "m"), *more], parts)
    if planes is not None:
        t = t + on_faces(planes)
    a = tiles(c["wc"], 1, lanes) * t + tiles(c["cf"], 2, lanes) * col_stiff(parts, c["kc"][...])
    return (a, *rest) if more else a


def mid_apply(t, parts, c):
    y = right(c, "k", parts)
    return c["wc"][...] * t + tiles(c["cf"], t.shape[0] // 32, 1) * y


def mid_own(u, c, planes=None):
    parts = split(u)
    t = left(c, "m", parts)
    if planes is not None:
        t = t + mid_faces(c["pf"][...], planes)
    return mid_apply(t, parts, c)


class Table:
    def __init__(self, ref, at, shape, count):
        self.ref, self.at, self.shape, self.count = ref, at, shape, count

    def __getitem__(self, index):
        rows, lanes = self.shape
        step = rows + -rows % 16
        parts = [self.ref[self.at + step * k : self.at + step * k + rows] for k in range(self.count)]
        value = parts[0] if self.count == 1 else jnp.concatenate(parts, axis=1)
        value = value[:, :lanes]
        return value if index is Ellipsis else value[index]


def packed(consts):
    arrays, places = [], {}
    for kind in (np.float32, ml_dtypes.bfloat16):
        pieces, at = [], 0
        for name in sorted(consts):
            t = consts[name]
            if t.dtype != kind:
                continue
            rows, lanes = t.shape
            count = -(-lanes // 128)
            t = np.pad(t, ((0, -rows % 16), (0, count * 128 - lanes)))
            places[name] = (len(arrays), at, (rows, lanes), count)
            pieces += [t[:, 128 * k : 128 * k + 128] for k in range(count)]
            at += count * t.shape[0]
        if pieces:
            arrays.append(np.concatenate(pieces, axis=0))
    return arrays, places


def ready(held):
    def body(c, ins, outs):
        outs[0][...] = jnp.zeros((8, 128), f32)

    return call(body, [(8, 128)], held, ())[0]


def call(body, outs, held, args, scratch=(), vmem=24):
    arrays, places = held
    n, k = len(arrays), len(args)

    def kernel(*refs):
        c = {name: Table(refs[p[0]], *p[1:]) for name, p in places.items()}
        body(c, refs[n : n + k], refs[n + k :])

    spec = pl.BlockSpec(memory_space=pltpu.VMEM)
    return pl.pallas_call(
        kernel,
        out_shape=[jax.ShapeDtypeStruct(s, f32) for s in outs],
        in_specs=[spec] * (n + k),
        out_specs=[spec] * len(outs),
        scratch_shapes=list(scratch),
        compiler_params=pltpu.CompilerParams(vmem_limit_bytes=vmem * MB),
    )(*arrays, *args)


def under(c, prefix):
    return {k[2:]: v for k, v in c.items() if k.startswith(prefix)}


def rhs_tables(consts):
    w = np.kron(np.tile(FINE.w, 2), FINE.w)[:, None] * np.tile(FINE.w, 16)[None, :]
    consts["w"] = (0.125 * w).astype(np.float32)


def fine_rhs(held, first, second, from_right, from_left, at_hand):
    def body(c, ins, outs):
        parts = ins[:4]
        b_out, low, high = outs
        w = tiles(c["w"], 1, 4)
        src = []
        for e in range(2):
            s = slice(8 * e, 8 * e + 8)
            src.append(jnp.concatenate([v[:, s, :].reshape(128, 128) for v in parts], axis=1) * w)
        b = []
        for y in (row_sum(None, src[0], src[1]), row_sum(src[0], src[1], None)):
            y = col_sum(y)
            inner = y[56:64] + y[64:72]
            b.append(jnp.concatenate([y[:56], inner, inner, y[72:]], axis=0))
        face0 = b[0].reshape(16, 8, 512)[:, 0, :]
        face1 = b[1].reshape(16, 8, 512)[:, 7, :]
        b = jnp.concatenate(b, axis=0)
        b_out[...] = b
        planes = left(c, "f_pl", split(tiles(c["f_d1"], 2, 4) * b))
        low[0:16] = face0
        low[16:32] = planes[:16]
        high[0:16] = face1
        high[16:32] = planes[16:]

    return call(
        body,
        [(256, 512), (32, 512), (32, 512)],
        held,
        (first, second, from_right, from_left, at_hand),
    )


def faced(low, high, at, rows):
    return jnp.concatenate([low[at : at + rows], high[at : at + rows]], axis=0)


def rhs_depth():
    return MID.sum_z @ blocks(J_FINE.T, 2) @ np.diag(FINE.m_z)


def middle_tables(consts):
    inside = np.ones(8)
    inside[0] = inside[7] = 0.0
    q = plane_matrix(8, J_FINE[:, 0] * inside, J_FINE[:, 3] * inside)
    q = blocks(rhs_depth(), 2) @ q
    pair(consts, "q", q)
    outer = np.zeros((2, 16, 8))
    outer[0, :, 0] = outer[1, :, 7] = 1.0
    pair(consts, "qm", (q @ closed_operator(FINE, 2)) * (1.0 - outer.reshape(1, 256)))
    pair(consts, "qc", q * np.tile(0.5 * np.kron(FINE.w_z, FINE.w_p), 2)[None, :])


def fine_middle(held, b, below, above):
    def body(c, ins, outs):
        b, below, above = ins
        x_out, r_out, d_out, low, high = outs
        b = b[...] + on_faces(faced(below, above, 0, 16))
        f = under(c, "f_")
        d1, d2, d3 = (tiles(f[k], 2, 4) for k in ("d1", "d2", "d3"))
        d = d1 * b
        x = d
        r = b - fine_own(split(d), f, faced(below, above, 16, 16))
        d = FINE.steps[0][0] * d + d2 * r
        x_out[...] = (x + d)[:, :256]
        a, plane1 = fine_own(split(d), f, more=[(f, "pl")])
        r = r - a
        d = FINE.steps[1][0] * d + d3 * r
        r_out[...] = r
        d_out[...] = d
        parts = split(d)
        plane2, rows, columns = lefts([(f, "pl"), (c, "qm"), (c, "qc")], parts)
        plane3 = left(c, "q", split(r)) - tiles(f["wc"], 1, 4) * rows
        plane3 = plane3 - col_stiff(split(columns), f["kc"][...])
        for k, plane in enumerate((plane1, plane2)):
            low[16 * k : 16 * k + 16] = plane[:16]
            high[16 * k : 16 * k + 16] = plane[16:]
        low[32:40] = plane3[:8]
        high[32:40] = plane3[8:]

    return call(
        body,
        [(256, 256), (256, 512), (256, 512), (40, 512), (40, 512)],
        held,
        (b, below, above),
    )


def last_tables(consts):
    kappa = float(np.sum(J_FINE[1:7, 0] * FINE.k[1:7, 0]))
    t = kappa * plane_matrix(8, np.eye(8)[0], np.eye(8)[7], weight=0.5 * FINE.w_z)
    z = rhs_depth()
    pair(consts, "e", blocks(z, 2) @ t)
    rows = sum_matrix(2, 4, False) @ blocks(J_FINE.T @ np.diag(FINE.m_p), 2)
    rows[0, 0] += 0.5
    rows[-1, -1] += 0.5
    t = np.einsum("zy,eafb->ezafyb", z, rows.reshape(2, 4, 2, 8)).reshape(64, 256)
    pair(consts, "ra", t)
    consts["rp"] = face_matrix(MID).astype(ml_dtypes.bfloat16)
    t = sum_matrix(64, 4, True) @ blocks(J_FINE.T @ np.diag(FINE.m_p), 64)
    pair(consts, "rc", t.T)


def fine_last(held, x, r, d, below, above):
    def body(c, ins, outs):
        x, r, d, below, above = ins
        x0, r0, b_out, r1_out, low, high = outs
        f, m = under(c, "f_"), under(c, "m_")
        wc = tiles(f["wc"], 1, 4)
        change = wc * on_faces(faced(below, above, 0, 16))
        r = r[...] - change
        d = d[...] - tiles(f["d3"], 2, 4) * change
        x0[...] = x[...] + d[:, :256]
        parts = split(d)
        a, inside = fine_own(parts, f, faced(below, above, 16, 16), [(c, "e")])
        r = r - a
        lane = lax.broadcasted_iota(jnp.int32, (256, 128), 1)
        r0[:, :256] = r[:, :256]
        r0[:, 256:] = jnp.where(lane < 64, r[:, 256:384], r[:, 384:])
        beyond = faced(below, above, 32, 8) - wc * inside
        b = left(c, "ra", split(r)) + mid_faces(c["rp"][...], beyond)
        b = right(c, "rc", split(b))
        b_out[...] = b
        d = tiles(m["d1"], 2, 1) * b
        plane1 = left(m, "pl", split(d))
        r = b - mid_own(d, m)
        r1_out[...] = r
        d = MID.steps[0][0] * d + tiles(m["d2"], 2, 1) * r
        plane2 = left(m, "pl", split(d))
        for k, plane in enumerate((plane1, plane2)):
            low[8 * k : 8 * k + 8] = plane[:8]
            high[8 * k : 8 * k + 8] = plane[8:]

    return call(
        body,
        [(256, 256), (256, 384), (64, 256), (64, 256), (16, 256), (16, 256)],
        held,
        (x, r, d, below, above),
    )


def share_tables(consts):
    top = np.zeros((3, 4))
    top[0, 0] = top[1, 1] = top[1, 2] = top[2, 3] = 1.0
    jz = top @ blocks(J_MID.T, 2)

    def down(z_part, r_part):
        t = np.zeros((4, 4, 2, 8, 4))
        for e in range(2):
            for k in range(2):
                t[e + k, :3, e] += np.einsum("zy,b->zyb", jz @ z_part, (J_MID.T @ r_part)[k])
        return t.reshape(16, 64)

    def across(part):
        t = np.zeros((256, 32))
        for v in range(32):
            t[4 * v : 4 * v + 4, v] += (J_MID.T @ part)[0]
            at = (4 * v - 4) % 256
            t[at : at + 4, v] += (J_MID.T @ part)[1]
        return np.tile(t, (1, 4))

    wz, wr = blocks(np.diag(MID.w), 2), np.diag(MID.w)
    kz = blocks(MID.k, 2)
    pair(consts, "sm", down(np.diag(MID.m_z), np.diag(MID.m_p)))
    pair(
        consts,
        "s1",
        0.5 * down(kz, wr) + 0.5 * down(wz, MID.k) + mass_coef * down(wz, wr),
    )
    pair(consts, "s2", 0.5 * down(wz, wr))
    pair(
        consts,
        "sc",
        np.concatenate([across(np.diag(MID.m_p)), -across(wr), -across(MID.k)], axis=0),
    )


def mid_last(held, b, r1, below, above):
    def body(c, ins, outs):
        b, r1, below, above = ins
        chunk, lo, hi, lo2, hi2 = outs
        down, c = c, under(c, "m_")
        d1, d2, d3 = (tiles(c[k], 2, 1) for k in ("d1", "d2", "d3"))
        d = d1 * b[...]
        x = d
        r = r1[...] - c["wc"][...] * mid_faces(c["pf"][...], faced(below, above, 0, 8))
        d = MID.steps[0][0] * d + d2 * r
        x = x + d
        r = r - mid_own(d, c, faced(below, above, 8, 8))
        d = MID.steps[1][0] * d + d3 * r
        x = x + d
        parts = split(d)
        t = jnp.concatenate(
            [left(down, "sm", split(r)), *lefts([(down, "s1"), (down, "s2")], parts)], axis=1
        )
        t = right(down, "sc", split(t))
        t = jnp.concatenate([t, t, t], axis=1)
        q = lax.broadcasted_iota(jnp.int32, t.shape, 0)
        lane = lax.broadcasted_iota(jnp.int32, t.shape, 1) // 32
        chunk[...] = jnp.sum(jnp.where(q == lane, t, 0.0), axis=0, keepdims=True)
        plane1 = left(c, "pl", parts)
        r = r - mid_own(d, c)
        plane2 = left(c, "pl", split(d1 * r))
        for near, far, at in ((lo, lo2, 0), (hi, hi2, 1)):
            near[0:64] = r
            near[64:72] = plane1[8 * at : 8 * at + 8]
            near[72:104] = x[32 * at : 32 * at + 32]
            far[0:8] = plane1[8 * at : 8 * at + 8]
            far[8:16] = plane2[8 * at : 8 * at + 8]

    return call(
        body,
        [(1, 384), (104, 256), (104, 256), (16, 256), (16, 256)],
        held,
        (b, r1, below, above),
    )


def coarse_operator():
    row = lax.broadcasted_iota(jnp.int32, (128, 128), 0)
    lane = lax.broadcasted_iota(jnp.int32, (128, 128), 1)
    z, z2 = row >> 5, lane >> 5
    apart = jnp.abs((row & 31) - (lane & 31))
    w = jnp.where(z == 1, 2.0, jnp.where(z == 3, 0.0, 1.0))
    w = jnp.where(z == z2, w, 0.0)
    next_plane = (jnp.abs(z - z2) == 1) & (z + z2 < 5)
    inner = jnp.where(apart == 0, 3.0 * w - next_plane.astype(f32), 0.0)
    inner = inner - jnp.where(apart == 1, 0.5 * w, 0.0)
    ends = jnp.where(apart == 31, -0.5 * w, 0.0)
    m = jnp.concatenate([inner, ends], axis=1).astype(bf16)
    return jnp.concatenate([m, m], axis=0)


def coarse_solve(g):
    m = coarse_operator()
    plane = lax.broadcasted_iota(jnp.int32, (1, 128), 1) // 32
    wz = jnp.where(plane == 1, 2.0, jnp.where(plane == 3, 0.0, 1.0))

    def after(u):
        return jnp.concatenate([u[8:], u[:8]], axis=0)

    def before(u):
        return jnp.concatenate([u[-8:], u[:-8]], axis=0)

    column = lax.broadcasted_iota(jnp.int32, (32, 8, 128), 2) % 32

    def columns(u):
        t = dot(jnp.concatenate(split(u), axis=1), m)
        ends = t[:, 128:].reshape(32, 8, 128)
        ends = jnp.where(
            column == 31,
            pltpu.roll(ends, 7, 1),
            jnp.where(column == 0, pltpu.roll(ends, 1, 1), 0.0),
        )
        return t[:, :128] + ends.reshape(256, 128)

    half = -0.5 * wz
    mass = 4.0 * mass_coef * wz

    def apply(p):
        p0, p1 = p
        return (
            columns(p0) + half * (p1 + before(p1)) + mass * p0,
            columns(p1) + half * (p0 + after(p0)) + mass * p1,
        )

    def inner_product(a, b):
        s = jnp.sum(a[0] * b[0] + a[1] * b[1], axis=0, keepdims=True)
        return jnp.sum(s, axis=1, keepdims=True)

    r = (g[:, 0:128] + before(g[:, 256:384]), g[:, 128:256])
    p = r
    x = (jnp.zeros_like(r[0]), jnp.zeros_like(r[1]))
    norm = inner_product(r, r)
    for it in range(CG_ITERS):
        q = apply(p)
        alpha = norm / inner_product(p, q)
        x = tuple(a + alpha * b for a, b in zip(x, p))
        if it + 1 < CG_ITERS:
            r = tuple(a - alpha * b for a, b in zip(r, q))
            new = inner_product(r, r)
            beta = new / norm
            p = tuple(a + beta * b for a, b in zip(r, p))
            norm = new
    return jnp.concatenate(x, axis=1)


def second_tables(consts):
    pair(consts, "a", window_operator(MID, 6))
    pair(consts, "c", closed_operator(MID, 6))
    t = np.concatenate([blocks(face_matrix(MID), 3), face_matrix(MID, 6)], axis=1)
    consts["p"] = t.astype(ml_dtypes.bfloat16)
    pair(consts, "po", beside_planes(MID))
    jc = np.zeros((4, 32, 256))
    for e in range(64):
        element = e if e < 48 else e - 64
        for k in range(2):
            v = element + k
            dev, col = v // 32 + 1, v % 32
            jc[dev, col, 4 * e : 4 * e + 4] = J_MID[:, k]
    jc = jc.reshape(128, 256)
    pair(consts, "vc", jc)
    pair(consts, "vk", jc @ (sum_matrix(64, 4, True) @ blocks(MID.k, 64)).T)
    jz = np.zeros((8, 3))
    jz[:4, :2] += J_MID
    jz[4:, 1:] += J_MID
    jdr = np.zeros((10, 8, 4, 3, 16))
    for e in range(10):
        for k in range(2):
            jdr[e, :, :, :, e + k] += np.einsum("zp,a->zap", jz, J_MID[:, k])
    order = [2 * (q % 8) + q // 8 for q in range(16)]
    vd = jdr[..., order].reshape(320, 48)
    pair(consts, "vd", vd)
    pair(consts, "va", window_operator(MID, 10) @ vd)
    pair(consts, "fo", blocks(J_FINE.T, 32))
    fc = np.zeros((128, 128))
    for e in range(16):
        src = e if e < 8 else e + 16
        fc[4 * src : 4 * src + 4, 8 * e : 8 * e + 8] = J_FINE.T
    pair(consts, "fh", fc)
    fd = np.kron(blocks(J_FINE, 2), J_FINE)
    pair(consts, "fd", blocks(fd, 2))
    pair(consts, "fp", beside_planes(FINE) @ blocks(fd, 2))


def second_smoothing(held, gathered, x0, r0, own_lo, own_hi, below, above, below2, above2):
    def body(c, ins, outs):
        gathered, x0, r0, own_lo, own_hi, below, above, below2, above2 = ins
        s_out, r_out, d_out, low, high, twice = outs
        i, j = lax.axis_index("gx"), lax.axis_index("gy")
        f, m = under(c, "f_"), under(c, "m_")
        x2 = coarse_solve(gathered)
        twice[0:256] = x2
        twice[256:512] = x2
        first = lax.rem(i + 30, 32)
        picked = twice[pl.ds(pl.multiple_of(first * 8, 8), 64), :].reshape(8, 8, 256)
        sub = lax.broadcasted_iota(jnp.int32, (8, 8, 256), 1)
        near = []
        for g in range(3):
            v = jnp.sum(jnp.where(sub == lax.rem(j + 7 + g, 8), picked, 0.0), axis=1)
            near.append(jnp.concatenate([v[:, :128], v[:, 128:]], axis=0))
        block = lax.broadcasted_iota(jnp.int32, (16, 128), 1) // 32
        y = []
        for z in range(3):
            v = [pltpu.roll(near[g], (32 * (g - z)) % 128, 1) if g != z else near[g] for g in range(3)]
            y.append(
                jnp.where(block == 0, v[0], jnp.where(block == 1, v[1], jnp.where(block == 2, v[2], 0.0)))
            )
        parts = split(jnp.concatenate(y, axis=0))
        yk = left(c, "vd", split(right(c, "vk", parts)))
        e2, ya = lefts([(c, "vd"), (c, "va")], split(right(c, "vc", parts)))
        g = m["wc"][...] * ya + tiles(m["cf"], 8, 1) * yk[32:-32]

        def table(name, count):
            return tiles(m[name], count, 1)

        planes = jnp.concatenate(
            [
                below2[:8],
                own_lo[64:72],
                below[64:72],
                above[64:72],
                own_hi[64:72],
                above2[:8],
            ],
            axis=0,
        )
        r = jnp.concatenate([below[:64], own_lo[:64], above[:64]], axis=0)
        r = r - m["wc"][...] * mid_faces(c["p"][:, :48], planes) - g[32:224]
        d = table("d1", 6) * r
        x = jnp.concatenate([below[72:104], own_lo[72:104], own_hi[72:104], above[72:104]], axis=0)
        x = x + e2[96:224] + d[32:160]
        outer = jnp.concatenate([g[:32], g[224:]], axis=0) * table("d1", 2)
        planes = faced(below2, above2, 8, 8) - left(c, "po", split(outer))
        parts = split(d)
        r = r - mid_apply(left(c, "c", parts) + mid_faces(c["p"][:, 48:], planes), parts, m)
        d = MID.steps[0][0] * d + table("d2", 6) * r
        x = x + d[32:160]
        h, l = split(d)
        r = r[32:160] - mid_apply(left(c, "a", (h, l)), (h[32:-32], l[32:-32]), m)
        d = MID.steps[1][0] * d[32:160] + table("d3", 4) * r
        x = x + d
        h, l = split(x)
        x = jnp.concatenate(
            [
                right(c, "fo", (h[:, :128], l[:, :128])),
                right(c, "fh", (h[:, 128:], l[:, 128:])),
            ],
            axis=1,
        )
        e1 = left(c, "fd", split(x[32:96]))
        planes = left(c, "fp", split(jnp.concatenate([x[:32], x[96:]], axis=0)))
        r = r0[...] - fine_own(split(e1), f, planes)
        d = tiles(f["d1"], 2, 3) * r
        s_out[...] = x0[...] + (e1 + d)[:, :256]
        a, plane1 = fine_own(split(d), f, more=[(f, "pl")])
        r = r - a
        d = FINE.steps[0][0] * d + tiles(f["d2"], 2, 3) * r
        plane2 = left(f, "pl", split(d))
        r_out[...] = r
        d_out[...] = d
        for k, plane in enumerate((plane1, plane2)):
            low[16 * k : 16 * k + 16] = plane[:16]
            high[16 * k : 16 * k + 16] = plane[16:]

    return call(
        body,
        [(256, 256), (256, 384), (256, 384), (32, 384), (32, 384)],
        held,
        (gathered, x0, r0, own_lo, own_hi, below, above, below2, above2),
        scratch=[pltpu.VMEM((512, 256), f32)],
    )


def last_step(held, s, r, d, below, above):
    def body(c, ins, outs):
        c = under(c, "f_")
        s, r, d, below, above = ins
        (out,) = outs
        change = tiles(c["wc"], 1, 3) * on_faces(faced(below, above, 0, 16))
        r = r[...] - change
        d = d[...] - tiles(c["d2"], 2, 3) * change
        r = r - fine_own(split(d), c, faced(below, above, 16, 16))
        v = s[...] + d[:, :256]
        d = FINE.steps[1][0] * d + tiles(c["d3"], 2, 3) * r
        v = v + d[:, :256]
        for e in range(2):
            out[:, 8 * e : 8 * e + 8, :] = v[128 * e : 128 * e + 128].reshape(16, 8, 256)

    return call(body, [(16, 16, 256)], held, (s, r, d, below, above))[0]


def fetch(value, axis, offset):
    count = lax.axis_size(axis)
    return lax.ppermute(value, axis, [((i + offset) % count, i) for i in range(count)])


def both(low, high, offset=1):
    return fetch(high, "gx", -offset), fetch(low, "gx", offset)


def tables(*adds, mid=mid_own_constants):
    consts = {"f_" + k: v for k, v in own_constants().items()}
    consts.update({"m_" + k: v for k, v in mid().items()})
    for add in adds:
        add(consts)
    arrays, places = packed(consts)
    return [jnp.asarray(a) for a in arrays], places


def local(source):
    first, second = source[:, :, :128], source[:, :, 128:]
    from_right, from_left = fetch(first, "gy", 1), fetch(second, "gy", -1)
    held = tables(rhs_tables, middle_tables, last_tables, share_tables)
    b, low, high = fine_rhs(held, first, second, from_right, from_left, ready(held))
    x, r, d, low, high = fine_middle(held, b, *both(low, high))
    x0, r0, b, r1, low, high = fine_last(held, x, r, d, *both(low, high))
    chunk, lo, hi, lo2, hi2 = mid_last(held, b, r1, *both(low, high))
    chunk = jnp.broadcast_to(chunk, (lax.axis_size("gx") * lax.axis_size("gy"), 384))
    gathered = lax.all_to_all(chunk, ("gx", "gy"), 0, 0, tiled=True)
    s, r, d, low, high = second_smoothing(
        tables(second_tables, mid=mid_constants), gathered, x0, r0, lo, hi, *both(lo, hi), *both(lo2, hi2, 2)
    )
    return last_step(tables(mid=dict), s, r, d, *both(low, high))


def solution(mesh):
    return jax.shard_map(
        local,
        mesh=mesh,
        in_specs=(P(None, "gx", "gy"),),
        out_specs=P(None, "gx", "gy"),
        check_vma=False,
    )
```

```python
import math

import jax
import jax.numpy as jnp
import ml_dtypes
import numpy as np
from jax import lax
from jax.experimental import pallas as pl
from jax.experimental.pallas import tpu as pltpu
from jax.sharding import PartitionSpec as P

CG_ITERS = 8
mass_coef = 0.000125
cheb_ratio = 0.1
f32 = jnp.float32
bf16 = jnp.bfloat16
MB = 1024 * 1024


def legendre_pair(points, order):
    previous = 0.0 * points + 1.0
    current = points * 1.0
    for degree in range(2, order + 1):
        previous, current = (
            current,
            ((2.0 * degree - 1.0) * points * current - (degree - 1.0) * previous) / degree,
        )
    return (previous, current)


def gll_tables(order):
    count_nodes = order + 1
    points = -np.cos(math.pi * np.arange(count_nodes) / order)
    for sweep in range(60):
        previous, values_at = legendre_pair(points, order)
        points = points - (points * values_at - previous) / (count_nodes * values_at)
    previous, values_at = legendre_pair(points, order)
    weights = 2.0 / (order * (order + 1) * values_at * values_at)
    spacing = points[:, None] - points[None, :]
    safe_spacing = np.where(spacing == 0.0, 1.0, spacing)
    derivative = values_at[:, None] / (values_at[None, :] * safe_spacing)
    derivative = derivative * (1.0 - np.eye(count_nodes))
    corner_value = order * (order + 1) / 4.0
    end_values = np.concatenate(
        [np.array([-corner_value]), np.zeros(count_nodes - 2), np.array([corner_value])]
    )
    return (points, weights, derivative + np.eye(count_nodes) * end_values[None, :])


def interp_table(fine_order, coarse_order):
    fine_points = gll_tables(fine_order)[0]
    coarse_points = gll_tables(coarse_order)[0]
    numer = fine_points[:, None, None] - coarse_points[None, None, :]
    denom = coarse_points[None, :, None] - coarse_points[None, None, :]
    same_node = np.eye(len(coarse_points))[None, :, :] > 0.5
    ratio = np.where(same_node, 1.0, numer / np.where(same_node, 1.0, denom))
    return ratio.prod(axis=2)


def element_bound(order):
    points, weights, derivative = gll_tables(order)
    mass = np.eye(order + 1) * weights[None, :]
    stiff = np.dot(derivative.T, np.dot(mass, derivative))
    full = 0.5 * (
        np.kron(np.kron(mass, mass), stiff)
        + np.kron(np.kron(mass, stiff), mass)
        + np.kron(np.kron(stiff, mass), mass)
    ) + mass_coef * np.kron(np.kron(mass, mass), mass)
    diagonal_entries = np.sum(full * np.eye(full.shape[0]), axis=1)
    ratio = np.abs(full).sum(axis=1) / diagonal_entries
    return float(ratio.max())


def sum_matrix(elements, n, cyclic):
    out = np.eye(elements * n)
    for e in range(elements):
        if cyclic or e + 1 < elements:
            a, b = e * n + n - 1, ((e + 1) % elements) * n
            out[a, b] += 1.0
            out[b, a] += 1.0
    return out


def blocks(matrix, count):
    return np.kron(np.eye(count), matrix)


class Level:
    def __init__(self, order):
        n = self.n = order + 1
        _, w, dm = gll_tables(order)
        self.w = w
        self.k = dm.T @ np.diag(w) @ dm
        self.sum_z = sum_matrix(2, n, False)
        self.k_z = self.sum_z @ blocks(self.k, 2)
        self.w_z = self.sum_z @ np.tile(w, 2)
        self.w_p = w.copy()
        self.w_p[0] += w[-1]
        self.w_p[-1] += w[0]
        kd = np.diag(self.k).copy()
        kd_p = kd.copy()
        kd_p[0] += kd[-1]
        kd_p[-1] += kd[0]
        kd_z = self.sum_z @ np.tile(kd, 2)
        wz, wp = self.w_z, self.w_p
        diag = 0.5 * (
            np.einsum("z,r,c->zrc", wz, kd_p, wp)
            + np.einsum("z,r,c->zrc", wz, wp, kd_p)
            + np.einsum("z,r,c->zrc", kd_z, wp, wp)
        ) + mass_coef * np.einsum("z,r,c->zrc", wz, wp, wp)
        self.dinv = 1.0 / diag
        upper = element_bound(order)
        lower = cheb_ratio * upper
        center, half = 0.5 * (upper + lower), 0.5 * (upper - lower)
        sigma = center / half
        rho = 1.0 / sigma
        self.first = 1.0 / center
        self.steps = []
        for _ in range(2):
            rho2 = 1.0 / (2.0 * sigma - rho)
            self.steps.append((float(rho2 * rho), 2.0 * rho2 / half))
            rho = rho2
        self.m_p = np.ones(n)
        self.m_p[0] = self.m_p[-1] = 0.5
        self.m_z = np.ones(2 * n)
        self.m_z[n - 1] = self.m_z[n] = 0.5


def hi_lo(matrix):
    matrix = np.asarray(matrix, np.float64)
    hi = matrix.astype(ml_dtypes.bfloat16)
    lo = (matrix - hi.astype(np.float64)).astype(ml_dtypes.bfloat16)
    return hi, lo


def packed_left(matrix):
    hi, lo = hi_lo(matrix)
    return np.block([[hi, hi], [lo, np.zeros_like(lo)]])


def packed_right(matrix):
    hi, lo = hi_lo(matrix)
    return np.block([[hi, lo], [hi, np.zeros_like(lo)]])


FINE, MID, COARSE = Level(7), Level(3), Level(1)
J_FINE, J_MID = interp_table(7, 3), interp_table(3, 1)


def pattern(level, lanes):
    d = level.dinv.reshape(2 * level.n * level.n, level.n)
    return np.tile(d, (1, lanes // level.n))


def closed_operator(level, rows):
    n = level.n
    k_r = sum_matrix(rows, n, False) @ blocks(level.k, rows)
    k_r[0, 0] += level.k[-1, -1]
    k_r[-1, -1] += level.k[0, 0]
    return tensor_rows(level, k_r.reshape(rows, n, rows, n), rows)


def tensor_rows(level, k_r, rows):
    n = level.n
    w_r = np.diag(np.tile(level.w_p, rows)).reshape(rows, n, rows, n)
    kz, wz = level.k_z, np.diag(level.w_z)
    t = (
        0.5 * np.einsum("zy,eafb->ezafyb", kz, w_r)
        + 0.5 * np.einsum("zy,eafb->ezafyb", wz, k_r)
        + mass_coef * np.einsum("zy,eafb->ezafyb", wz, w_r)
    )
    return t.reshape(rows * 2 * n * n, rows * 2 * n * n)


def window_operator(level, rows):
    n = level.n
    k_r = sum_matrix(rows, n, False) @ blocks(level.k, rows)
    size = 2 * n * n
    return tensor_rows(level, k_r.reshape(rows, n, rows, n), rows)[size:-size]


def plane_matrix(n, low, high, count=2, weight=None):
    t = np.zeros((2, 2 * n, count, 2 * n, n))
    for z in range(2 * n):
        t[0, z, 0, z] = low * (1.0 if weight is None else weight[z])
        t[1, z, count - 1, z] = high * (1.0 if weight is None else weight[z])
    return t.reshape(4 * n, count * 2 * n * n)


def row_planes(level):
    return plane_matrix(level.n, *inner_lines(level), weight=0.5 * level.w_z)


def beside_planes(level):
    low, high = inner_lines(level)
    return plane_matrix(level.n, high, low, weight=0.5 * level.w_z)


def inner_lines(level):
    low, high = level.k[0].copy(), level.k[-1].copy()
    low[0] = 0.0
    high[-1] = 0.0
    return low, high


def face_matrix(level, count=2):
    n = level.n
    return plane_matrix(n, np.eye(n)[0], np.eye(n)[-1], count).T


def pair(consts, name, matrix):
    consts[name + "h"], consts[name + "l"] = hi_lo(matrix)


def fine_constants():
    dinv = pattern(FINE, 128)
    return dict(
        kc=packed_right(blocks(FINE.k, 16).T),
        wc=np.tile(FINE.w_p, 16)[None, :].astype(np.float32),
        cf=np.repeat(0.5 * np.kron(FINE.w_z, FINE.w_p)[:, None], 128, axis=1).astype(np.float32),
        d1=(FINE.first * dinv).astype(np.float32),
    )


def own_constants():
    c = fine_constants()
    pair(c, "m", closed_operator(FINE, 2))
    pair(c, "pl", row_planes(FINE))
    return c


def mid_constants():
    dinv = pattern(MID, 256)
    c = dict(
        wc=np.tile(MID.w_p, 64)[None, :].astype(np.float32),
        cf=np.repeat(0.5 * np.kron(MID.w_z, MID.w_p)[:, None], 256, axis=1).astype(np.float32),
        d1=(MID.first * dinv).astype(np.float32),
    )
    pair(c, "k", (sum_matrix(64, 4, True) @ blocks(MID.k, 64)).T)
    return c


def mid_own_constants():
    c = mid_constants()
    pair(c, "m", closed_operator(MID, 2))
    pair(c, "pl", row_planes(MID))
    c["pf"] = face_matrix(MID).astype(ml_dtypes.bfloat16)
    return c


def dot(a, b):
    return jnp.dot(a, b, preferred_element_type=f32)


def split(u):
    h = u.astype(bf16)
    return h, (u - h.astype(f32)).astype(bf16)


def left(c, name, parts):
    h, l = parts
    th, tl = c[name + "h"][...], c[name + "l"][...]
    return dot(th, h) + dot(th, l) + dot(tl, h)


def lefts(tables, parts):
    h, l = parts
    th = jnp.concatenate([c[name + "h"][...] for c, name in tables], axis=0)
    tl = jnp.concatenate([c[name + "l"][...] for c, name in tables], axis=0)
    t = dot(th, h) + dot(th, l) + dot(tl, h)
    out, at = [], 0
    for c, name in tables:
        rows = c[name + "h"].shape[0]
        out.append(t[at : at + rows])
        at += rows
    return out


def on_faces(planes):
    cube = (32, 8, planes.shape[1])
    which = lax.broadcasted_iota(jnp.int32, cube, 0)
    node = lax.broadcasted_iota(jnp.int32, cube, 1)
    outer = ((which < 16) & (node == 0)) | ((which >= 16) & (node == 7))
    return jnp.where(outer, planes.reshape(32, 1, -1), 0.0).reshape(256, -1)


def mid_faces(table, planes):
    h, l = split(planes)
    return dot(table, h) + dot(table, l)


def right(c, name, parts):
    h, l = parts
    th, tl = c[name + "h"][...], c[name + "l"][...]
    return dot(h, th) + dot(l, th) + dot(h, tl)


def tiles(ref, rows, lanes):
    t = ref[...]
    if lanes > 1:
        t = jnp.concatenate([t] * lanes, axis=1)
    if rows > 1:
        t = jnp.concatenate([t] * rows, axis=0)
    return t


def damping(level, c, step, rows, lanes):
    t = c["d1"][...]
    if step:
        t = t * (level.steps[step - 1][1] / level.first)
    t = jnp.concatenate([t] * lanes, axis=1) if lanes > 1 else t
    return jnp.concatenate([t] * rows, axis=0) if rows > 1 else t


def row_sum(before, here, after):
    lanes = here.shape[-1]
    cube = (16, 8, lanes)
    node = lax.broadcasted_iota(jnp.int32, cube, 1)
    out = here.reshape(cube)
    if before is not None:
        out = out + jnp.where(node == 0, pltpu.roll(before.reshape(cube), 1, 1), 0.0)
    if after is not None:
        out = out + jnp.where(node == 7, pltpu.roll(after.reshape(cube), 7, 1), 0.0)
    return out.reshape(128, lanes)


def col_sum(y):
    lanes = y.shape[-1]
    node = lax.broadcasted_iota(jnp.int32, y.shape, 1) % 8
    b = pltpu.roll(y, 1, 1)
    a = pltpu.roll(y, lanes - 1, 1)
    return y + jnp.where(node == 0, b, 0.0) + jnp.where(node == 7, a, 0.0)


def col_stiff(parts, kc):
    h, l = parts
    y = []
    for k in range(h.shape[1] // 128):
        s = slice(128 * k, 128 * k + 128)
        z = dot(jnp.concatenate([h[:, s], l[:, s]], axis=1), kc)
        y.append(z[:, :128] + z[:, 128:])
    return col_sum(jnp.concatenate(y, axis=1))


def fine_own(parts, c, planes=None, more=()):
    lanes = parts[0].shape[1] // 128
    t, *rest = lefts([(c, "m"), *more], parts)
    if planes is not None:
        t = t + on_faces(planes)
    a = tiles(c["wc"], 1, lanes) * t + tiles(c["cf"], 2, lanes) * col_stiff(parts, c["kc"][...])
    return (a, *rest) if more else a


def mid_apply(t, parts, c):
    y = right(c, "k", parts)
    return c["wc"][...] * t + tiles(c["cf"], t.shape[0] // 32, 1) * y


def mid_own(u, c, planes=None):
    parts = split(u)
    t = left(c, "m", parts)
    if planes is not None:
        t = t + mid_faces(c["pf"][...], planes)
    return mid_apply(t, parts, c)


class Table:
    def __init__(self, ref, at, shape, count):
        self.ref, self.at, self.shape, self.count = ref, at, shape, count

    def __getitem__(self, index):
        rows, lanes = self.shape
        step = rows + -rows % 16
        parts = [self.ref[self.at + step * k : self.at + step * k + rows] for k in range(self.count)]
        value = parts[0] if self.count == 1 else jnp.concatenate(parts, axis=1)
        value = value[:, :lanes]
        return value if index is Ellipsis else value[index]


def packed(consts):
    arrays, places = [], {}
    for kind in (np.float32, ml_dtypes.bfloat16):
        pieces, at = [], 0
        for name in sorted(consts):
            t = consts[name]
            if t.dtype != kind:
                continue
            rows, lanes = t.shape
            count = -(-lanes // 128)
            t = np.pad(t, ((0, -rows % 16), (0, count * 128 - lanes)))
            places[name] = (len(arrays), at, (rows, lanes), count)
            pieces += [t[:, 128 * k : 128 * k + 128] for k in range(count)]
            at += count * t.shape[0]
        if pieces:
            arrays.append(np.concatenate(pieces, axis=0))
    return arrays, places


def ready(held):
    def body(c, ins, outs):
        outs[0][...] = jnp.zeros((8, 128), f32)

    return call(body, [(8, 128)], held, ())[0]


def call(body, outs, held, args, scratch=(), vmem=24):
    arrays, places = held
    n, k = len(arrays), len(args)

    def kernel(*refs):
        c = {name: Table(refs[p[0]], *p[1:]) for name, p in places.items()}
        body(c, refs[n : n + k], refs[n + k :])

    spec = pl.BlockSpec(memory_space=pltpu.VMEM)
    return pl.pallas_call(
        kernel,
        out_shape=[jax.ShapeDtypeStruct(s, f32) for s in outs],
        in_specs=[spec] * (n + k),
        out_specs=[spec] * len(outs),
        scratch_shapes=list(scratch),
        compiler_params=pltpu.CompilerParams(vmem_limit_bytes=vmem * MB),
    )(*arrays, *args)


def under(c, prefix):
    return {k[2:]: v for k, v in c.items() if k.startswith(prefix)}


def rhs_tables(consts):
    w = np.kron(np.tile(FINE.w, 2), FINE.w)[:, None] * np.tile(FINE.w, 16)[None, :]
    consts["w"] = (0.125 * w).astype(np.float32)


def fine_rhs(held, first, second, from_right, from_left, at_hand):
    def body(c, ins, outs):
        parts = ins[:4]
        b_out, low, high = outs
        w = tiles(c["w"], 1, 4)
        src = []
        for e in range(2):
            s = slice(8 * e, 8 * e + 8)
            src.append(jnp.concatenate([v[:, s, :].reshape(128, 128) for v in parts], axis=1) * w)
        b = []
        for y in (row_sum(None, src[0], src[1]), row_sum(src[0], src[1], None)):
            y = col_sum(y)
            inner = y[56:64] + y[64:72]
            b.append(jnp.concatenate([y[:56], inner, inner, y[72:]], axis=0))
        face0 = b[0].reshape(16, 8, 512)[:, 0, :]
        face1 = b[1].reshape(16, 8, 512)[:, 7, :]
        b = jnp.concatenate(b, axis=0)
        b_out[...] = b
        planes = left(c, "f_pl", split(tiles(c["f_d1"], 2, 4) * b))
        low[0:16] = face0
        low[16:32] = planes[:16]
        high[0:16] = face1
        high[16:32] = planes[16:]

    return call(
        body,
        [(256, 512), (32, 512), (32, 512)],
        held,
        (first, second, from_right, from_left, at_hand),
    )


def faced(low, high, at, rows):
    return jnp.concatenate([low[at : at + rows], high[at : at + rows]], axis=0)


def rhs_depth():
    return MID.sum_z @ blocks(J_FINE.T, 2) @ np.diag(FINE.m_z)


def middle_tables(consts):
    inside = np.ones(8)
    inside[0] = inside[7] = 0.0
    q = plane_matrix(8, J_FINE[:, 0] * inside, J_FINE[:, 3] * inside)
    q = blocks(rhs_depth(), 2) @ q
    pair(consts, "q", q)
    outer = np.zeros((2, 16, 8))
    outer[0, :, 0] = outer[1, :, 7] = 1.0
    pair(consts, "qm", (q @ closed_operator(FINE, 2)) * (1.0 - outer.reshape(1, 256)))
    pair(consts, "qc", q * np.tile(0.5 * np.kron(FINE.w_z, FINE.w_p), 2)[None, :])


def fine_middle(held, b, below, above):
    def body(c, ins, outs):
        b, below, above = ins
        x_out, r_out, d_out, low, high = outs
        b = b[...] + on_faces(faced(below, above, 0, 16))
        f = under(c, "f_")
        d1, d2, d3 = (damping(FINE, f, k, 2, 4) for k in range(3))
        d = d1 * b
        x = d
        r = b - fine_own(split(d), f, faced(below, above, 16, 16))
        d = FINE.steps[0][0] * d + d2 * r
        x_out[...] = (x + d)[:, :256]
        a, plane1 = fine_own(split(d), f, more=[(f, "pl")])
        r = r - a
        d = FINE.steps[1][0] * d + d3 * r
        r_out[...] = r
        d_out[...] = d
        parts = split(d)
        plane2, rows, columns = lefts([(f, "pl"), (c, "qm"), (c, "qc")], parts)
        plane3 = left(c, "q", split(r)) - tiles(f["wc"], 1, 4) * rows
        plane3 = plane3 - col_stiff(split(columns), f["kc"][...])
        for k, plane in enumerate((plane1, plane2)):
            low[16 * k : 16 * k + 16] = plane[:16]
            high[16 * k : 16 * k + 16] = plane[16:]
        low[32:40] = plane3[:8]
        high[32:40] = plane3[8:]

    return call(
        body,
        [(256, 256), (256, 512), (256, 512), (40, 512), (40, 512)],
        held,
        (b, below, above),
    )


def last_tables(consts):
    kappa = float(np.sum(J_FINE[1:7, 0] * FINE.k[1:7, 0]))
    t = kappa * plane_matrix(8, np.eye(8)[0], np.eye(8)[7], weight=0.5 * FINE.w_z)
    z = rhs_depth()
    pair(consts, "e", blocks(z, 2) @ t)
    rows = sum_matrix(2, 4, False) @ blocks(J_FINE.T @ np.diag(FINE.m_p), 2)
    rows[0, 0] += 0.5
    rows[-1, -1] += 0.5
    t = np.einsum("zy,eafb->ezafyb", z, rows.reshape(2, 4, 2, 8)).reshape(64, 256)
    pair(consts, "ra", t)
    consts["rp"] = face_matrix(MID).astype(ml_dtypes.bfloat16)
    t = sum_matrix(64, 4, True) @ blocks(J_FINE.T @ np.diag(FINE.m_p), 64)
    pair(consts, "rc", t.T)


def fine_last(held, x, r, d, below, above):
    def body(c, ins, outs):
        x, r, d, below, above = ins
        x0, r0, b_out, r1_out, low, high = outs
        f, m = under(c, "f_"), under(c, "m_")
        wc = tiles(f["wc"], 1, 4)
        change = wc * on_faces(faced(below, above, 0, 16))
        r = r[...] - change
        d = d[...] - damping(FINE, f, 2, 2, 4) * change
        x0[...] = x[...] + d[:, :256]
        parts = split(d)
        a, inside = fine_own(parts, f, faced(below, above, 16, 16), [(c, "e")])
        r = r - a
        lane = lax.broadcasted_iota(jnp.int32, (256, 128), 1)
        r0[:, :256] = r[:, :256]
        r0[:, 256:] = jnp.where(lane < 64, r[:, 256:384], r[:, 384:])
        beyond = faced(below, above, 32, 8) - wc * inside
        b = left(c, "ra", split(r)) + mid_faces(c["rp"][...], beyond)
        b = right(c, "rc", split(b))
        b_out[...] = b
        d = tiles(m["d1"], 2, 1) * b
        plane1 = left(m, "pl", split(d))
        r = b - mid_own(d, m)
        r1_out[...] = r
        d = MID.steps[0][0] * d + damping(MID, m, 1, 2, 1) * r
        plane2 = left(m, "pl", split(d))
        for k, plane in enumerate((plane1, plane2)):
            low[8 * k : 8 * k + 8] = plane[:8]
            high[8 * k : 8 * k + 8] = plane[8:]

    return call(
        body,
        [(256, 256), (256, 384), (64, 256), (64, 256), (16, 256), (16, 256)],
        held,
        (x, r, d, below, above),
    )


def share_tables(consts):
    top = np.zeros((3, 4))
    top[0, 0] = top[1, 1] = top[1, 2] = top[2, 3] = 1.0
    jz = top @ blocks(J_MID.T, 2)

    def down(z_part, r_part):
        t = np.zeros((4, 4, 2, 8, 4))
        for e in range(2):
            for k in range(2):
                t[e + k, :3, e] += np.einsum("zy,b->zyb", jz @ z_part, (J_MID.T @ r_part)[k])
        return t.reshape(16, 64)

    def across(part):
        t = np.zeros((256, 32))
        for v in range(32):
            t[4 * v : 4 * v + 4, v] += (J_MID.T @ part)[0]
            at = (4 * v - 4) % 256
            t[at : at + 4, v] += (J_MID.T @ part)[1]
        return np.tile(t, (1, 4))

    wz, wr = blocks(np.diag(MID.w), 2), np.diag(MID.w)
    kz = blocks(MID.k, 2)
    pair(consts, "sm", down(np.diag(MID.m_z), np.diag(MID.m_p)))
    pair(
        consts,
        "s1",
        0.5 * down(kz, wr) + 0.5 * down(wz, MID.k) + mass_coef * down(wz, wr),
    )
    pair(consts, "s2", 0.5 * down(wz, wr))
    pair(
        consts,
        "sc",
        np.concatenate([across(np.diag(MID.m_p)), -across(wr), -across(MID.k)], axis=0),
    )


def mid_last(held, b, r1, below, above):
    def body(c, ins, outs):
        b, r1, below, above = ins
        chunk, lo, hi, lo2, hi2 = outs
        down, c = c, under(c, "m_")
        d1, d2, d3 = (damping(MID, c, k, 2, 1) for k in range(3))
        d = d1 * b[...]
        x = d
        r = r1[...] - c["wc"][...] * mid_faces(c["pf"][...], faced(below, above, 0, 8))
        d = MID.steps[0][0] * d + d2 * r
        x = x + d
        r = r - mid_own(d, c, faced(below, above, 8, 8))
        d = MID.steps[1][0] * d + d3 * r
        x = x + d
        parts = split(d)
        t = jnp.concatenate(
            [left(down, "sm", split(r)), *lefts([(down, "s1"), (down, "s2")], parts)], axis=1
        )
        t = right(down, "sc", split(t))
        t = jnp.concatenate([t, t, t], axis=1)
        q = lax.broadcasted_iota(jnp.int32, t.shape, 0)
        lane = lax.broadcasted_iota(jnp.int32, t.shape, 1) // 32
        t = jnp.sum(jnp.where(q == lane, t, 0.0), axis=0, keepdims=True)
        which = lax.broadcasted_iota(jnp.int32, chunk.shape, 0) % 3
        chunk[...] = jnp.where(
            which == 0, t[:, :128], jnp.where(which == 1, t[:, 128:256], t[:, 256:])
        )
        plane1 = left(c, "pl", parts)
        r = r - mid_own(d, c)
        plane2 = left(c, "pl", split(d1 * r))
        for near, far, at in ((lo, lo2, 0), (hi, hi2, 1)):
            near[0:64] = r
            near[64:72] = plane1[8 * at : 8 * at + 8]
            near[72:104] = x[32 * at : 32 * at + 32]
            far[0:8] = plane1[8 * at : 8 * at + 8]
            far[8:16] = plane2[8 * at : 8 * at + 8]

    return call(
        body,
        [(768, 128), (104, 256), (104, 256), (16, 256), (16, 256)],
        held,
        (b, r1, below, above),
    )


def coarse_operator():
    row = lax.broadcasted_iota(jnp.int32, (128, 128), 0)
    lane = lax.broadcasted_iota(jnp.int32, (128, 128), 1)
    z, z2 = row >> 5, lane >> 5
    apart = jnp.abs((row & 31) - (lane & 31))
    w = jnp.where(z == 1, 2.0, jnp.where(z == 3, 0.0, 1.0))
    w = jnp.where(z == z2, w, 0.0)
    next_plane = (jnp.abs(z - z2) == 1) & (z + z2 < 5)
    inner = jnp.where(apart == 0, 3.0 * w - next_plane.astype(f32), 0.0)
    inner = inner - jnp.where(apart == 1, 0.5 * w, 0.0)
    ends = jnp.where(apart == 31, -0.5 * w, 0.0)
    m = jnp.concatenate([inner, ends], axis=1).astype(bf16)
    return jnp.concatenate([m, m], axis=0)


def coarse_solve(g):
    m = coarse_operator()
    plane = lax.broadcasted_iota(jnp.int32, (1, 128), 1) // 32
    wz = jnp.where(plane == 1, 2.0, jnp.where(plane == 3, 0.0, 1.0))

    def after(u):
        return jnp.concatenate([u[8:], u[:8]], axis=0)

    def before(u):
        return jnp.concatenate([u[-8:], u[:-8]], axis=0)

    column = lax.broadcasted_iota(jnp.int32, (32, 8, 128), 2) % 32

    def columns(u):
        h = u.astype(bf16)
        rest = u - h.astype(f32)
        k, l = split(rest)
        t = dot(jnp.concatenate([h, k], axis=1), m) + dot(l, m[:128])
        ends = t[:, 128:].reshape(32, 8, 128)
        ends = jnp.where(
            column == 31,
            pltpu.roll(ends, 7, 1),
            jnp.where(column == 0, pltpu.roll(ends, 1, 1), 0.0),
        )
        return t[:, :128] + ends.reshape(256, 128)

    half = -0.5 * wz
    mass = 4.0 * mass_coef * wz

    def apply(p):
        p0, p1 = p
        return (
            columns(p0) + half * (p1 + before(p1)) + mass * p0,
            columns(p1) + half * (p0 + after(p0)) + mass * p1,
        )

    def inner_product(a, b):
        s = jnp.sum(a[0] * b[0] + a[1] * b[1], axis=0, keepdims=True)
        return jnp.sum(s, axis=1, keepdims=True)

    r = (g[:, 0:128] + before(g[:, 256:384]), g[:, 128:256])
    p = r
    x = (jnp.zeros_like(r[0]), jnp.zeros_like(r[1]))
    norm = inner_product(r, r)
    for it in range(CG_ITERS):
        q = apply(p)
        alpha = norm / inner_product(p, q)
        x = tuple(a + alpha * b for a, b in zip(x, p))
        if it + 1 < CG_ITERS:
            r = tuple(a - alpha * b for a, b in zip(r, q))
            new = inner_product(r, r)
            beta = new / norm
            p = tuple(a + beta * b for a, b in zip(r, p))
            norm = new
    return jnp.concatenate(x, axis=1)


def second_tables(consts):
    pair(consts, "c", closed_operator(MID, 6))
    t = np.concatenate([blocks(face_matrix(MID), 3), face_matrix(MID, 6)], axis=1)
    consts["p"] = t.astype(ml_dtypes.bfloat16)
    pair(consts, "po", beside_planes(MID))
    jc = np.zeros((4, 32, 256))
    for e in range(64):
        element = e if e < 48 else e - 64
        for k in range(2):
            v = element + k
            dev, col = v // 32 + 1, v % 32
            jc[dev, col, 4 * e : 4 * e + 4] = J_MID[:, k]
    jc = jc.reshape(128, 256)
    pair(consts, "vc", jc)
    pair(consts, "vk", jc @ (sum_matrix(64, 4, True) @ blocks(MID.k, 64)).T)
    jz = np.zeros((8, 3))
    jz[:4, :2] += J_MID
    jz[4:, 1:] += J_MID
    jdr = np.zeros((10, 8, 4, 3, 16))
    for e in range(10):
        for k in range(2):
            jdr[e, :, :, :, e + k] += np.einsum("zp,a->zap", jz, J_MID[:, k])
    order = [2 * (q % 8) + q // 8 for q in range(16)]
    vd = jdr[..., order].reshape(320, 48)
    pair(consts, "vd", vd)
    pair(consts, "va", window_operator(MID, 10) @ vd)
    pair(consts, "fo", blocks(J_FINE.T, 32))
    fc = np.zeros((128, 128))
    for e in range(16):
        src = e if e < 8 else e + 16
        fc[4 * src : 4 * src + 4, 8 * e : 8 * e + 8] = J_FINE.T
    pair(consts, "fh", fc)
    fd = np.kron(blocks(J_FINE, 2), J_FINE)
    pair(consts, "fd", blocks(fd, 2))
    pair(consts, "fp", beside_planes(FINE) @ blocks(fd, 2))


def second_smoothing(held, gathered, x0, r0, own_lo, own_hi, below, above, below2, above2):
    def body(c, ins, outs):
        gathered, x0, r0, own_lo, own_hi, below, above, below2, above2 = ins
        s_out, r_out, d_out, low, high, twice = outs
        i, j = lax.axis_index("gx"), lax.axis_index("gy")
        f, m = under(c, "f_"), under(c, "m_")
        x2 = coarse_solve(gathered)
        twice[0:256] = x2
        twice[256:512] = x2
        first = lax.rem(i + 30, 32)
        picked = twice[pl.ds(pl.multiple_of(first * 8, 8), 64), :].reshape(8, 8, 256)
        sub = lax.broadcasted_iota(jnp.int32, (8, 8, 256), 1)
        near = []
        for g in range(3):
            v = jnp.sum(jnp.where(sub == lax.rem(j + 7 + g, 8), picked, 0.0), axis=1)
            near.append(jnp.concatenate([v[:, :128], v[:, 128:]], axis=0))
        block = lax.broadcasted_iota(jnp.int32, (16, 128), 1) // 32
        y = []
        for z in range(3):
            v = [pltpu.roll(near[g], (32 * (g - z)) % 128, 1) if g != z else near[g] for g in range(3)]
            y.append(
                jnp.where(block == 0, v[0], jnp.where(block == 1, v[1], jnp.where(block == 2, v[2], 0.0)))
            )
        parts = split(jnp.concatenate(y, axis=0))
        yk = left(c, "vd", split(right(c, "vk", parts)))
        e2, ya = lefts([(c, "vd"), (c, "va")], split(right(c, "vc", parts)))
        g = m["wc"][...] * ya + tiles(m["cf"], 8, 1) * yk[32:-32]

        def table(step, count):
            return damping(MID, m, step, count, 1)

        planes = jnp.concatenate(
            [
                below2[:8],
                own_lo[64:72],
                below[64:72],
                above[64:72],
                own_hi[64:72],
                above2[:8],
            ],
            axis=0,
        )
        r = jnp.concatenate([below[:64], own_lo[:64], above[:64]], axis=0)
        r = r - m["wc"][...] * mid_faces(c["p"][:, :48], planes) - g[32:224]
        d = table(0, 6) * r
        x = jnp.concatenate([below[72:104], own_lo[72:104], own_hi[72:104], above[72:104]], axis=0)
        x = x + e2[96:224] + d[32:160]
        outer = jnp.concatenate([g[:32], g[224:]], axis=0) * table(0, 2)
        planes = faced(below2, above2, 8, 8) - left(c, "po", split(outer))
        parts = split(d)
        r = r - mid_apply(left(c, "c", parts) + mid_faces(c["p"][:, 48:], planes), parts, m)
        d = MID.steps[0][0] * d + table(1, 6) * r
        x = x + d[32:160]
        h, l = split(d)
        inner = {"h": c["ch"][32:160], "l": c["cl"][32:160]}
        r = r[32:160] - mid_apply(left(inner, "", (h, l)), (h[32:-32], l[32:-32]), m)
        d = MID.steps[1][0] * d[32:160] + table(2, 4) * r
        x = x + d
        h, l = split(x)
        x = jnp.concatenate(
            [
                right(c, "fo", (h[:, :128], l[:, :128])),
                right(c, "fh", (h[:, 128:], l[:, 128:])),
            ],
            axis=1,
        )
        e1 = left(c, "fd", split(x[32:96]))
        planes = left(c, "fp", split(jnp.concatenate([x[:32], x[96:]], axis=0)))
        r = r0[...] - fine_own(split(e1), f, planes)
        d = tiles(f["d1"], 2, 3) * r
        s_out[...] = x0[...] + (e1 + d)[:, :256]
        a, plane1 = fine_own(split(d), f, more=[(f, "pl")])
        r = r - a
        d = FINE.steps[0][0] * d + damping(FINE, f, 1, 2, 3) * r
        plane2 = left(f, "pl", split(d))
        r_out[...] = r
        d_out[...] = d
        for k, plane in enumerate((plane1, plane2)):
            low[16 * k : 16 * k + 16] = plane[:16]
            high[16 * k : 16 * k + 16] = plane[16:]

    return call(
        body,
        [(256, 256), (256, 384), (256, 384), (32, 384), (32, 384)],
        held,
        (gathered, x0, r0, own_lo, own_hi, below, above, below2, above2),
        scratch=[pltpu.VMEM((512, 256), f32)],
    )


def last_step(held, s, r, d, below, above):
    def body(c, ins, outs):
        c = under(c, "f_")
        s, r, d, below, above = ins
        (out,) = outs
        change = tiles(c["wc"], 1, 3) * on_faces(faced(below, above, 0, 16))
        r = r[...] - change
        d = d[...] - damping(FINE, c, 1, 2, 3) * change
        r = r - fine_own(split(d), c, faced(below, above, 16, 16))
        v = s[...] + d[:, :256]
        d = FINE.steps[1][0] * d + damping(FINE, c, 2, 2, 3) * r
        v = v + d[:, :256]
        for e in range(2):
            out[:, 8 * e : 8 * e + 8, :] = v[128 * e : 128 * e + 128].reshape(16, 8, 256)

    return call(body, [(16, 16, 256)], held, (s, r, d, below, above))[0]


def fetch(value, axis, offset):
    count = lax.axis_size(axis)
    return lax.ppermute(value, axis, [((i + offset) % count, i) for i in range(count)])


def both(low, high, offset=1):
    return fetch(high, "gx", -offset), fetch(low, "gx", offset)


def tables(*adds, mid=mid_own_constants):
    consts = {"f_" + k: v for k, v in own_constants().items()}
    consts.update({"m_" + k: v for k, v in mid().items()})
    for add in adds:
        add(consts)
    arrays, places = packed(consts)
    return [jnp.asarray(a) for a in arrays], places


def local(source):
    first, second = source[:, :, :128], source[:, :, 128:]
    from_right, from_left = fetch(first, "gy", 1), fetch(second, "gy", -1)
    held = tables(rhs_tables, middle_tables, last_tables, share_tables)
    b, low, high = fine_rhs(held, first, second, from_right, from_left, ready(held))
    x, r, d, low, high = fine_middle(held, b, *both(low, high))
    x0, r0, b, r1, low, high = fine_last(held, x, r, d, *both(low, high))
    chunk, lo, hi, lo2, hi2 = mid_last(held, b, r1, *both(low, high))
    gathered = lax.all_to_all(chunk.reshape(256, 384), ("gx", "gy"), 0, 0, tiled=True)
    s, r, d, low, high = second_smoothing(
        tables(second_tables, mid=mid_constants), gathered, x0, r0, lo, hi, *both(lo, hi), *both(lo2, hi2, 2)
    )
    return last_step(tables(mid=dict), s, r, d, *both(low, high))


def solution(mesh):
    return jax.shard_map(
        local,
        mesh=mesh,
        in_specs=(P(None, "gx", "gy"),),
        out_specs=P(None, "gx", "gy"),
        check_vma=False,
    )
```

```python
import math

import jax
import jax.numpy as jnp
import ml_dtypes
import numpy as np
from jax import lax
from jax.experimental import pallas as pl
from jax.experimental.pallas import tpu as pltpu
from jax.sharding import PartitionSpec as P

CG_ITERS = 8
mass_coef = 0.000125
cheb_ratio = 0.1
f32 = jnp.float32
bf16 = jnp.bfloat16
MB = 1024 * 1024


def legendre_pair(points, order):
    previous = 0.0 * points + 1.0
    current = points * 1.0
    for degree in range(2, order + 1):
        previous, current = (
            current,
            ((2.0 * degree - 1.0) * points * current - (degree - 1.0) * previous) / degree,
        )
    return (previous, current)


def gll_tables(order):
    count_nodes = order + 1
    points = -np.cos(math.pi * np.arange(count_nodes) / order)
    for sweep in range(60):
        previous, values_at = legendre_pair(points, order)
        points = points - (points * values_at - previous) / (count_nodes * values_at)
    previous, values_at = legendre_pair(points, order)
    weights = 2.0 / (order * (order + 1) * values_at * values_at)
    spacing = points[:, None] - points[None, :]
    safe_spacing = np.where(spacing == 0.0, 1.0, spacing)
    derivative = values_at[:, None] / (values_at[None, :] * safe_spacing)
    derivative = derivative * (1.0 - np.eye(count_nodes))
    corner_value = order * (order + 1) / 4.0
    end_values = np.concatenate(
        [np.array([-corner_value]), np.zeros(count_nodes - 2), np.array([corner_value])]
    )
    return (points, weights, derivative + np.eye(count_nodes) * end_values[None, :])


def interp_table(fine_order, coarse_order):
    fine_points = gll_tables(fine_order)[0]
    coarse_points = gll_tables(coarse_order)[0]
    numer = fine_points[:, None, None] - coarse_points[None, None, :]
    denom = coarse_points[None, :, None] - coarse_points[None, None, :]
    same_node = np.eye(len(coarse_points))[None, :, :] > 0.5
    ratio = np.where(same_node, 1.0, numer / np.where(same_node, 1.0, denom))
    return ratio.prod(axis=2)


def element_bound(order):
    points, weights, derivative = gll_tables(order)
    mass = np.eye(order + 1) * weights[None, :]
    stiff = np.dot(derivative.T, np.dot(mass, derivative))
    full = 0.5 * (
        np.kron(np.kron(mass, mass), stiff)
        + np.kron(np.kron(mass, stiff), mass)
        + np.kron(np.kron(stiff, mass), mass)
    ) + mass_coef * np.kron(np.kron(mass, mass), mass)
    diagonal_entries = np.sum(full * np.eye(full.shape[0]), axis=1)
    ratio = np.abs(full).sum(axis=1) / diagonal_entries
    return float(ratio.max())


def sum_matrix(elements, n, cyclic):
    out = np.eye(elements * n)
    for e in range(elements):
        if cyclic or e + 1 < elements:
            a, b = e * n + n - 1, ((e + 1) % elements) * n
            out[a, b] += 1.0
            out[b, a] += 1.0
    return out


def blocks(matrix, count):
    return np.kron(np.eye(count), matrix)


class Level:
    def __init__(self, order):
        n = self.n = order + 1
        _, w, dm = gll_tables(order)
        self.w = w
        self.k = dm.T @ np.diag(w) @ dm
        self.sum_z = sum_matrix(2, n, False)
        self.k_z = self.sum_z @ blocks(self.k, 2)
        self.w_z = self.sum_z @ np.tile(w, 2)
        self.w_p = w.copy()
        self.w_p[0] += w[-1]
        self.w_p[-1] += w[0]
        kd = np.diag(self.k).copy()
        kd_p = kd.copy()
        kd_p[0] += kd[-1]
        kd_p[-1] += kd[0]
        kd_z = self.sum_z @ np.tile(kd, 2)
        wz, wp = self.w_z, self.w_p
        diag = 0.5 * (
            np.einsum("z,r,c->zrc", wz, kd_p, wp)
            + np.einsum("z,r,c->zrc", wz, wp, kd_p)
            + np.einsum("z,r,c->zrc", kd_z, wp, wp)
        ) + mass_coef * np.einsum("z,r,c->zrc", wz, wp, wp)
        self.dinv = 1.0 / diag
        upper = element_bound(order)
        lower = cheb_ratio * upper
        center, half = 0.5 * (upper + lower), 0.5 * (upper - lower)
        sigma = center / half
        rho = 1.0 / sigma
        self.first = 1.0 / center
        self.steps = []
        for _ in range(2):
            rho2 = 1.0 / (2.0 * sigma - rho)
            self.steps.append((float(rho2 * rho), 2.0 * rho2 / half))
            rho = rho2
        self.m_p = np.ones(n)
        self.m_p[0] = self.m_p[-1] = 0.5
        self.m_z = np.ones(2 * n)
        self.m_z[n - 1] = self.m_z[n] = 0.5


def hi_lo(matrix):
    matrix = np.asarray(matrix, np.float64)
    hi = matrix.astype(ml_dtypes.bfloat16)
    lo = (matrix - hi.astype(np.float64)).astype(ml_dtypes.bfloat16)
    return hi, lo


def packed_left(matrix):
    hi, lo = hi_lo(matrix)
    return np.block([[hi, hi], [lo, np.zeros_like(lo)]])


def packed_right(matrix):
    hi, lo = hi_lo(matrix)
    return np.block([[hi, lo], [hi, np.zeros_like(lo)]])


FINE, MID, COARSE = Level(7), Level(3), Level(1)
J_FINE, J_MID = interp_table(7, 3), interp_table(3, 1)


def pattern(level, lanes):
    d = level.dinv.reshape(2 * level.n * level.n, level.n)
    return np.tile(d, (1, lanes // level.n))


def closed_operator(level, rows):
    n = level.n
    k_r = sum_matrix(rows, n, False) @ blocks(level.k, rows)
    k_r[0, 0] += level.k[-1, -1]
    k_r[-1, -1] += level.k[0, 0]
    return tensor_rows(level, k_r.reshape(rows, n, rows, n), rows)


def tensor_rows(level, k_r, rows):
    n = level.n
    w_r = np.diag(np.tile(level.w_p, rows)).reshape(rows, n, rows, n)
    kz, wz = level.k_z, np.diag(level.w_z)
    t = (
        0.5 * np.einsum("zy,eafb->ezafyb", kz, w_r)
        + 0.5 * np.einsum("zy,eafb->ezafyb", wz, k_r)
        + mass_coef * np.einsum("zy,eafb->ezafyb", wz, w_r)
    )
    return t.reshape(rows * 2 * n * n, rows * 2 * n * n)


def window_operator(level, rows):
    n = level.n
    k_r = sum_matrix(rows, n, False) @ blocks(level.k, rows)
    size = 2 * n * n
    return tensor_rows(level, k_r.reshape(rows, n, rows, n), rows)[size:-size]


def plane_matrix(n, low, high, count=2, weight=None):
    t = np.zeros((2, 2 * n, count, 2 * n, n))
    for z in range(2 * n):
        t[0, z, 0, z] = low * (1.0 if weight is None else weight[z])
        t[1, z, count - 1, z] = high * (1.0 if weight is None else weight[z])
    return t.reshape(4 * n, count * 2 * n * n)


def row_planes(level):
    return plane_matrix(level.n, *inner_lines(level), weight=0.5 * level.w_z)


def beside_planes(level):
    low, high = inner_lines(level)
    return plane_matrix(level.n, high, low, weight=0.5 * level.w_z)


def inner_lines(level):
    low, high = level.k[0].copy(), level.k[-1].copy()
    low[0] = 0.0
    high[-1] = 0.0
    return low, high


def face_matrix(level, count=2):
    n = level.n
    return plane_matrix(n, np.eye(n)[0], np.eye(n)[-1], count).T


def pair(consts, name, matrix):
    consts[name + "h"], consts[name + "l"] = hi_lo(matrix)


def fine_constants():
    dinv = pattern(FINE, 128)
    return dict(
        kc=packed_right(blocks(FINE.k, 16).T),
        wc=np.tile(FINE.w_p, 16)[None, :].astype(np.float32),
        cf=np.repeat(0.5 * np.kron(FINE.w_z, FINE.w_p)[:, None], 128, axis=1).astype(np.float32),
        d1=(FINE.first * dinv).astype(np.float32),
    )


def own_constants():
    c = fine_constants()
    pair(c, "m", closed_operator(FINE, 2))
    pair(c, "pl", row_planes(FINE))
    return c


def mid_constants():
    dinv = pattern(MID, 256)
    c = dict(
        wc=np.tile(MID.w_p, 64)[None, :].astype(np.float32),
        cf=np.repeat(0.5 * np.kron(MID.w_z, MID.w_p)[:, None], 256, axis=1).astype(np.float32),
        d1=(MID.first * dinv).astype(np.float32),
    )
    pair(c, "k", (sum_matrix(64, 4, True) @ blocks(MID.k, 64)).T)
    return c


def mid_own_constants():
    c = mid_constants()
    pair(c, "m", closed_operator(MID, 2))
    pair(c, "pl", row_planes(MID))
    c["pf"] = face_matrix(MID).astype(ml_dtypes.bfloat16)
    return c


def dot(a, b):
    return jnp.dot(a, b, preferred_element_type=f32)


def split(u):
    h = u.astype(bf16)
    return h, (u - h.astype(f32)).astype(bf16)


def left(c, name, parts):
    h, l = parts
    th, tl = c[name + "h"][...], c[name + "l"][...]
    return dot(th, h) + dot(th, l) + dot(tl, h)


def lefts(tables, parts):
    h, l = parts
    th = jnp.concatenate([c[name + "h"][...] for c, name in tables], axis=0)
    tl = jnp.concatenate([c[name + "l"][...] for c, name in tables], axis=0)
    t = dot(th, h) + dot(th, l) + dot(tl, h)
    out, at = [], 0
    for c, name in tables:
        rows = c[name + "h"].shape[0]
        out.append(t[at : at + rows])
        at += rows
    return out


def on_faces(planes):
    cube = (32, 8, planes.shape[1])
    which = lax.broadcasted_iota(jnp.int32, cube, 0)
    node = lax.broadcasted_iota(jnp.int32, cube, 1)
    outer = ((which < 16) & (node == 0)) | ((which >= 16) & (node == 7))
    return jnp.where(outer, planes.reshape(32, 1, -1), 0.0).reshape(256, -1)


def mid_faces(table, planes):
    h, l = split(planes)
    return dot(table, h) + dot(table, l)


def right(c, name, parts):
    h, l = parts
    th, tl = c[name + "h"][...], c[name + "l"][...]
    return dot(h, th) + dot(l, th) + dot(h, tl)


def tiles(ref, rows, lanes):
    t = ref[...]
    if lanes > 1:
        t = jnp.concatenate([t] * lanes, axis=1)
    if rows > 1:
        t = jnp.concatenate([t] * rows, axis=0)
    return t


def damping(level, c, step, rows, lanes):
    t = c["d1"][...]
    if step:
        t = t * (level.steps[step - 1][1] / level.first)
    t = jnp.concatenate([t] * lanes, axis=1) if lanes > 1 else t
    return jnp.concatenate([t] * rows, axis=0) if rows > 1 else t


def row_sum(before, here, after):
    lanes = here.shape[-1]
    cube = (16, 8, lanes)
    node = lax.broadcasted_iota(jnp.int32, cube, 1)
    out = here.reshape(cube)
    if before is not None:
        out = out + jnp.where(node == 0, pltpu.roll(before.reshape(cube), 1, 1), 0.0)
    if after is not None:
        out = out + jnp.where(node == 7, pltpu.roll(after.reshape(cube), 7, 1), 0.0)
    return out.reshape(128, lanes)


def col_sum(y):
    lanes = y.shape[-1]
    node = lax.broadcasted_iota(jnp.int32, y.shape, 1) % 8
    b = pltpu.roll(y, 1, 1)
    a = pltpu.roll(y, lanes - 1, 1)
    return y + jnp.where(node == 0, b, 0.0) + jnp.where(node == 7, a, 0.0)


def col_stiff(parts, kc):
    h, l = parts
    y = []
    for k in range(h.shape[1] // 128):
        s = slice(128 * k, 128 * k + 128)
        z = dot(jnp.concatenate([h[:, s], l[:, s]], axis=1), kc)
        y.append(z[:, :128] + z[:, 128:])
    return col_sum(jnp.concatenate(y, axis=1))


def fine_own(parts, c, planes=None, more=()):
    lanes = parts[0].shape[1] // 128
    t, *rest = lefts([(c, "m"), *more], parts)
    if planes is not None:
        t = t + on_faces(planes)
    a = tiles(c["wc"], 1, lanes) * t + tiles(c["cf"], 2, lanes) * col_stiff(parts, c["kc"][...])
    return (a, *rest) if more else a


def mid_apply(t, parts, c):
    y = right(c, "k", parts)
    return c["wc"][...] * t + tiles(c["cf"], t.shape[0] // 32, 1) * y


def mid_own(u, c, planes=None):
    parts = split(u)
    t = left(c, "m", parts)
    if planes is not None:
        t = t + mid_faces(c["pf"][...], planes)
    return mid_apply(t, parts, c)


class Table:
    def __init__(self, ref, at, shape, count):
        self.ref, self.at, self.shape, self.count = ref, at, shape, count

    def __getitem__(self, index):
        rows, lanes = self.shape
        step = rows + -rows % 16
        parts = [self.ref[self.at + step * k : self.at + step * k + rows] for k in range(self.count)]
        value = parts[0] if self.count == 1 else jnp.concatenate(parts, axis=1)
        value = value[:, :lanes]
        return value if index is Ellipsis else value[index]


def packed(consts):
    arrays, places = [], {}
    for kind in (np.float32, ml_dtypes.bfloat16):
        pieces, at = [], 0
        for name in sorted(consts):
            t = consts[name]
            if t.dtype != kind:
                continue
            rows, lanes = t.shape
            count = -(-lanes // 128)
            t = np.pad(t, ((0, -rows % 16), (0, count * 128 - lanes)))
            places[name] = (len(arrays), at, (rows, lanes), count)
            pieces += [t[:, 128 * k : 128 * k + 128] for k in range(count)]
            at += count * t.shape[0]
        if pieces:
            arrays.append(np.concatenate(pieces, axis=0))
    return arrays, places


def ready(held):
    def body(c, ins, outs):
        outs[0][...] = jnp.zeros((8, 128), f32)

    return call(body, [(8, 128)], held, ())[0]


def call(body, outs, held, args, scratch=(), vmem=24, direct=0):
    arrays, places = held
    n, k = len(arrays), len(args)

    def kernel(*refs):
        c = {name: Table(refs[p[0]], *p[1:]) for name, p in places.items()}
        body(c, refs[n : n + k], refs[n + k :])

    spec = pl.BlockSpec(memory_space=pltpu.VMEM)
    return pl.pallas_call(
        kernel,
        out_shape=[jax.ShapeDtypeStruct(s, f32) for s in outs],
        in_specs=[spec] * (n + k),
        out_specs=[pl.BlockSpec(memory_space=pl.ANY)] * direct + [spec] * (len(outs) - direct),
        scratch_shapes=list(scratch),
        compiler_params=pltpu.CompilerParams(vmem_limit_bytes=vmem * MB),
    )(*arrays, *args)


def under(c, prefix):
    return {k[2:]: v for k, v in c.items() if k.startswith(prefix)}


def rhs_tables(consts):
    w = np.kron(np.tile(FINE.w, 2), FINE.w)[:, None] * np.tile(FINE.w, 16)[None, :]
    consts["w"] = (0.125 * w).astype(np.float32)


def fine_rhs(held, first, second, from_right, from_left, at_hand):
    def body(c, ins, outs):
        parts = ins[:4]
        b_out, low, high = outs
        w = tiles(c["w"], 1, 4)
        src = []
        for e in range(2):
            s = slice(8 * e, 8 * e + 8)
            src.append(jnp.concatenate([v[:, s, :].reshape(128, 128) for v in parts], axis=1) * w)
        b = []
        for y in (row_sum(None, src[0], src[1]), row_sum(src[0], src[1], None)):
            y = col_sum(y)
            inner = y[56:64] + y[64:72]
            b.append(jnp.concatenate([y[:56], inner, inner, y[72:]], axis=0))
        face0 = b[0].reshape(16, 8, 512)[:, 0, :]
        face1 = b[1].reshape(16, 8, 512)[:, 7, :]
        b = jnp.concatenate(b, axis=0)
        b_out[...] = b
        planes = left(c, "f_pl", split(tiles(c["f_d1"], 2, 4) * b))
        low[0:16] = face0
        low[16:32] = planes[:16]
        high[0:16] = face1
        high[16:32] = planes[16:]

    return call(
        body,
        [(256, 512), (32, 512), (32, 512)],
        held,
        (first, second, from_right, from_left, at_hand),
    )


def faced(low, high, at, rows):
    return jnp.concatenate([low[at : at + rows], high[at : at + rows]], axis=0)


def rhs_depth():
    return MID.sum_z @ blocks(J_FINE.T, 2) @ np.diag(FINE.m_z)


def middle_tables(consts):
    inside = np.ones(8)
    inside[0] = inside[7] = 0.0
    q = plane_matrix(8, J_FINE[:, 0] * inside, J_FINE[:, 3] * inside)
    q = blocks(rhs_depth(), 2) @ q
    pair(consts, "q", q)
    outer = np.zeros((2, 16, 8))
    outer[0, :, 0] = outer[1, :, 7] = 1.0
    pair(consts, "qm", (q @ closed_operator(FINE, 2)) * (1.0 - outer.reshape(1, 256)))
    pair(consts, "qc", q * np.tile(0.5 * np.kron(FINE.w_z, FINE.w_p), 2)[None, :])


def fine_middle(held, b, below, above):
    def body(c, ins, outs):
        b, below, above = ins
        x_out, r_out, d_out, low, high = outs
        b = b[...] + on_faces(faced(below, above, 0, 16))
        f = under(c, "f_")
        d1, d2, d3 = (damping(FINE, f, k, 2, 4) for k in range(3))
        d = d1 * b
        x = d
        r = b - fine_own(split(d), f, faced(below, above, 16, 16))
        d = FINE.steps[0][0] * d + d2 * r
        x_out[...] = (x + d)[:, :256]
        a, plane1 = fine_own(split(d), f, more=[(f, "pl")])
        r = r - a
        d = FINE.steps[1][0] * d + d3 * r
        r_out[...] = r
        d_out[...] = d
        parts = split(d)
        plane2, rows, columns = lefts([(f, "pl"), (c, "qm"), (c, "qc")], parts)
        plane3 = left(c, "q", split(r)) - tiles(f["wc"], 1, 4) * rows
        plane3 = plane3 - col_stiff(split(columns), f["kc"][...])
        for k, plane in enumerate((plane1, plane2)):
            low[16 * k : 16 * k + 16] = plane[:16]
            high[16 * k : 16 * k + 16] = plane[16:]
        low[32:40] = plane3[:8]
        high[32:40] = plane3[8:]

    return call(
        body,
        [(256, 256), (256, 512), (256, 512), (40, 512), (40, 512)],
        held,
        (b, below, above),
    )


def last_tables(consts):
    kappa = float(np.sum(J_FINE[1:7, 0] * FINE.k[1:7, 0]))
    t = kappa * plane_matrix(8, np.eye(8)[0], np.eye(8)[7], weight=0.5 * FINE.w_z)
    z = rhs_depth()
    pair(consts, "e", blocks(z, 2) @ t)
    rows = sum_matrix(2, 4, False) @ blocks(J_FINE.T @ np.diag(FINE.m_p), 2)
    rows[0, 0] += 0.5
    rows[-1, -1] += 0.5
    t = np.einsum("zy,eafb->ezafyb", z, rows.reshape(2, 4, 2, 8)).reshape(64, 256)
    pair(consts, "ra", t)
    consts["rp"] = face_matrix(MID).astype(ml_dtypes.bfloat16)
    t = sum_matrix(64, 4, True) @ blocks(J_FINE.T @ np.diag(FINE.m_p), 64)
    pair(consts, "rc", t.T)


def fine_last(held, x, r, d, below, above):
    def body(c, ins, outs):
        x, r, d, below, above = ins
        x0, r0, b_out, r1_out, low, high = outs
        f, m = under(c, "f_"), under(c, "m_")
        wc = tiles(f["wc"], 1, 4)
        change = wc * on_faces(faced(below, above, 0, 16))
        r = r[...] - change
        d = d[...] - damping(FINE, f, 2, 2, 4) * change
        x0[...] = x[...] + d[:, :256]
        parts = split(d)
        a, inside = fine_own(parts, f, faced(below, above, 16, 16), [(c, "e")])
        r = r - a
        lane = lax.broadcasted_iota(jnp.int32, (256, 128), 1)
        r0[:, :256] = r[:, :256]
        r0[:, 256:] = jnp.where(lane < 64, r[:, 256:384], r[:, 384:])
        beyond = faced(below, above, 32, 8) - wc * inside
        b = left(c, "ra", split(r)) + mid_faces(c["rp"][...], beyond)
        b = right(c, "rc", split(b))
        b_out[...] = b
        d = tiles(m["d1"], 2, 1) * b
        plane1 = left(m, "pl", split(d))
        r = b - mid_own(d, m)
        r1_out[...] = r
        d = MID.steps[0][0] * d + damping(MID, m, 1, 2, 1) * r
        plane2 = left(m, "pl", split(d))
        for k, plane in enumerate((plane1, plane2)):
            low[8 * k : 8 * k + 8] = plane[:8]
            high[8 * k : 8 * k + 8] = plane[8:]

    return call(
        body,
        [(256, 256), (256, 384), (64, 256), (64, 256), (16, 256), (16, 256)],
        held,
        (x, r, d, below, above),
    )


def share_tables(consts):
    top = np.zeros((3, 4))
    top[0, 0] = top[1, 1] = top[1, 2] = top[2, 3] = 1.0
    jz = top @ blocks(J_MID.T, 2)

    def down(z_part, r_part):
        t = np.zeros((4, 4, 2, 8, 4))
        for e in range(2):
            for k in range(2):
                t[e + k, :3, e] += np.einsum("zy,b->zyb", jz @ z_part, (J_MID.T @ r_part)[k])
        return t.reshape(16, 64)

    def across(part):
        t = np.zeros((256, 32))
        for v in range(32):
            t[4 * v : 4 * v + 4, v] += (J_MID.T @ part)[0]
            at = (4 * v - 4) % 256
            t[at : at + 4, v] += (J_MID.T @ part)[1]
        return np.tile(t, (1, 4))

    wz, wr = blocks(np.diag(MID.w), 2), np.diag(MID.w)
    kz = blocks(MID.k, 2)
    pair(consts, "sm", down(np.diag(MID.m_z), np.diag(MID.m_p)))
    pair(
        consts,
        "s1",
        0.5 * down(kz, wr) + 0.5 * down(wz, MID.k) + mass_coef * down(wz, wr),
    )
    pair(consts, "s2", 0.5 * down(wz, wr))
    pair(
        consts,
        "sc",
        np.concatenate([across(np.diag(MID.m_p)), -across(wr), -across(MID.k)], axis=0),
    )


def mid_last(held, b, r1, below, above):
    def body(c, ins, outs):
        b, r1, below, above = ins
        chunk, lo, hi, lo2, hi2, block, sems = outs
        down, c = c, under(c, "m_")
        d1, d2, d3 = (damping(MID, c, k, 2, 1) for k in range(3))
        d = d1 * b[...]
        x = d
        r = r1[...] - c["wc"][...] * mid_faces(c["pf"][...], faced(below, above, 0, 8))
        d = MID.steps[0][0] * d + d2 * r
        x = x + d
        r = r - mid_own(d, c, faced(below, above, 8, 8))
        d = MID.steps[1][0] * d + d3 * r
        x = x + d
        parts = split(d)
        t = jnp.concatenate(
            [left(down, "sm", split(r)), *lefts([(down, "s1"), (down, "s2")], parts)], axis=1
        )
        t = right(down, "sc", split(t))
        t = jnp.concatenate([t, t, t], axis=1)
        q = lax.broadcasted_iota(jnp.int32, t.shape, 0)
        lane = lax.broadcasted_iota(jnp.int32, t.shape, 1) // 32
        t = jnp.sum(jnp.where(q == lane, t, 0.0), axis=0, keepdims=True)
        which = lax.broadcasted_iota(jnp.int32, block.shape, 0) % 3
        block[...] = jnp.where(
            which == 0, t[:, :128], jnp.where(which == 1, t[:, 128:256], t[:, 256:])
        )
        copies = [
            pltpu.make_async_copy(block, chunk.at[pl.ds(192 * k, 192)], sems.at[k]) for k in range(4)
        ]
        for copy in copies:
            copy.start()
        plane1 = left(c, "pl", parts)
        r = r - mid_own(d, c)
        plane2 = left(c, "pl", split(d1 * r))
        for near, far, at in ((lo, lo2, 0), (hi, hi2, 1)):
            near[0:64] = r
            near[64:72] = plane1[8 * at : 8 * at + 8]
            near[72:104] = x[32 * at : 32 * at + 32]
            far[0:8] = plane1[8 * at : 8 * at + 8]
            far[8:16] = plane2[8 * at : 8 * at + 8]
        for copy in copies:
            copy.wait()

    return call(
        body,
        [(768, 128), (104, 256), (104, 256), (16, 256), (16, 256)],
        held,
        (b, r1, below, above),
        scratch=[pltpu.VMEM((192, 128), f32), pltpu.SemaphoreType.DMA((4,))],
        direct=1,
    )


def coarse_operator():
    row = lax.broadcasted_iota(jnp.int32, (128, 128), 0)
    lane = lax.broadcasted_iota(jnp.int32, (128, 128), 1)
    z, z2 = row >> 5, lane >> 5
    apart = jnp.abs((row & 31) - (lane & 31))
    w = jnp.where(z == 1, 2.0, jnp.where(z == 3, 0.0, 1.0))
    w = jnp.where(z == z2, w, 0.0)
    next_plane = (jnp.abs(z - z2) == 1) & (z + z2 < 5)
    inner = jnp.where(apart == 0, 3.0 * w - next_plane.astype(f32), 0.0)
    inner = inner - jnp.where(apart == 1, 0.5 * w, 0.0)
    ends = jnp.where(apart == 31, -0.5 * w, 0.0)
    m = jnp.concatenate([inner, ends], axis=1).astype(bf16)
    return jnp.concatenate([m, m], axis=0)


def coarse_solve(g):
    m = coarse_operator()
    plane = lax.broadcasted_iota(jnp.int32, (1, 128), 1) // 32
    wz = jnp.where(plane == 1, 2.0, jnp.where(plane == 3, 0.0, 1.0))

    def after(u):
        return jnp.concatenate([u[8:], u[:8]], axis=0)

    def before(u):
        return jnp.concatenate([u[-8:], u[:-8]], axis=0)

    column = lax.broadcasted_iota(jnp.int32, (32, 8, 128), 2) % 32

    def columns(u):
        h = u.astype(bf16)
        rest = u - h.astype(f32)
        k, l = split(rest)
        t = dot(jnp.concatenate([h, k], axis=1), m) + dot(l, m[:128])
        ends = t[:, 128:].reshape(32, 8, 128)
        ends = jnp.where(
            column == 31,
            pltpu.roll(ends, 7, 1),
            jnp.where(column == 0, pltpu.roll(ends, 1, 1), 0.0),
        )
        return t[:, :128] + ends.reshape(256, 128)

    half = -0.5 * wz
    mass = 4.0 * mass_coef * wz

    def apply(p):
        p0, p1 = p
        return (
            columns(p0) + half * (p1 + before(p1)) + mass * p0,
            columns(p1) + half * (p0 + after(p0)) + mass * p1,
        )

    def inner_product(a, b):
        s = jnp.sum(a[0] * b[0] + a[1] * b[1], axis=0, keepdims=True)
        return jnp.sum(s, axis=1, keepdims=True)

    r = (g[:, 0:128] + before(g[:, 256:384]), g[:, 128:256])
    p = r
    x = (jnp.zeros_like(r[0]), jnp.zeros_like(r[1]))
    norm = inner_product(r, r)
    for it in range(CG_ITERS):
        q = apply(p)
        alpha = norm / inner_product(p, q)
        x = tuple(a + alpha * b for a, b in zip(x, p))
        if it + 1 < CG_ITERS:
            r = tuple(a - alpha * b for a, b in zip(r, q))
            new = inner_product(r, r)
            beta = new / norm
            p = tuple(a + beta * b for a, b in zip(r, p))
            norm = new
    return jnp.concatenate(x, axis=1)


def second_tables(consts):
    pair(consts, "c", closed_operator(MID, 6))
    t = np.concatenate([blocks(face_matrix(MID), 3), face_matrix(MID, 6)], axis=1)
    consts["p"] = t.astype(ml_dtypes.bfloat16)
    pair(consts, "po", beside_planes(MID))
    jc = np.zeros((4, 32, 256))
    for e in range(64):
        element = e if e < 48 else e - 64
        for k in range(2):
            v = element + k
            dev, col = v // 32 + 1, v % 32
            jc[dev, col, 4 * e : 4 * e + 4] = J_MID[:, k]
    jc = jc.reshape(128, 256)
    pair(consts, "vc", jc)
    pair(consts, "vk", jc @ (sum_matrix(64, 4, True) @ blocks(MID.k, 64)).T)
    jz = np.zeros((8, 3))
    jz[:4, :2] += J_MID
    jz[4:, 1:] += J_MID
    jdr = np.zeros((10, 8, 4, 3, 16))
    for e in range(10):
        for k in range(2):
            jdr[e, :, :, :, e + k] += np.einsum("zp,a->zap", jz, J_MID[:, k])
    order = [2 * (q % 8) + q // 8 for q in range(16)]
    vd = jdr[..., order].reshape(320, 48)
    pair(consts, "vd", vd)
    pair(consts, "va", window_operator(MID, 10) @ vd)
    pair(consts, "fo", blocks(J_FINE.T, 32))
    fc = np.zeros((128, 128))
    for e in range(16):
        src = e if e < 8 else e + 16
        fc[4 * src : 4 * src + 4, 8 * e : 8 * e + 8] = J_FINE.T
    pair(consts, "fh", fc)
    fd = np.kron(blocks(J_FINE, 2), J_FINE)
    pair(consts, "fd", blocks(fd, 2))
    pair(consts, "fp", beside_planes(FINE) @ blocks(fd, 2))


def second_smoothing(held, gathered, x0, r0, own_lo, own_hi, below, above, below2, above2):
    def body(c, ins, outs):
        gathered, x0, r0, own_lo, own_hi, below, above, below2, above2 = ins
        s_out, r_out, d_out, low, high, twice = outs
        i, j = lax.axis_index("gx"), lax.axis_index("gy")
        f, m = under(c, "f_"), under(c, "m_")
        x2 = coarse_solve(gathered)
        twice[0:256] = x2
        twice[256:512] = x2
        first = lax.rem(i + 30, 32)
        picked = twice[pl.ds(pl.multiple_of(first * 8, 8), 64), :].reshape(8, 8, 256)
        sub = lax.broadcasted_iota(jnp.int32, (8, 8, 256), 1)
        near = []
        for g in range(3):
            v = jnp.sum(jnp.where(sub == lax.rem(j + 7 + g, 8), picked, 0.0), axis=1)
            near.append(jnp.concatenate([v[:, :128], v[:, 128:]], axis=0))
        block = lax.broadcasted_iota(jnp.int32, (16, 128), 1) // 32
        y = []
        for z in range(3):
            v = [pltpu.roll(near[g], (32 * (g - z)) % 128, 1) if g != z else near[g] for g in range(3)]
            y.append(
                jnp.where(block == 0, v[0], jnp.where(block == 1, v[1], jnp.where(block == 2, v[2], 0.0)))
            )
        parts = split(jnp.concatenate(y, axis=0))
        yk = left(c, "vd", split(right(c, "vk", parts)))
        e2, ya = lefts([(c, "vd"), (c, "va")], split(right(c, "vc", parts)))
        g = m["wc"][...] * ya + tiles(m["cf"], 8, 1) * yk[32:-32]

        def table(step, count):
            return damping(MID, m, step, count, 1)

        planes = jnp.concatenate(
            [
                below2[:8],
                own_lo[64:72],
                below[64:72],
                above[64:72],
                own_hi[64:72],
                above2[:8],
            ],
            axis=0,
        )
        r = jnp.concatenate([below[:64], own_lo[:64], above[:64]], axis=0)
        r = r - m["wc"][...] * mid_faces(c["p"][:, :48], planes) - g[32:224]
        d = table(0, 6) * r
        x = jnp.concatenate([below[72:104], own_lo[72:104], own_hi[72:104], above[72:104]], axis=0)
        x = x + e2[96:224] + d[32:160]
        outer = jnp.concatenate([g[:32], g[224:]], axis=0) * table(0, 2)
        planes = faced(below2, above2, 8, 8) - left(c, "po", split(outer))
        parts = split(d)
        r = r - mid_apply(left(c, "c", parts) + mid_faces(c["p"][:, 48:], planes), parts, m)
        d = MID.steps[0][0] * d + table(1, 6) * r
        x = x + d[32:160]
        h, l = split(d)
        inner = {"h": c["ch"][32:160], "l": c["cl"][32:160]}
        r = r[32:160] - mid_apply(left(inner, "", (h, l)), (h[32:-32], l[32:-32]), m)
        d = MID.steps[1][0] * d[32:160] + table(2, 4) * r
        x = x + d
        h, l = split(x)
        x = jnp.concatenate(
            [
                right(c, "fo", (h[:, :128], l[:, :128])),
                right(c, "fh", (h[:, 128:], l[:, 128:])),
            ],
            axis=1,
        )
        e1 = left(c, "fd", split(x[32:96]))
        planes = left(c, "fp", split(jnp.concatenate([x[:32], x[96:]], axis=0)))
        r = r0[...] - fine_own(split(e1), f, planes)
        d = tiles(f["d1"], 2, 3) * r
        s_out[...] = x0[...] + (e1 + d)[:, :256]
        a, plane1 = fine_own(split(d), f, more=[(f, "pl")])
        r = r - a
        d = FINE.steps[0][0] * d + damping(FINE, f, 1, 2, 3) * r
        plane2 = left(f, "pl", split(d))
        r_out[...] = r
        d_out[...] = d
        for k, plane in enumerate((plane1, plane2)):
            low[16 * k : 16 * k + 16] = plane[:16]
            high[16 * k : 16 * k + 16] = plane[16:]

    return call(
        body,
        [(256, 256), (256, 384), (256, 384), (32, 384), (32, 384)],
        held,
        (gathered, x0, r0, own_lo, own_hi, below, above, below2, above2),
        scratch=[pltpu.VMEM((512, 256), f32)],
    )


def last_step(held, s, r, d, below, above):
    def body(c, ins, outs):
        c = under(c, "f_")
        s, r, d, below, above = ins
        (out,) = outs
        change = tiles(c["wc"], 1, 3) * on_faces(faced(below, above, 0, 16))
        r = r[...] - change
        d = d[...] - damping(FINE, c, 1, 2, 3) * change
        r = r - fine_own(split(d), c, faced(below, above, 16, 16))
        v = s[...] + d[:, :256]
        d = FINE.steps[1][0] * d + damping(FINE, c, 2, 2, 3) * r
        v = v + d[:, :256]
        for e in range(2):
            out[:, 8 * e : 8 * e + 8, :] = v[128 * e : 128 * e + 128].reshape(16, 8, 256)

    return call(body, [(16, 16, 256)], held, (s, r, d, below, above))[0]


def fetch(value, axis, offset):
    count = lax.axis_size(axis)
    return lax.ppermute(value, axis, [((i + offset) % count, i) for i in range(count)])


def both(low, high, offset=1):
    return fetch(high, "gx", -offset), fetch(low, "gx", offset)


def tables(*adds, mid=mid_own_constants):
    consts = {"f_" + k: v for k, v in own_constants().items()}
    consts.update({"m_" + k: v for k, v in mid().items()})
    for add in adds:
        add(consts)
    arrays, places = packed(consts)
    return [jnp.asarray(a) for a in arrays], places


def local(source):
    first, second = source[:, :, :128], source[:, :, 128:]
    from_right, from_left = fetch(first, "gy", 1), fetch(second, "gy", -1)
    held = tables(rhs_tables, middle_tables, last_tables, share_tables)
    b, low, high = fine_rhs(held, first, second, from_right, from_left, ready(held))
    x, r, d, low, high = fine_middle(held, b, *both(low, high))
    x0, r0, b, r1, low, high = fine_last(held, x, r, d, *both(low, high))
    chunk, lo, hi, lo2, hi2 = mid_last(held, b, r1, *both(low, high))
    gathered = lax.all_to_all(chunk.reshape(256, 384), ("gx", "gy"), 0, 0, tiled=True)
    s, r, d, low, high = second_smoothing(
        tables(second_tables, mid=mid_constants), gathered, x0, r0, lo, hi, *both(lo, hi), *both(lo2, hi2, 2)
    )
    return last_step(tables(mid=dict), s, r, d, *both(low, high))


def solution(mesh):
    return jax.shard_map(
        local,
        mesh=mesh,
        in_specs=(P(None, "gx", "gy"),),
        out_specs=P(None, "gx", "gy"),
        check_vma=False,
    )
```

```python
import math

import jax
import jax.numpy as jnp
import ml_dtypes
import numpy as np
from jax import lax
from jax.experimental import pallas as pl
from jax.experimental.pallas import tpu as pltpu
from jax.sharding import PartitionSpec as P

CG_ITERS = 8
mass_coef = 0.000125
cheb_ratio = 0.1
f32 = jnp.float32
bf16 = jnp.bfloat16
MB = 1024 * 1024


def legendre_pair(points, order):
    previous = 0.0 * points + 1.0
    current = points * 1.0
    for degree in range(2, order + 1):
        previous, current = (
            current,
            ((2.0 * degree - 1.0) * points * current - (degree - 1.0) * previous) / degree,
        )
    return (previous, current)


def gll_tables(order):
    count_nodes = order + 1
    points = -np.cos(math.pi * np.arange(count_nodes) / order)
    for sweep in range(60):
        previous, values_at = legendre_pair(points, order)
        points = points - (points * values_at - previous) / (count_nodes * values_at)
    previous, values_at = legendre_pair(points, order)
    weights = 2.0 / (order * (order + 1) * values_at * values_at)
    spacing = points[:, None] - points[None, :]
    safe_spacing = np.where(spacing == 0.0, 1.0, spacing)
    derivative = values_at[:, None] / (values_at[None, :] * safe_spacing)
    derivative = derivative * (1.0 - np.eye(count_nodes))
    corner_value = order * (order + 1) / 4.0
    end_values = np.concatenate(
        [np.array([-corner_value]), np.zeros(count_nodes - 2), np.array([corner_value])]
    )
    return (points, weights, derivative + np.eye(count_nodes) * end_values[None, :])


def interp_table(fine_order, coarse_order):
    fine_points = gll_tables(fine_order)[0]
    coarse_points = gll_tables(coarse_order)[0]
    numer = fine_points[:, None, None] - coarse_points[None, None, :]
    denom = coarse_points[None, :, None] - coarse_points[None, None, :]
    same_node = np.eye(len(coarse_points))[None, :, :] > 0.5
    ratio = np.where(same_node, 1.0, numer / np.where(same_node, 1.0, denom))
    return ratio.prod(axis=2)


def element_bound(order):
    points, weights, derivative = gll_tables(order)
    mass = np.eye(order + 1) * weights[None, :]
    stiff = np.dot(derivative.T, np.dot(mass, derivative))
    full = 0.5 * (
        np.kron(np.kron(mass, mass), stiff)
        + np.kron(np.kron(mass, stiff), mass)
        + np.kron(np.kron(stiff, mass), mass)
    ) + mass_coef * np.kron(np.kron(mass, mass), mass)
    diagonal_entries = np.sum(full * np.eye(full.shape[0]), axis=1)
    ratio = np.abs(full).sum(axis=1) / diagonal_entries
    return float(ratio.max())


def sum_matrix(elements, n, cyclic):
    out = np.eye(elements * n)
    for e in range(elements):
        if cyclic or e + 1 < elements:
            a, b = e * n + n - 1, ((e + 1) % elements) * n
            out[a, b] += 1.0
            out[b, a] += 1.0
    return out


def blocks(matrix, count):
    return np.kron(np.eye(count), matrix)


class Level:
    def __init__(self, order):
        n = self.n = order + 1
        _, w, dm = gll_tables(order)
        self.w = w
        self.k = dm.T @ np.diag(w) @ dm
        self.sum_z = sum_matrix(2, n, False)
        self.k_z = self.sum_z @ blocks(self.k, 2)
        self.w_z = self.sum_z @ np.tile(w, 2)
        self.w_p = w.copy()
        self.w_p[0] += w[-1]
        self.w_p[-1] += w[0]
        kd = np.diag(self.k).copy()
        kd_p = kd.copy()
        kd_p[0] += kd[-1]
        kd_p[-1] += kd[0]
        kd_z = self.sum_z @ np.tile(kd, 2)
        wz, wp = self.w_z, self.w_p
        diag = 0.5 * (
            np.einsum("z,r,c->zrc", wz, kd_p, wp)
            + np.einsum("z,r,c->zrc", wz, wp, kd_p)
            + np.einsum("z,r,c->zrc", kd_z, wp, wp)
        ) + mass_coef * np.einsum("z,r,c->zrc", wz, wp, wp)
        self.dinv = 1.0 / diag
        upper = element_bound(order)
        lower = cheb_ratio * upper
        center, half = 0.5 * (upper + lower), 0.5 * (upper - lower)
        sigma = center / half
        rho = 1.0 / sigma
        self.first = 1.0 / center
        self.steps = []
        for _ in range(2):
            rho2 = 1.0 / (2.0 * sigma - rho)
            self.steps.append((float(rho2 * rho), 2.0 * rho2 / half))
            rho = rho2
        self.m_p = np.ones(n)
        self.m_p[0] = self.m_p[-1] = 0.5
        self.m_z = np.ones(2 * n)
        self.m_z[n - 1] = self.m_z[n] = 0.5


def hi_lo(matrix):
    matrix = np.asarray(matrix, np.float64)
    hi = matrix.astype(ml_dtypes.bfloat16)
    lo = (matrix - hi.astype(np.float64)).astype(ml_dtypes.bfloat16)
    return hi, lo


def packed_left(matrix):
    hi, lo = hi_lo(matrix)
    return np.block([[hi, hi], [lo, np.zeros_like(lo)]])


def packed_right(matrix):
    hi, lo = hi_lo(matrix)
    return np.block([[hi, lo], [hi, np.zeros_like(lo)]])


FINE, MID, COARSE = Level(7), Level(3), Level(1)
J_FINE, J_MID = interp_table(7, 3), interp_table(3, 1)


def pattern(level, lanes):
    d = level.dinv.reshape(2 * level.n * level.n, level.n)
    return np.tile(d, (1, lanes // level.n))


def closed_operator(level, rows):
    n = level.n
    k_r = sum_matrix(rows, n, False) @ blocks(level.k, rows)
    k_r[0, 0] += level.k[-1, -1]
    k_r[-1, -1] += level.k[0, 0]
    return tensor_rows(level, k_r.reshape(rows, n, rows, n), rows)


def tensor_rows(level, k_r, rows):
    n = level.n
    w_r = np.diag(np.tile(level.w_p, rows)).reshape(rows, n, rows, n)
    kz, wz = level.k_z, np.diag(level.w_z)
    t = (
        0.5 * np.einsum("zy,eafb->ezafyb", kz, w_r)
        + 0.5 * np.einsum("zy,eafb->ezafyb", wz, k_r)
        + mass_coef * np.einsum("zy,eafb->ezafyb", wz, w_r)
    )
    return t.reshape(rows * 2 * n * n, rows * 2 * n * n)


def window_operator(level, rows):
    n = level.n
    k_r = sum_matrix(rows, n, False) @ blocks(level.k, rows)
    size = 2 * n * n
    return tensor_rows(level, k_r.reshape(rows, n, rows, n), rows)[size:-size]


def plane_matrix(n, low, high, count=2, weight=None):
    t = np.zeros((2, 2 * n, count, 2 * n, n))
    for z in range(2 * n):
        t[0, z, 0, z] = low * (1.0 if weight is None else weight[z])
        t[1, z, count - 1, z] = high * (1.0 if weight is None else weight[z])
    return t.reshape(4 * n, count * 2 * n * n)


def row_planes(level):
    return plane_matrix(level.n, *inner_lines(level), weight=0.5 * level.w_z)


def beside_planes(level):
    low, high = inner_lines(level)
    return plane_matrix(level.n, high, low, weight=0.5 * level.w_z)


def inner_lines(level):
    low, high = level.k[0].copy(), level.k[-1].copy()
    low[0] = 0.0
    high[-1] = 0.0
    return low, high


def face_matrix(level, count=2):
    n = level.n
    return plane_matrix(n, np.eye(n)[0], np.eye(n)[-1], count).T


def pair(consts, name, matrix):
    consts[name + "h"], consts[name + "l"] = hi_lo(matrix)


def fine_constants():
    dinv = pattern(FINE, 128)
    return dict(
        kc=packed_right(blocks(FINE.k, 16).T),
        wc=np.tile(FINE.w_p, 16)[None, :].astype(np.float32),
        cf=np.repeat(0.5 * np.kron(FINE.w_z, FINE.w_p)[:, None], 128, axis=1).astype(np.float32),
        d1=(FINE.first * dinv).astype(np.float32),
    )


def own_constants():
    c = fine_constants()
    pair(c, "m", closed_operator(FINE, 2))
    pair(c, "pl", row_planes(FINE))
    return c


def mid_constants():
    dinv = pattern(MID, 256)
    c = dict(
        wc=np.tile(MID.w_p, 64)[None, :].astype(np.float32),
        cf=np.repeat(0.5 * np.kron(MID.w_z, MID.w_p)[:, None], 256, axis=1).astype(np.float32),
        d1=(MID.first * dinv).astype(np.float32),
    )
    pair(c, "k", (sum_matrix(64, 4, True) @ blocks(MID.k, 64)).T)
    return c


def mid_own_constants():
    c = mid_constants()
    pair(c, "m", closed_operator(MID, 2))
    pair(c, "pl", row_planes(MID))
    c["pf"] = face_matrix(MID).astype(ml_dtypes.bfloat16)
    return c


def dot(a, b):
    return jnp.dot(a, b, preferred_element_type=f32)


def split(u):
    h = u.astype(bf16)
    return h, (u - h.astype(f32)).astype(bf16)


def left(c, name, parts):
    h, l = parts
    th, tl = c[name + "h"][...], c[name + "l"][...]
    return dot(th, h) + dot(th, l) + dot(tl, h)


def lefts(tables, parts):
    h, l = parts
    th = jnp.concatenate([c[name + "h"][...] for c, name in tables], axis=0)
    tl = jnp.concatenate([c[name + "l"][...] for c, name in tables], axis=0)
    t = dot(th, h) + dot(th, l) + dot(tl, h)
    out, at = [], 0
    for c, name in tables:
        rows = c[name + "h"].shape[0]
        out.append(t[at : at + rows])
        at += rows
    return out


def on_faces(planes):
    cube = (32, 8, planes.shape[1])
    which = lax.broadcasted_iota(jnp.int32, cube, 0)
    node = lax.broadcasted_iota(jnp.int32, cube, 1)
    outer = ((which < 16) & (node == 0)) | ((which >= 16) & (node == 7))
    return jnp.where(outer, planes.reshape(32, 1, -1), 0.0).reshape(256, -1)


def mid_faces(table, planes):
    h, l = split(planes)
    return dot(table, h) + dot(table, l)


def right(c, name, parts):
    h, l = parts
    th, tl = c[name + "h"][...], c[name + "l"][...]
    return dot(h, th) + dot(l, th) + dot(h, tl)


def tiles(ref, rows, lanes):
    t = ref[...]
    if lanes > 1:
        t = jnp.concatenate([t] * lanes, axis=1)
    if rows > 1:
        t = jnp.concatenate([t] * rows, axis=0)
    return t


def damping(level, c, step, rows, lanes):
    t = c["d1"][...]
    if step:
        t = t * (level.steps[step - 1][1] / level.first)
    t = jnp.concatenate([t] * lanes, axis=1) if lanes > 1 else t
    return jnp.concatenate([t] * rows, axis=0) if rows > 1 else t


def row_sum(before, here, after):
    lanes = here.shape[-1]
    cube = (16, 8, lanes)
    node = lax.broadcasted_iota(jnp.int32, cube, 1)
    out = here.reshape(cube)
    if before is not None:
        out = out + jnp.where(node == 0, pltpu.roll(before.reshape(cube), 1, 1), 0.0)
    if after is not None:
        out = out + jnp.where(node == 7, pltpu.roll(after.reshape(cube), 7, 1), 0.0)
    return out.reshape(128, lanes)


def col_sum(y):
    lanes = y.shape[-1]
    node = lax.broadcasted_iota(jnp.int32, y.shape, 1) % 8
    b = pltpu.roll(y, 1, 1)
    a = pltpu.roll(y, lanes - 1, 1)
    return y + jnp.where(node == 0, b, 0.0) + jnp.where(node == 7, a, 0.0)


def col_stiff(parts, kc):
    h, l = parts
    y = []
    for k in range(h.shape[1] // 128):
        s = slice(128 * k, 128 * k + 128)
        z = dot(jnp.concatenate([h[:, s], l[:, s]], axis=1), kc)
        y.append(z[:, :128] + z[:, 128:])
    return col_sum(jnp.concatenate(y, axis=1))


def fine_own(parts, c, planes=None, more=()):
    lanes = parts[0].shape[1] // 128
    t, *rest = lefts([(c, "m"), *more], parts)
    if planes is not None:
        t = t + on_faces(planes)
    a = tiles(c["wc"], 1, lanes) * t + tiles(c["cf"], 2, lanes) * col_stiff(parts, c["kc"][...])
    return (a, *rest) if more else a


def mid_apply(t, parts, c):
    y = right(c, "k", parts)
    return c["wc"][...] * t + tiles(c["cf"], t.shape[0] // 32, 1) * y


def mid_own(u, c, planes=None):
    parts = split(u)
    t = left(c, "m", parts)
    if planes is not None:
        t = t + mid_faces(c["pf"][...], planes)
    return mid_apply(t, parts, c)


class Table:
    def __init__(self, ref, at, shape, count):
        self.ref, self.at, self.shape, self.count = ref, at, shape, count

    def __getitem__(self, index):
        rows, lanes = self.shape
        step = rows + -rows % 16
        parts = [self.ref[self.at + step * k : self.at + step * k + rows] for k in range(self.count)]
        value = parts[0] if self.count == 1 else jnp.concatenate(parts, axis=1)
        value = value[:, :lanes]
        return value if index is Ellipsis else value[index]


def packed(consts):
    arrays, places = [], {}
    for kind in (np.float32, ml_dtypes.bfloat16):
        pieces, at = [], 0
        for name in sorted(consts):
            t = consts[name]
            if t.dtype != kind:
                continue
            rows, lanes = t.shape
            count = -(-lanes // 128)
            t = np.pad(t, ((0, -rows % 16), (0, count * 128 - lanes)))
            places[name] = (len(arrays), at, (rows, lanes), count)
            pieces += [t[:, 128 * k : 128 * k + 128] for k in range(count)]
            at += count * t.shape[0]
        if pieces:
            arrays.append(np.concatenate(pieces, axis=0))
    return arrays, places


def ready(held):
    def body(c, ins, outs):
        outs[0][...] = jnp.zeros((8, 128), f32)

    return call(body, [(8, 128)], held, ())[0]


def call(body, outs, held, args, scratch=(), vmem=24, direct=0):
    arrays, places = held
    n, k = len(arrays), len(args)

    def kernel(*refs):
        c = {name: Table(refs[p[0]], *p[1:]) for name, p in places.items()}
        body(c, refs[n : n + k], refs[n + k :])

    spec = pl.BlockSpec(memory_space=pltpu.VMEM)
    return pl.pallas_call(
        kernel,
        out_shape=[jax.ShapeDtypeStruct(s, f32) for s in outs],
        in_specs=[spec] * (n + k),
        out_specs=[pl.BlockSpec(memory_space=pl.ANY)] * direct + [spec] * (len(outs) - direct),
        scratch_shapes=list(scratch),
        compiler_params=pltpu.CompilerParams(vmem_limit_bytes=vmem * MB),
    )(*arrays, *args)


def under(c, prefix):
    return {k[2:]: v for k, v in c.items() if k.startswith(prefix)}


def rhs_tables(consts):
    w = np.kron(np.tile(FINE.w, 2), FINE.w)[:, None] * np.tile(FINE.w, 16)[None, :]
    consts["w"] = (0.125 * w).astype(np.float32)


def fine_rhs(held, first, second, from_right, from_left, at_hand):
    def body(c, ins, outs):
        parts = ins[:4]
        b_out, low, high = outs
        w = tiles(c["w"], 1, 4)
        src = []
        for e in range(2):
            s = slice(8 * e, 8 * e + 8)
            src.append(jnp.concatenate([v[:, s, :].reshape(128, 128) for v in parts], axis=1) * w)
        b = []
        for y in (row_sum(None, src[0], src[1]), row_sum(src[0], src[1], None)):
            y = col_sum(y)
            inner = y[56:64] + y[64:72]
            b.append(jnp.concatenate([y[:56], inner, inner, y[72:]], axis=0))
        face0 = b[0].reshape(16, 8, 512)[:, 0, :]
        face1 = b[1].reshape(16, 8, 512)[:, 7, :]
        b = jnp.concatenate(b, axis=0)
        b_out[...] = b
        planes = left(c, "f_pl", split(tiles(c["f_d1"], 2, 4) * b))
        low[0:16] = face0
        low[16:32] = planes[:16]
        high[0:16] = face1
        high[16:32] = planes[16:]

    return call(
        body,
        [(256, 512), (32, 512), (32, 512)],
        held,
        (first, second, from_right, from_left, at_hand),
    )


def faced(low, high, at, rows):
    return jnp.concatenate([low[at : at + rows], high[at : at + rows]], axis=0)


def rhs_depth():
    return MID.sum_z @ blocks(J_FINE.T, 2) @ np.diag(FINE.m_z)


def middle_tables(consts):
    inside = np.ones(8)
    inside[0] = inside[7] = 0.0
    q = plane_matrix(8, J_FINE[:, 0] * inside, J_FINE[:, 3] * inside)
    q = blocks(rhs_depth(), 2) @ q
    pair(consts, "q", q)
    outer = np.zeros((2, 16, 8))
    outer[0, :, 0] = outer[1, :, 7] = 1.0
    pair(consts, "qm", (q @ closed_operator(FINE, 2)) * (1.0 - outer.reshape(1, 256)))
    pair(consts, "qc", q * np.tile(0.5 * np.kron(FINE.w_z, FINE.w_p), 2)[None, :])


def fine_middle(held, b, below, above):
    def body(c, ins, outs):
        b, below, above = ins
        x_out, r_out, d_out, low, high = outs
        b = b[...] + on_faces(faced(below, above, 0, 16))
        f = under(c, "f_")
        d1, d2, d3 = (damping(FINE, f, k, 2, 4) for k in range(3))
        d = d1 * b
        x = d
        r = b - fine_own(split(d), f, faced(below, above, 16, 16))
        d = FINE.steps[0][0] * d + d2 * r
        x_out[...] = (x + d)[:, :256]
        a, plane1 = fine_own(split(d), f, more=[(f, "pl")])
        r = r - a
        d = FINE.steps[1][0] * d + d3 * r
        r_out[...] = r
        d_out[...] = d
        parts = split(d)
        plane2, rows, columns = lefts([(f, "pl"), (c, "qm"), (c, "qc")], parts)
        plane3 = left(c, "q", split(r)) - tiles(f["wc"], 1, 4) * rows
        plane3 = plane3 - col_stiff(split(columns), f["kc"][...])
        for k, plane in enumerate((plane1, plane2)):
            low[16 * k : 16 * k + 16] = plane[:16]
            high[16 * k : 16 * k + 16] = plane[16:]
        low[32:40] = plane3[:8]
        high[32:40] = plane3[8:]

    return call(
        body,
        [(256, 256), (256, 512), (256, 512), (40, 512), (40, 512)],
        held,
        (b, below, above),
    )


def last_tables(consts):
    kappa = float(np.sum(J_FINE[1:7, 0] * FINE.k[1:7, 0]))
    t = kappa * plane_matrix(8, np.eye(8)[0], np.eye(8)[7], weight=0.5 * FINE.w_z)
    z = rhs_depth()
    pair(consts, "e", blocks(z, 2) @ t)
    rows = sum_matrix(2, 4, False) @ blocks(J_FINE.T @ np.diag(FINE.m_p), 2)
    rows[0, 0] += 0.5
    rows[-1, -1] += 0.5
    t = np.einsum("zy,eafb->ezafyb", z, rows.reshape(2, 4, 2, 8)).reshape(64, 256)
    pair(consts, "ra", t)
    consts["rp"] = face_matrix(MID).astype(ml_dtypes.bfloat16)
    t = sum_matrix(64, 4, True) @ blocks(J_FINE.T @ np.diag(FINE.m_p), 64)
    pair(consts, "rc", t.T)


def fine_last(held, x, r, d, below, above):
    def body(c, ins, outs):
        x, r, d, below, above = ins
        x0, r0, b_out, r1_out, low, high = outs
        f, m = under(c, "f_"), under(c, "m_")
        wc = tiles(f["wc"], 1, 4)
        change = wc * on_faces(faced(below, above, 0, 16))
        r = r[...] - change
        d = d[...] - damping(FINE, f, 2, 2, 4) * change
        x0[...] = x[...] + d[:, :256]
        parts = split(d)
        a, inside = fine_own(parts, f, faced(below, above, 16, 16), [(c, "e")])
        r = r - a
        lane = lax.broadcasted_iota(jnp.int32, (256, 128), 1)
        r0[:, :256] = r[:, :256]
        r0[:, 256:] = jnp.where(lane < 64, r[:, 256:384], r[:, 384:])
        beyond = faced(below, above, 32, 8) - wc * inside
        b = left(c, "ra", split(r)) + mid_faces(c["rp"][...], beyond)
        b = right(c, "rc", split(b))
        b_out[...] = b
        d = tiles(m["d1"], 2, 1) * b
        plane1 = left(m, "pl", split(d))
        r = b - mid_own(d, m)
        r1_out[...] = r
        d = MID.steps[0][0] * d + damping(MID, m, 1, 2, 1) * r
        plane2 = left(m, "pl", split(d))
        for k, plane in enumerate((plane1, plane2)):
            low[8 * k : 8 * k + 8] = plane[:8]
            high[8 * k : 8 * k + 8] = plane[8:]

    return call(
        body,
        [(256, 256), (256, 384), (64, 256), (64, 256), (16, 256), (16, 256)],
        held,
        (x, r, d, below, above),
    )


def share_tables(consts):
    top = np.zeros((3, 4))
    top[0, 0] = top[1, 1] = top[1, 2] = top[2, 3] = 1.0
    jz = top @ blocks(J_MID.T, 2)

    def down(z_part, r_part):
        t = np.zeros((4, 4, 2, 8, 4))
        for e in range(2):
            for k in range(2):
                t[e + k, :3, e] += np.einsum("zy,b->zyb", jz @ z_part, (J_MID.T @ r_part)[k])
        return t.reshape(16, 64)

    def across(part):
        t = np.zeros((256, 32))
        for v in range(32):
            t[4 * v : 4 * v + 4, v] += (J_MID.T @ part)[0]
            at = (4 * v - 4) % 256
            t[at : at + 4, v] += (J_MID.T @ part)[1]
        return np.tile(t, (1, 4))

    wz, wr = blocks(np.diag(MID.w), 2), np.diag(MID.w)
    kz = blocks(MID.k, 2)
    pair(consts, "sm", down(np.diag(MID.m_z), np.diag(MID.m_p)))
    pair(
        consts,
        "s1",
        0.5 * down(kz, wr) + 0.5 * down(wz, MID.k) + mass_coef * down(wz, wr),
    )
    pair(consts, "s2", 0.5 * down(wz, wr))
    pair(
        consts,
        "sc",
        np.concatenate([across(np.diag(MID.m_p)), -across(wr), -across(MID.k)], axis=0),
    )


def mid_last(held, b, r1, below, above):
    def body(c, ins, outs):
        b, r1, below, above = ins
        chunk, lo, hi, lo2, hi2, block, sems = outs
        down, c = c, under(c, "m_")
        d1, d2, d3 = (damping(MID, c, k, 2, 1) for k in range(3))
        d = d1 * b[...]
        x = d
        r = r1[...] - c["wc"][...] * mid_faces(c["pf"][...], faced(below, above, 0, 8))
        d = MID.steps[0][0] * d + d2 * r
        x = x + d
        r = r - mid_own(d, c, faced(below, above, 8, 8))
        d = MID.steps[1][0] * d + d3 * r
        x = x + d
        parts = split(d)
        t = jnp.concatenate(
            [left(down, "sm", split(r)), *lefts([(down, "s1"), (down, "s2")], parts)], axis=1
        )
        t = right(down, "sc", split(t))
        t = jnp.concatenate([t, t, t], axis=1)
        q = lax.broadcasted_iota(jnp.int32, t.shape, 0)
        lane = lax.broadcasted_iota(jnp.int32, t.shape, 1) // 32
        t = jnp.sum(jnp.where(q == lane, t, 0.0), axis=0, keepdims=True)
        which = lax.broadcasted_iota(jnp.int32, block.shape, 0) % 3
        block[...] = jnp.where(
            which == 0, t[:, :128], jnp.where(which == 1, t[:, 128:256], t[:, 256:])
        )
        copies = [
            pltpu.make_async_copy(block, chunk.at[pl.ds(192 * k, 192)], sems.at[k]) for k in range(4)
        ]
        for copy in copies:
            copy.start()
        plane1 = left(c, "pl", parts)
        r = r - mid_own(d, c)
        plane2 = left(c, "pl", split(d1 * r))
        for near, far, at in ((lo, lo2, 0), (hi, hi2, 1)):
            near[0:64] = r
            near[64:72] = plane1[8 * at : 8 * at + 8]
            near[72:104] = x[32 * at : 32 * at + 32]
            far[0:8] = plane1[8 * at : 8 * at + 8]
            far[8:16] = plane2[8 * at : 8 * at + 8]
        for copy in copies:
            copy.wait()

    return call(
        body,
        [(768, 128), (104, 256), (104, 256), (16, 256), (16, 256)],
        held,
        (b, r1, below, above),
        scratch=[pltpu.VMEM((192, 128), f32), pltpu.SemaphoreType.DMA((4,))],
        direct=1,
    )


def coarse_operator():
    row = lax.broadcasted_iota(jnp.int32, (128, 128), 0)
    lane = lax.broadcasted_iota(jnp.int32, (128, 128), 1)
    z, z2 = row >> 5, lane >> 5
    apart = jnp.abs((row & 31) - (lane & 31))
    w = jnp.where(z == 1, 2.0, jnp.where(z == 3, 0.0, 1.0))
    w = jnp.where(z == z2, w, 0.0)
    next_plane = (jnp.abs(z - z2) == 1) & (z + z2 < 5)
    inner = jnp.where(apart == 0, 3.0 * w - next_plane.astype(f32), 0.0)
    inner = inner - jnp.where(apart == 1, 0.5 * w, 0.0)
    ends = jnp.where(apart == 31, -0.5 * w, 0.0)
    m = jnp.concatenate([inner, ends], axis=1).astype(bf16)
    return jnp.concatenate([m, m], axis=0)


def coarse_solve(g):
    m = coarse_operator()
    plane = lax.broadcasted_iota(jnp.int32, (1, 128), 1) // 32
    wz = jnp.where(plane == 1, 2.0, jnp.where(plane == 3, 0.0, 1.0))

    def after(u):
        return jnp.concatenate([u[8:], u[:8]], axis=0)

    def before(u):
        return jnp.concatenate([u[-8:], u[:-8]], axis=0)

    column = lax.broadcasted_iota(jnp.int32, (32, 8, 128), 2) % 32

    def columns(u):
        h = u.astype(bf16)
        rest = u - h.astype(f32)
        k, l = split(rest)
        t = dot(jnp.concatenate([h, k], axis=1), m) + dot(l, m[:128])
        ends = t[:, 128:].reshape(32, 8, 128)
        ends = jnp.where(
            column == 31,
            pltpu.roll(ends, 7, 1),
            jnp.where(column == 0, pltpu.roll(ends, 1, 1), 0.0),
        )
        return t[:, :128] + ends.reshape(256, 128)

    half = -0.5 * wz
    mass = 4.0 * mass_coef * wz

    def apply(p):
        p0, p1 = p
        return (
            columns(p0) + half * (p1 + before(p1)) + mass * p0,
            columns(p1) + half * (p0 + after(p0)) + mass * p1,
        )

    def inner_product(a, b):
        s = jnp.sum(a[0] * b[0] + a[1] * b[1], axis=0, keepdims=True)
        return jnp.sum(s, axis=1, keepdims=True)

    r = (g[:, 0:128] + before(g[:, 256:384]), g[:, 128:256])
    p = r
    x = (jnp.zeros_like(r[0]), jnp.zeros_like(r[1]))
    norm = inner_product(r, r)
    for it in range(CG_ITERS):
        q = apply(p)
        alpha = norm / inner_product(p, q)
        x = tuple(a + alpha * b for a, b in zip(x, p))
        if it + 1 < CG_ITERS:
            r = tuple(a - alpha * b for a, b in zip(r, q))
            new = inner_product(r, r)
            beta = new / norm
            p = tuple(a + beta * b for a, b in zip(r, p))
            norm = new
    return jnp.concatenate(x, axis=1)


def second_tables(consts):
    pair(consts, "c", closed_operator(MID, 6))
    t = np.concatenate([blocks(face_matrix(MID), 3), face_matrix(MID, 6)], axis=1)
    consts["p"] = t.astype(ml_dtypes.bfloat16)
    pair(consts, "po", beside_planes(MID))
    jc = np.zeros((4, 32, 256))
    for e in range(64):
        element = e if e < 48 else e - 64
        for k in range(2):
            v = element + k
            dev, col = v // 32 + 1, v % 32
            jc[dev, col, 4 * e : 4 * e + 4] = J_MID[:, k]
    jc = jc.reshape(128, 256)
    pair(consts, "vc", jc)
    pair(consts, "vk", jc @ (sum_matrix(64, 4, True) @ blocks(MID.k, 64)).T)
    jz = np.zeros((8, 3))
    jz[:4, :2] += J_MID
    jz[4:, 1:] += J_MID
    jdr = np.zeros((10, 8, 4, 3, 16))
    for e in range(10):
        for k in range(2):
            jdr[e, :, :, :, e + k] += np.einsum("zp,a->zap", jz, J_MID[:, k])
    order = [2 * (q % 8) + q // 8 for q in range(16)]
    vd = jdr[..., order].reshape(320, 48)
    pair(consts, "vd", vd)
    pair(consts, "va", window_operator(MID, 10) @ vd)
    pair(consts, "fo", blocks(J_FINE.T, 32))
    fc = np.zeros((128, 128))
    for e in range(16):
        src = e if e < 8 else e + 16
        fc[4 * src : 4 * src + 4, 8 * e : 8 * e + 8] = J_FINE.T
    pair(consts, "fh", fc)
    fd = np.kron(blocks(J_FINE, 2), J_FINE)
    pair(consts, "fd", blocks(fd, 2))
    pair(consts, "fp", beside_planes(FINE) @ blocks(fd, 2))


def second_smoothing(held, gathered, x0, r0, own_lo, own_hi, below, above, below2, above2):
    def body(c, ins, outs):
        gathered, x0, r0, own_lo, own_hi, below, above, below2, above2 = ins
        s_out, r_out, d_out, low, high, twice = outs
        i, j = lax.axis_index("gx"), lax.axis_index("gy")
        f, m = under(c, "f_"), under(c, "m_")
        x2 = coarse_solve(gathered)
        twice[0:256] = x2
        twice[256:512] = x2
        first = lax.rem(i + 30, 32)
        picked = twice[pl.ds(pl.multiple_of(first * 8, 8), 64), :].reshape(8, 8, 256)
        sub = lax.broadcasted_iota(jnp.int32, (8, 8, 256), 1)
        near = []
        for g in range(3):
            v = jnp.sum(jnp.where(sub == lax.rem(j + 7 + g, 8), picked, 0.0), axis=1)
            near.append(jnp.concatenate([v[:, :128], v[:, 128:]], axis=0))
        block = lax.broadcasted_iota(jnp.int32, (16, 128), 1) // 32
        y = []
        for z in range(3):
            v = [pltpu.roll(near[g], (32 * (g - z)) % 128, 1) if g != z else near[g] for g in range(3)]
            y.append(
                jnp.where(block == 0, v[0], jnp.where(block == 1, v[1], jnp.where(block == 2, v[2], 0.0)))
            )
        parts = split(jnp.concatenate(y, axis=0))
        yk = left(c, "vd", split(right(c, "vk", parts)))
        e2, ya = lefts([(c, "vd"), (c, "va")], split(right(c, "vc", parts)))
        g = m["wc"][...] * ya + tiles(m["cf"], 8, 1) * yk[32:-32]

        def table(step, count):
            return damping(MID, m, step, count, 1)

        planes = jnp.concatenate(
            [
                below2[:8],
                own_lo[64:72],
                below[64:72],
                above[64:72],
                own_hi[64:72],
                above2[:8],
            ],
            axis=0,
        )
        r = jnp.concatenate([below[:64], own_lo[:64], above[:64]], axis=0)
        r = r - m["wc"][...] * mid_faces(c["p"][:, :48], planes) - g[32:224]
        d = table(0, 6) * r
        x = jnp.concatenate([below[72:104], own_lo[72:104], own_hi[72:104], above[72:104]], axis=0)
        x = x + e2[96:224] + d[32:160]
        outer = jnp.concatenate([g[:32], g[224:]], axis=0) * table(0, 2)
        planes = faced(below2, above2, 8, 8) - left(c, "po", split(outer))
        parts = split(d)
        r = r - mid_apply(left(c, "c", parts) + mid_faces(c["p"][:, 48:], planes), parts, m)
        d = MID.steps[0][0] * d + table(1, 6) * r
        x = x + d[32:160]
        h, l = split(d)
        inner = {"h": c["ch"][32:160], "l": c["cl"][32:160]}
        r = r[32:160] - mid_apply(left(inner, "", (h, l)), (h[32:-32], l[32:-32]), m)
        d = MID.steps[1][0] * d[32:160] + table(2, 4) * r
        x = x + d
        h, l = split(x)
        x = jnp.concatenate(
            [
                right(c, "fo", (h[:, :128], l[:, :128])),
                right(c, "fh", (h[:, 128:], l[:, 128:])),
            ],
            axis=1,
        )
        e1 = left(c, "fd", split(x[32:96]))
        planes = left(c, "fp", split(jnp.concatenate([x[:32], x[96:]], axis=0)))
        r = r0[...] - fine_own(split(e1), f, planes)
        d = tiles(f["d1"], 2, 3) * r
        s_out[...] = x0[...] + (e1 + d)[:, :256]
        a, plane1 = fine_own(split(d), f, more=[(f, "pl")])
        r = r - a
        d = FINE.steps[0][0] * d + damping(FINE, f, 1, 2, 3) * r
        plane2 = left(f, "pl", split(d))
        r_out[...] = r
        d_out[...] = d
        for k, plane in enumerate((plane1, plane2)):
            low[16 * k : 16 * k + 16] = plane[:16]
            high[16 * k : 16 * k + 16] = plane[16:]

    return call(
        body,
        [(256, 256), (256, 384), (256, 384), (32, 384), (32, 384)],
        held,
        (gathered, x0, r0, own_lo, own_hi, below, above, below2, above2),
        scratch=[pltpu.VMEM((512, 256), f32)],
    )


def last_step(held, s, r, d, below, above):
    def body(c, ins, outs):
        c = under(c, "f_")
        s, r, d, below, above = ins
        (out,) = outs
        change = tiles(c["wc"], 1, 3) * on_faces(faced(below, above, 0, 16))
        r = r[...] - change
        d = d[...] - damping(FINE, c, 1, 2, 3) * change
        r = r - fine_own(split(d), c, faced(below, above, 16, 16))
        v = s[...] + d[:, :256]
        d = FINE.steps[1][0] * d + damping(FINE, c, 2, 2, 3) * r
        v = v + d[:, :256]
        for e in range(2):
            out[:, 8 * e : 8 * e + 8, :] = v[128 * e : 128 * e + 128].reshape(16, 8, 256)

    return call(body, [(16, 16, 256)], held, (s, r, d, below, above))[0]


def fetch(value, axis, offset):
    count = lax.axis_size(axis)
    return lax.ppermute(value, axis, [((i + offset) % count, i) for i in range(count)])


def both(low, high, offset=1):
    return fetch(high, "gx", -offset), fetch(low, "gx", offset)


def tables(*adds, mid=mid_own_constants):
    consts = {"f_" + k: v for k, v in own_constants().items()}
    consts.update({"m_" + k: v for k, v in mid().items()})
    for add in adds:
        add(consts)
    arrays, places = packed(consts)
    return [jnp.asarray(a) for a in arrays], places


def local(source):
    first, second = source[:, :, :128], source[:, :, 128:]
    from_right, from_left = fetch(first, "gy", 1), fetch(second, "gy", -1)
    held = tables(rhs_tables, middle_tables, last_tables, share_tables)
    b, low, high = fine_rhs(held, first, second, from_right, from_left, ready(held))
    x, r, d, low, high = fine_middle(held, b, *both(low, high))
    x0, r0, b, r1, low, high = fine_last(held, x, r, d, *both(low, high))
    chunk, lo, hi, lo2, hi2 = mid_last(held, b, r1, *both(low, high))
    gathered = lax.all_to_all(chunk.reshape(256, 384), ("gx", "gy"), 0, 0, tiled=True)
    far = both(lo2, hi2, 2)
    s, r, d, low, high = second_smoothing(
        tables(second_tables, mid=mid_constants), gathered, x0, r0, lo, hi, *both(lo, hi), *far
    )
    return last_step(tables(mid=dict), s, r, d, *both(low, high))


def solution(mesh):
    return jax.shard_map(
        local,
        mesh=mesh,
        in_specs=(P(None, "gx", "gy"),),
        out_specs=P(None, "gx", "gy"),
        check_vma=False,
    )
```
